32 devices in a mesh: dp: 16 (over z, x, core), seq: 2 (over y).
Axes of the slice: x: 2, y: 2, z: 4, core: 2. Of those that a mesh axis runs over, the one named last changes fastest.
Arguments:
- inputs: bfloat16 [1024, 16, 768], P('seq', 'dp'), may hold values from -6 to 6
- cotangent: bfloat16 [1024, 16, 768], P('seq', 'dp'), may hold values from -6 to 6
- tie_slots: int32 [12], replicated, may hold values from 0 to 1
- gain_first: float32 [2, 768], P(None, 'dp'), may hold values from 0.1 to 1.9
- shift_first: float32 [2, 768], P(None, 'dp'), may hold values from -3 to 3
- weight_triple: float32 [2, 768, 2304], P(None, 'dp'), may hold values from -0.3125 to 0.3125
- bias_pair: float32 [2, 1536], P(None, 'dp'), may hold values from -3 to 3
- weight_merge: float32 [2, 768, 768], P(None, 'dp'), may hold values from -1.25 to 1.25
- bias_merge: float32 [2, 768], P(None, 'dp'), may hold values from -4 to 4
- gain_second: float32 [2, 768], P(None, 'dp'), may hold values from 0.1 to 1.9
- shift_second: float32 [2, 768], P(None, 'dp'), may hold values from -3 to 3
- weight_expand: float32 [2, 768, 3072], P(None, 'dp'), may hold values from -0.21875 to 0.21875
- bias_expand: float32 [2, 3072], P(None, 'dp'), may hold values from -3 to 3
- weight_shrink: float32 [2, 3072, 768], P(None, 'dp'), may hold values from -0.109375 to 0.109375
- bias_shrink: float32 [2, 768], P(None, 'dp'), may hold values from -4 to 4
Outputs:
- layer_output: bfloat16 [1024, 16, 768], P('seq', 'dp')
- input_grad: float32 [1024, 16, 768], P('seq', 'dp')
- grad_gain_first: float32 [2, 768], P(None, 'dp')
- grad_shift_first: float32 [2, 768], P(None, 'dp')
- grad_weight_triple: float32 [2, 768, 2304], P(None, 'dp')
- grad_bias_pair: float32 [2, 1536], P(None, 'dp')
- grad_weight_merge: float32 [2, 768, 768], P(None, 'dp')
- grad_bias_merge: float32 [2, 768], P(None, 'dp')
- grad_gain_second: float32 [2, 768], P(None, 'dp')
- grad_shift_second: float32 [2, 768], P(None, 'dp')
- grad_weight_expand: float32 [2, 768, 3072], P(None, 'dp')
- grad_bias_expand: float32 [2, 3072], P(None, 'dp')
- grad_weight_shrink: float32 [2, 3072, 768], P(None, 'dp')
- grad_bias_shrink: float32 [2, 768], P(None, 'dp')
The draws below stay inside these ranges and needn't reach their ends.
Inputs may be any that keep to these rules, and one draw needn't show every extreme that they name: `tie_slots`: entry i picks the slot of parameter tensor i, in the order of the masters among the arguments.
All inputs are finite; a program needn't handle non-finite values.
Results may differ from the reference program's by a relative error of at most 0.034.
Values may be sent and summed in bfloat16 or wider, within the bound.
No kernel may reach another device: no remote copies, remote signals or barrier semaphores. Data moves between devices by JAX's collectives and lax.ppermute only.
A program may use at most 128 MiB of HBM per device.

```python
import math
import jax
import jax.numpy as jnp
from jax import lax

D = 768
H = 12
HD = 64
FF = 3072
SEQ_LEN = 1024
SLOTS = 2
SEQS_ALL = 16


def place_ends(values, stream_key, smallest, high):
    extent = values.shape
    spot = [jax.random.randint(jax.random.fold_in(stream_key, axis), (), 0, extent[axis]) for axis in range(len(extent))]
    values = values.at[tuple(spot)].set(smallest)
    longest = extent.index(max(extent))
    spot[longest] = (spot[longest] + 1) % extent[longest]
    return values.at[tuple(spot)].set(high)


def block_levels(own_key, dims, split, least, largest):
    def one(axis_at, parts):
        steps = jax.random.uniform(jax.random.fold_in(jax.random.fold_in(own_key, 6), axis_at), (parts,), jnp.float32, least / len(split), largest / len(split))
        return jnp.repeat(jnp.exp(steps), dims[axis_at] // parts).reshape((-1,) + (1,) * (len(dims) - axis_at - 1))

    loudness = one(*split[0])
    for cut in split[1:]:
        loudness = loudness * one(*cut)
    return loudness


def normal_values(stream_key, shape, scale, bound, cuts=(), kind=jnp.bfloat16):
    loudness = block_levels(stream_key, shape, cuts, -0.22, 0.18) if cuts else 1.0
    values = jax.random.normal(stream_key, shape, jnp.float32) * scale * loudness
    return jnp.minimum(jnp.maximum(values, -bound), bound).astype(kind)


def setup_inputs(seed: int = 0) -> dict:
    arg_keys = jax.random.split(jax.random.key(seed), 16)
    inputs = normal_values(arg_keys[0], (SEQ_LEN, SEQS_ALL, D), 1.0, 6.0, ((0, 2), (1, 16)))
    cotangent = normal_values(arg_keys[1], (SEQ_LEN, SEQS_ALL, D), 1.0, 6.0, ((0, 2), (1, 16)))
    tie_slots = place_ends(jax.random.randint(arg_keys[2], (12,), 0, SLOTS), jax.random.fold_in(arg_keys[2], 1), 0, SLOTS - 1).astype(jnp.int32)
    gain_first = jnp.clip(1.0 + 0.18 * jax.random.normal(arg_keys[3], (SLOTS, D), jnp.float32), 0.1, 1.9)
    shift_first = normal_values(arg_keys[4], (SLOTS, D), 0.5, 3.0, ((1, 16),), jnp.float32)
    weight_triple = normal_values(arg_keys[5], (SLOTS, D, 3 * D), (D // 2) ** -0.5, 0.3125, ((1, 16),), jnp.float32)
    bias_pair = normal_values(arg_keys[6], (SLOTS, 2 * D), 0.5, 3.0, ((1, 16),), jnp.float32)
    weight_merge = normal_values(arg_keys[7], (SLOTS, D, D), (D // 32) ** -0.5, 1.25, ((1, 16),), jnp.float32)
    bias_merge = normal_values(arg_keys[8], (SLOTS, D), 1.0, 4.0, ((1, 16),), jnp.float32)
    gain_second = jnp.clip(1.0 + 0.18 * jax.random.normal(arg_keys[9], (SLOTS, D), jnp.float32), 0.1, 1.9)
    shift_second = normal_values(arg_keys[10], (SLOTS, D), 0.5, 3.0, ((1, 16),), jnp.float32)
    weight_expand = normal_values(arg_keys[11], (SLOTS, D, FF), D ** -0.5, 0.21875, ((1, 16),), jnp.float32)
    bias_expand = normal_values(arg_keys[12], (SLOTS, FF), 0.5, 3.0, ((1, 16),), jnp.float32)
    weight_shrink = normal_values(arg_keys[13], (SLOTS, FF, D), FF ** -0.5, 0.109375, ((1, 16),), jnp.float32)
    bias_shrink = normal_values(arg_keys[14], (SLOTS, D), 1.0, 4.0, ((1, 16),), jnp.float32)
    return dict(inputs=inputs, cotangent=cotangent, tie_slots=tie_slots, gain_first=gain_first, shift_first=shift_first, weight_triple=weight_triple, bias_pair=bias_pair, weight_merge=weight_merge, bias_merge=bias_merge, gain_second=gain_second, shift_second=shift_second, weight_expand=weight_expand, bias_expand=bias_expand, weight_shrink=weight_shrink, bias_shrink=bias_shrink)


@jax.custom_vjp
def low(v):
    return lax.optimization_barrier(v.astype(jnp.bfloat16)).astype(jnp.float32)

@jax.custom_vjp
def low_back(v):
    return v

def low_keep(v):
    return (low(v), None)

def low_pass(kept, grad):
    return (grad,)

def back_keep(v):
    return (v, None)

def back_low(kept, grad):
    return (low(grad),)
low.defvjp(low_keep, low_pass)
low_back.defvjp(back_keep, back_low)
EPSILON = 1e-05
NEGATIVE = -1e+30
HIGHEST = lax.Precision.HIGHEST

def layer_norm(values, gain, shift):
    average = lax.optimization_barrier(jnp.mean(values, axis=-1, keepdims=True))
    centered = values - average
    variance = lax.optimization_barrier(jnp.mean(centered * centered, axis=-1, keepdims=True))
    return centered * lax.rsqrt(variance + EPSILON) * gain + shift

def forward(masters, inputs, tie_slots):
    chosen = [low(lax.dynamic_index_in_dim(masters[number], tie_slots[number], 0, keepdims=False)) for number in range(12)]
    gain_one, shift_one, triple_weight, pair_bias, merge_weight, merge_bias = chosen[0:6]
    gain_two, shift_two, expand_weight, expand_bias, shrink_weight, shrink_bias = chosen[6:12]
    length, group, width = inputs.shape
    normed = low(layer_norm(inputs, gain_one, shift_one))
    bias_full = jnp.concatenate([pair_bias[:width], jnp.zeros((width,), pair_bias.dtype), pair_bias[width:]])
    triple = jnp.einsum('tsd,de->tse', normed, triple_weight, precision=HIGHEST) + bias_full
    triple = low(low_back(triple))
    queries = triple[:, :, :width].reshape(length, group, H, HD)
    key_rows = triple[:, :, width:2 * width].reshape(length, group, H, HD)
    value_rows = triple[:, :, 2 * width:].reshape(length, group, H, HD)
    scores = jnp.einsum('qshd,kshd->shqk', queries, key_rows, precision=HIGHEST) * (1.0 / math.sqrt(HD))
    scores = low_back(scores)
    position = jnp.arange(length)
    allowed = position[:, None] >= position[None, :]
    scores = jnp.where(allowed, scores, NEGATIVE)
    highest = lax.optimization_barrier(jnp.max(scores, axis=-1, keepdims=True))
    lifted = jnp.exp(scores - highest)
    probs = lifted / lax.optimization_barrier(jnp.sum(lifted, axis=-1, keepdims=True))
    attended = jnp.einsum('shqk,kshd->qshd', low(probs), value_rows, precision=HIGHEST).reshape(length, group, width)
    attended = low(low_back(attended))
    branch = low_back(jnp.einsum('tsd,de->tse', attended, merge_weight, precision=HIGHEST) + merge_bias)
    middle = inputs + branch
    second = low(layer_norm(middle, gain_two, shift_two))
    hidden = low_back(jnp.einsum('tsd,df->tsf', second, expand_weight, precision=HIGHEST) + expand_bias)
    active = low(jax.nn.gelu(hidden, approximate=True))
    return middle + jnp.einsum('tsf,fd->tsd', active, shrink_weight, precision=HIGHEST) + shrink_bias

def reference(inputs, cotangent, tie_slots, gain_first, shift_first, weight_triple, bias_pair, weight_merge, bias_merge, gain_second, shift_second, weight_expand, bias_expand, weight_shrink, bias_shrink):
    masters = (gain_first, shift_first, weight_triple, bias_pair, weight_merge, bias_merge, gain_second, shift_second, weight_expand, bias_expand, weight_shrink, bias_shrink)
    group = math.gcd(SEQS_ALL, max(1, 2048 // SEQ_LEN))
    rounds = SEQS_ALL // group

    def regroup(array):
        return jnp.transpose(array.astype(jnp.float32).reshape(SEQ_LEN, rounds, group, D), (1, 0, 2, 3))

    def ungroup(array):
        return jnp.transpose(array, (1, 0, 2, 3)).reshape(SEQ_LEN, SEQS_ALL, D)

    def step(totals, blocks):
        block_in, block_cot = blocks
        result, pull = jax.vjp(lambda params, values: forward(params, values, tie_slots), masters, block_in)
        param_grads, input_part = pull(block_cot)
        return (tuple((left + right for left, right in zip(totals, param_grads))), (result, input_part))
    start_totals = tuple((jnp.zeros_like(master) for master in masters))
    totals, outputs = lax.scan(step, start_totals, (regroup(inputs), regroup(cotangent)))
    results, input_parts = outputs
    return (ungroup(results).astype(jnp.bfloat16), ungroup(input_parts), totals[0], totals[1], totals[2], totals[3], totals[4], totals[5], totals[6], totals[7], totals[8], totals[9], totals[10], totals[11])
```

```python
import functools
import math

import jax
import jax.numpy as jnp
from jax import lax
from jax.experimental import pallas as pl
from jax.experimental.pallas import tpu as pltpu
from jax.sharding import PartitionSpec as P

H = 12
GROUPS = 16
EPSILON = 1e-05
NEGATIVE = -1e30
F32 = jnp.float32
BF16 = jnp.bfloat16
VMEM_LIMIT = 56 * 1024 * 1024


def layer_norm(values, gain, shift):
    average = jnp.mean(values, axis=-1, keepdims=True)
    centered = values - average
    variance = jnp.mean(centered * centered, axis=-1, keepdims=True)
    return centered * lax.rsqrt(variance + EPSILON) * gain + shift


def dot(left, right, left_dim, right_dim):
    return lax.dot_general(
        left, right, (((left_dim,), (right_dim,)), ((), ())), preferred_element_type=F32
    )


def pair_masks():
    lane = lax.broadcasted_iota(jnp.int32, (1, 128), 1)
    low = (lane < 64).astype(F32)
    return low, 1.0 - low


def causal(scores, block):
    key = lax.broadcasted_iota(jnp.int32, (block, block), 0)
    query = lax.broadcasted_iota(jnp.int32, (block, block), 1)
    return jnp.where(key <= query, scores, NEGATIVE)


def attend_kernel(count, q_ref, k_ref, v_ref, rk_ref, rv_ref, o_ref, lse_ref, *, block):
    rows = q_ref.shape[0]
    masks = pair_masks()
    for index in range(rows // block):
        here = slice(index * block, (index + 1) * block)
        size = (index + 1) * block
        state = []
        parts = []
        for head in range(2):
            query = q_ref[here, :] * (masks[head] * 0.125).astype(BF16)
            parts.append(query)
            scores = dot(k_ref[0:size, :], query, 1, 1)
            last = causal(scores[size - block :], block)
            top = jnp.max(last, axis=0, keepdims=True)
            if index:
                scores = jnp.concatenate([scores[: size - block], last], axis=0)
                top = jnp.max(scores, axis=0, keepdims=True)
            else:
                scores = last
            lifted = jnp.exp(scores - top)
            total = jnp.sum(lifted, axis=0, keepdims=True)
            state += [top, total, dot(v_ref[0:size, :], lifted.astype(BF16), 0, 0)]

        def far(step, state):
            start = pl.multiple_of(step * rows, rows)
            keys = rk_ref[pl.ds(start, rows), :]
            values = rv_ref[pl.ds(start, rows), :]
            result = []
            for head in range(2):
                top, total, gathered = state[3 * head : 3 * head + 3]
                scores = dot(keys, parts[head], 1, 1)
                new_top = jnp.maximum(top, jnp.max(scores, axis=0, keepdims=True))
                factor = jnp.exp(top - new_top)
                lifted = jnp.exp(scores - new_top)
                total = total * factor + jnp.sum(lifted, axis=0, keepdims=True)
                gathered = gathered * factor + dot(values, lifted.astype(BF16), 0, 0)
                result += [new_top, total, gathered]
            return tuple(result)

        top0, total0, sum0, top1, total1, sum1 = lax.fori_loop(0, count[0], far, tuple(state))
        joined = jnp.concatenate([sum0[:64] / total0, sum1[64:] / total1], axis=0)
        o_ref[here, :] = jnp.transpose(joined).astype(BF16)
        lse_ref[0, 0:1, here] = top0 + jnp.log(total0)
        lse_ref[0, 1:2, here] = top1 + jnp.log(total1)


def attend(count, queries, triple, remote, block):
    rows, width = queries.shape[0], triple.shape[1] // 3
    pairs = width // 128
    far_rows = remote.shape[0]
    column = lambda size, offset: pl.BlockSpec((size, 128), lambda h, c: (0, h + offset))
    return pl.pallas_call(
        functools.partial(attend_kernel, block=block),
        grid_spec=pltpu.PrefetchScalarGridSpec(
            num_scalar_prefetch=1,
            grid=(pairs,),
            in_specs=[
                column(rows, 0),
                column(rows, pairs),
                column(rows, 2 * pairs),
                column(far_rows, 0),
                column(far_rows, pairs),
            ],
            out_specs=[column(rows, 0), pl.BlockSpec((1, 2, rows), lambda h, c: (h, 0, 0))],
        ),
        out_shape=[
            jax.ShapeDtypeStruct((rows, width), BF16),
            jax.ShapeDtypeStruct((pairs, 2, rows), F32),
        ],
        compiler_params=pltpu.CompilerParams(vmem_limit_bytes=VMEM_LIMIT),
        cost_estimate=pl.CostEstimate(
            flops=8 * rows * rows * width, bytes_accessed=rows * width * 12, transcendentals=rows * rows * 12
        ),
        name="attend",
    )(count, triple, triple, triple, remote, remote)


def attend_back_kernel(
    count, q_ref, k_ref, v_ref, rk_ref, rv_ref, do_ref, o_ref, lse_ref,
    dq_ref, dk_ref, dv_ref, rdk_ref, rdv_ref, dq_sum, dk_sum, dv_sum, *, block,
):
    rows = q_ref.shape[0]
    far_rows = rk_ref.shape[0]
    masks = pair_masks()
    blocks = rows // block

    def prepare(index):
        here = slice(index * block, (index + 1) * block)
        out_grad = do_ref[here, :]
        product = jnp.transpose(out_grad.astype(F32) * o_ref[here, :].astype(F32))
        result = []
        for head in range(2):
            query = q_ref[here, :] * (masks[head] * 0.125).astype(BF16)
            masked = out_grad * masks[head].astype(BF16)
            delta = jnp.sum(product[64 * head : 64 * head + 64], axis=0, keepdims=True)
            lse = lse_ref[0, head : head + 1, here]
            result.append((query, masked, delta, lse))
        return result

    def terms(ready, keys, values, diagonal):
        key_grad = value_grad = query_grad = 0.0
        for head in range(2):
            query, masked, delta, lse = ready[head]
            scores = dot(keys, query, 1, 1)
            if diagonal:
                size = scores.shape[0]
                last = causal(scores[size - block :], block)
                if size > block:
                    scores = jnp.concatenate([scores[: size - block], last], axis=0)
                else:
                    scores = last
            probs = jnp.exp(scores - lse)
            prob_grad = dot(values, masked, 1, 1)
            score_grad = (probs * (prob_grad - delta)).astype(BF16)
            value_grad += dot(probs.astype(BF16), masked, 1, 0)
            key_grad += dot(score_grad, query, 1, 0)
            part = keys * (masks[head] * 0.125).astype(BF16)
            query_grad += dot(part, score_grad, 0, 0)
        return key_grad, value_grad, query_grad

    for index in reversed(range(blocks)):
        here = slice(index * block, (index + 1) * block)
        size = (index + 1) * block
        key_grad, value_grad, query_grad = terms(
            prepare(index), k_ref[0:size, :], v_ref[0:size, :], True
        )
        if index == blocks - 1:
            dk_sum[...] = key_grad
            dv_sum[...] = value_grad
        else:
            dk_sum[0:size, :] += key_grad
            dv_sum[0:size, :] += value_grad
        dq_sum[:, here] = query_grad

    def far(step, unused):
        start = pl.multiple_of(step * rows, rows)
        spot = pl.ds(start, rows)
        keys = rk_ref[spot, :]
        values = rv_ref[spot, :]
        key_total = value_total = 0.0
        for index in range(blocks):
            here = slice(index * block, (index + 1) * block)
            key_grad, value_grad, query_grad = terms(prepare(index), keys, values, False)
            key_total += key_grad
            value_total += value_grad
            dq_sum[:, here] += query_grad
        rdk_ref[spot, :] = key_total.astype(BF16)
        rdv_ref[spot, :] = value_total.astype(BF16)
        return unused

    lax.fori_loop(0, count[0], far, 0)

    def clear(step, unused):
        spot = pl.ds(pl.multiple_of(step * rows, rows), rows)
        rdk_ref[spot, :] = jnp.zeros((rows, 128), BF16)
        rdv_ref[spot, :] = jnp.zeros((rows, 128), BF16)
        return unused

    lax.fori_loop(count[0], far_rows // rows, clear, 0)
    dq_ref[...] = jnp.transpose(dq_sum[...]).astype(BF16)
    dk_ref[...] = dk_sum[...]
    dv_ref[...] = dv_sum[...]


def attend_back(count, triple, remote, out_grad, attended, lse, block):
    rows, width = attended.shape
    pairs = width // 128
    far_rows = remote.shape[0]
    column = lambda size, offset: pl.BlockSpec((size, 128), lambda h, c: (0, h + offset))
    return pl.pallas_call(
        functools.partial(attend_back_kernel, block=block),
        grid_spec=pltpu.PrefetchScalarGridSpec(
            num_scalar_prefetch=1,
            grid=(pairs,),
            in_specs=[
                column(rows, 0),
                column(rows, pairs),
                column(rows, 2 * pairs),
                column(far_rows, 0),
                column(far_rows, pairs),
                column(rows, 0),
                column(rows, 0),
                pl.BlockSpec((1, 2, rows), lambda h, c: (h, 0, 0)),
            ],
            out_specs=[
                column(rows, 0),
                column(rows, 0),
                column(rows, 0),
                column(far_rows, 0),
                column(far_rows, 0),
            ],
            scratch_shapes=[
                pltpu.VMEM((128, rows), F32),
                pltpu.VMEM((rows, 128), F32),
                pltpu.VMEM((rows, 128), F32),
            ],
        ),
        out_shape=[
            jax.ShapeDtypeStruct((rows, width), BF16),
            jax.ShapeDtypeStruct((rows, width), F32),
            jax.ShapeDtypeStruct((rows, width), F32),
            jax.ShapeDtypeStruct((far_rows, width), BF16),
            jax.ShapeDtypeStruct((far_rows, width), BF16),
        ],
        compiler_params=pltpu.CompilerParams(vmem_limit_bytes=VMEM_LIMIT),
        cost_estimate=pl.CostEstimate(
            flops=20 * rows * rows * width, bytes_accessed=rows * width * 30, transcendentals=rows * rows * 12
        ),
        name="attend_back",
    )(count, triple, triple, triple, remote, remote, out_grad, attended, lse)


def pairs_of(count, target):
    return [(index, target(index)) for index in range(count)]


def swap_cores(value, count):
    return lax.ppermute(value, "dp", pairs_of(count, lambda index: index ^ 1))


def swap_seq(value):
    return lax.ppermute(value, "seq", [(0, 1), (1, 0)])


def regroup(value, dp, moves):
    pairs = []
    for index in range(0, dp, 2):
        left, right = (index + 1) * 2, index * 2 + 1
        pairs += [(left, right), (right, left)]
    return jnp.where(moves, lax.ppermute(value, ("dp", "seq"), pairs), value)


def split_columns(value, width):
    return [value[:, at : at + width] for at in range(0, value.shape[1], width)]


def gather_pack(blocks, dp):
    sizes = [block.shape[0] for block in blocks]
    packed = lax.all_gather(jnp.concatenate(blocks, axis=0), "dp", axis=0)
    if dp == GROUPS:
        return packed
    parts, at = [], 0
    for size in sizes:
        part = packed[:, at : at + size]
        parts.append(part.reshape(GROUPS, -1, part.shape[2]))
        at += size
    return jnp.concatenate(parts, axis=1)


def scatter_pack(packed, sizes, dp):
    if dp != GROUPS:
        parts, at = [], 0
        for size in sizes:
            whole = size * dp // GROUPS
            part = packed[:, at : at + whole]
            parts.append(part.reshape(dp, size, part.shape[2]))
            at += whole
        packed = jnp.concatenate(parts, axis=1)
    return lax.psum_scatter(packed, "dp", scatter_dimension=0)


def sum_seq(value, sequence_parts):
    if sequence_parts == 2:
        return value.astype(F32) + swap_seq(value).astype(F32)
    return lax.psum(value, "seq").astype(F32)


def place(grad, master, slot):
    marker = (jnp.arange(master.shape[0]) == slot).astype(F32)
    return marker.reshape((-1,) + (1,) * grad.ndim) * grad[None]


def per_device(
    inputs,
    cotangent,
    tie_slots,
    *masters,
):
    dp, sequence_parts = lax.axis_size("dp"), lax.axis_size("seq")
    length, count, width = inputs.shape
    rows = length * count
    block = math.gcd(length, 256)
    moved = sequence_parts == 2 and dp % 2 == 0
    core = lax.axis_index("dp") % 2
    moves = core != lax.axis_index("seq")
    place_index = core if moved else lax.axis_index("seq")
    chosen = [
        lax.dynamic_index_in_dim(masters[number], tie_slots[number], 0, keepdims=False).astype(BF16)
        for number in range(12)
    ]
    part = width // dp
    ff = masters[10].shape[1] * dp
    small = jnp.concatenate([chosen[number] for number in (0, 1, 3, 5, 6, 7, 9, 11)])
    widths = [chosen[number].shape[0] for number in (0, 1, 3, 5, 6, 7, 9, 11)]
    pad = 16 * GROUPS // dp
    small = jnp.pad(small.reshape(1, -1), ((0, pad - 1), (0, width - small.shape[0])))
    head_blocks = split_columns(chosen[2], width) + [chosen[4], small]
    tail_blocks = [chosen[10]] + split_columns(chosen[8], width)
    head_sizes = [piece.shape[0] for piece in head_blocks]
    tail_sizes = [piece.shape[0] for piece in tail_blocks]
    head_pack = gather_pack(head_blocks, dp)
    flat_in = inputs.reshape(rows, width)
    flat_cot = cotangent.reshape(rows, width)
    if moved:
        flat_in = regroup(flat_in, dp, moves)
        flat_cot = regroup(flat_cot, dp, moves)
    tail_pack = gather_pack(tail_blocks, dp)

    group_rows = width // GROUPS
    matrix = lambda pack, at: pack[:, at * group_rows : (at + 1) * group_rows].reshape(width, width)
    triple_weight = jnp.concatenate([matrix(head_pack, at) for at in range(3)], axis=1)
    merge_weight = matrix(head_pack, 3)
    per_group = GROUPS // dp if dp < GROUPS else dp // GROUPS
    lines = head_pack[:, 4 * group_rows :].reshape(dp, pad, width)[:, 0]
    vectors, at = [], 0
    for size in widths:
        vectors.append(lines[:, at : at + size].reshape(-1).astype(F32))
        at += size
    gain_one, shift_one, pair_bias, merge_bias, gain_two, shift_two, expand_bias, shrink_bias = vectors

    flat_in = flat_in.astype(F32)
    normed, norm_one_pull = jax.vjp(layer_norm, flat_in, gain_one, shift_one)
    normed_low = normed.astype(BF16)
    bias_full = jnp.concatenate([pair_bias[:width], jnp.zeros((width,), F32), pair_bias[width:]])
    triple = (jnp.dot(normed_low, triple_weight, preferred_element_type=F32) + bias_full).astype(BF16)
    near = triple[:, width:]
    if moved:
        remote = swap_cores(near, dp)
    else:
        remote = lax.all_gather(near, "seq", axis=0, tiled=True)
    far_count = place_index.astype(jnp.int32).reshape(1)
    attended_low, lse = attend(far_count, triple, triple, remote, block)
    middle = flat_in + jnp.dot(attended_low, merge_weight, preferred_element_type=F32) + merge_bias

    ff_rows = ff // GROUPS
    shrink_weight = tail_pack[:, :ff_rows].reshape(ff, width)
    expand_weight = jnp.concatenate(
        [
            tail_pack[:, ff_rows + at * group_rows : ff_rows + (at + 1) * group_rows].reshape(width, width)
            for at in range(ff // width)
        ],
        axis=1,
    )
    second, norm_two_pull = jax.vjp(layer_norm, middle, gain_two, shift_two)
    second_low = second.astype(BF16)
    hidden = jnp.dot(second_low, expand_weight, preferred_element_type=F32) + expand_bias
    active, gelu_pull = jax.vjp(lambda values: jax.nn.gelu(values, approximate=True), hidden)
    active_low = active.astype(BF16)
    result = middle + jnp.dot(active_low, shrink_weight, preferred_element_type=F32) + shrink_bias
    output = result.astype(BF16)
    if moved:
        output = regroup(output, dp, moves)
    grad_shrink_weight = dot(active_low, flat_cot, 0, 0)
    grad_shrink_bias = jnp.sum(flat_cot.astype(F32), axis=0)
    active_grad = dot(flat_cot, shrink_weight, 1, 1)
    hidden_grad = gelu_pull(active_grad)[0].astype(BF16)
    grad_expand_weight = dot(second_low, hidden_grad, 0, 0)
    grad_expand_bias = jnp.sum(hidden_grad.astype(F32), axis=0)
    second_grad = dot(hidden_grad, expand_weight, 1, 1)
    middle_part, grad_gain_two, grad_shift_two = norm_two_pull(second_grad)
    middle_grad = flat_cot.astype(F32) + middle_part
    grouped = lambda value: value.astype(BF16).reshape(GROUPS, -1, width)
    tail_grads = jnp.concatenate(
        [grouped(grad_shrink_weight)] + [grouped(piece) for piece in split_columns(grad_expand_weight, width)],
        axis=1,
    )
    tail_own = sum_seq(scatter_pack(tail_grads, tail_sizes, dp), sequence_parts)

    branch_grad = middle_grad.astype(BF16)
    grad_merge_weight = dot(attended_low, branch_grad, 0, 0)
    grad_merge_bias = jnp.sum(branch_grad.astype(F32), axis=0)
    attended_grad = dot(branch_grad, merge_weight, 1, 1).astype(BF16)
    query_grad, key_grad, value_grad, far_key, far_value = attend_back(
        far_count, triple, remote, attended_grad, attended_low, lse, block
    )
    far_grad = jnp.concatenate([far_key, far_value], axis=1)
    pair_grad = jnp.concatenate([key_grad, value_grad], axis=1)
    if moved:
        pair_grad = pair_grad + swap_cores(far_grad, dp).astype(F32)
    else:
        pair_grad = pair_grad + lax.psum_scatter(far_grad, "seq", scatter_dimension=0, tiled=True).astype(F32)
    triple_grad = jnp.concatenate([query_grad, pair_grad.astype(BF16)], axis=1)
    grad_triple_weight = dot(normed_low, triple_grad, 0, 0)
    column_sums = jnp.sum(triple_grad.astype(F32), axis=0)
    grad_pair_bias = jnp.concatenate([column_sums[:width], column_sums[2 * width :]])
    normed_grad = dot(triple_grad, triple_weight, 1, 1)
    input_part, grad_gain_one, grad_shift_one = norm_one_pull(normed_grad)
    input_grad = middle_grad + input_part
    if moved:
        input_grad = regroup(input_grad, dp, moves)
    small_grads = [
        grad_gain_one, grad_shift_one, grad_pair_bias, grad_merge_bias,
        grad_gain_two, grad_shift_two, grad_expand_bias, grad_shrink_bias,
    ]
    lines = jnp.concatenate([piece.reshape(dp, -1) for piece in small_grads], axis=1).astype(BF16)
    lines = jnp.pad(lines[:, None], ((0, 0), (0, pad - 1), (0, width - lines.shape[1])))
    head_grads = jnp.concatenate(
        [grouped(piece) for piece in split_columns(grad_triple_weight, width)]
        + [grouped(grad_merge_weight), lines.reshape(GROUPS, -1, width)],
        axis=1,
    )
    head_own = sum_seq(scatter_pack(head_grads, head_sizes, dp), sequence_parts)

    piece_rows = chosen[4].shape[0]
    cut = lambda pack, at, size: pack[at : at + size]
    own_triple = jnp.concatenate([cut(head_own, at * piece_rows, piece_rows) for at in range(3)], axis=1)
    own_merge = cut(head_own, 3 * piece_rows, piece_rows)
    own_small, at = [], 0
    for size in widths:
        own_small.append(head_own[4 * piece_rows, at : at + size])
        at += size
    shrink_rows = chosen[10].shape[0]
    own_shrink = tail_own[:shrink_rows]
    own_expand = jnp.concatenate(
        [cut(tail_own, shrink_rows + at * piece_rows, piece_rows) for at in range(ff // width)], axis=1
    )
    own = [
        own_small[0], own_small[1], own_triple, own_small[2], own_merge, own_small[3],
        own_small[4], own_small[5], own_expand, own_small[6], own_shrink, own_small[7],
    ]
    shape = (length, count, width)
    return (output.reshape(shape), input_grad.reshape(shape)) + tuple(
        place(grad, master, tie_slots[number]) for number, (grad, master) in enumerate(zip(own, masters))
    )


def solution(mesh):
    in_specs = (
        P("seq", "dp", None),
        P("seq", "dp", None),
        P(),
        P(None, "dp"),
        P(None, "dp"),
        P(None, "dp", None),
        P(None, "dp"),
        P(None, "dp", None),
        P(None, "dp"),
        P(None, "dp"),
        P(None, "dp"),
        P(None, "dp", None),
        P(None, "dp"),
        P(None, "dp", None),
        P(None, "dp"),
    )
    out_specs = (
        P("seq", "dp", None),
        P("seq", "dp", None),
        P(None, "dp"),
        P(None, "dp"),
        P(None, "dp", None),
        P(None, "dp"),
        P(None, "dp", None),
        P(None, "dp"),
        P(None, "dp"),
        P(None, "dp"),
        P(None, "dp", None),
        P(None, "dp"),
        P(None, "dp", None),
        P(None, "dp"),
    )
    return jax.shard_map(
        per_device, mesh=mesh, in_specs=in_specs, out_specs=out_specs, check_vma=False
    )
```

```python
import functools
import math

import jax
import jax.numpy as jnp
from jax import lax
from jax.experimental import pallas as pl
from jax.experimental.pallas import tpu as pltpu
from jax.sharding import PartitionSpec as P

H = 12
GROUPS = 16
SMALL = (0, 1, 3, 5, 6, 7, 9, 11)
EPSILON = 1e-05
NEGATIVE = -1e30
F32 = jnp.float32
BF16 = jnp.bfloat16
VMEM_LIMIT = 56 * 1024 * 1024


def layer_norm(values, gain, shift):
    average = jnp.mean(values, axis=-1, keepdims=True)
    centered = values - average
    variance = jnp.mean(centered * centered, axis=-1, keepdims=True)
    return centered * lax.rsqrt(variance + EPSILON) * gain + shift


def dot(left, right, left_dim, right_dim):
    return lax.dot_general(
        left, right, (((left_dim,), (right_dim,)), ((), ())), preferred_element_type=F32
    )


def pair_masks():
    lane = lax.broadcasted_iota(jnp.int32, (1, 128), 1)
    low = (lane < 64).astype(F32)
    return low, 1.0 - low


def causal(scores, block):
    key = lax.broadcasted_iota(jnp.int32, (block, block), 0)
    query = lax.broadcasted_iota(jnp.int32, (block, block), 1)
    return jnp.where(key <= query, scores, NEGATIVE)


def attend_kernel(count, q_ref, k_ref, v_ref, rk_ref, rv_ref, o_ref, lse_ref, *, block):
    rows = q_ref.shape[0]
    masks = pair_masks()
    for index in range(rows // block):
        here = slice(index * block, (index + 1) * block)
        size = (index + 1) * block
        state = []
        parts = []
        for head in range(2):
            query = q_ref[here, :] * (masks[head] * 0.125).astype(BF16)
            parts.append(query)
            scores = dot(k_ref[0:size, :], query, 1, 1)
            last = causal(scores[size - block :], block)
            top = jnp.max(last, axis=0, keepdims=True)
            if index:
                scores = jnp.concatenate([scores[: size - block], last], axis=0)
                top = jnp.max(scores, axis=0, keepdims=True)
            else:
                scores = last
            lifted = jnp.exp(scores - top)
            total = jnp.sum(lifted, axis=0, keepdims=True)
            state += [top, total, dot(v_ref[0:size, :], lifted.astype(BF16), 0, 0)]

        def far(step, state):
            start = pl.multiple_of(step * rows, rows)
            keys = rk_ref[pl.ds(start, rows), :]
            values = rv_ref[pl.ds(start, rows), :]
            result = []
            for head in range(2):
                top, total, gathered = state[3 * head : 3 * head + 3]
                scores = dot(keys, parts[head], 1, 1)
                new_top = jnp.maximum(top, jnp.max(scores, axis=0, keepdims=True))
                factor = jnp.exp(top - new_top)
                lifted = jnp.exp(scores - new_top)
                total = total * factor + jnp.sum(lifted, axis=0, keepdims=True)
                gathered = gathered * factor + dot(values, lifted.astype(BF16), 0, 0)
                result += [new_top, total, gathered]
            return tuple(result)

        top0, total0, sum0, top1, total1, sum1 = lax.fori_loop(0, count[0], far, tuple(state))
        joined = jnp.concatenate([sum0[:64] / total0, sum1[64:] / total1], axis=0)
        o_ref[here, :] = jnp.transpose(joined).astype(BF16)
        lse_ref[0, 0:1, here] = top0 + jnp.log(total0)
        lse_ref[0, 1:2, here] = top1 + jnp.log(total1)


def attend(count, queries, near, remote, block):
    rows, width = queries.shape
    pairs = width // 128
    far_rows = remote.shape[0]
    column = lambda size, offset: pl.BlockSpec((size, 128), lambda h, c: (0, h + offset))
    return pl.pallas_call(
        functools.partial(attend_kernel, block=block),
        grid_spec=pltpu.PrefetchScalarGridSpec(
            num_scalar_prefetch=1,
            grid=(pairs,),
            in_specs=[
                column(rows, 0),
                column(rows, 0),
                column(rows, pairs),
                column(far_rows, 0),
                column(far_rows, pairs),
            ],
            out_specs=[column(rows, 0), pl.BlockSpec((1, 2, rows), lambda h, c: (h, 0, 0))],
        ),
        out_shape=[
            jax.ShapeDtypeStruct((rows, width), BF16),
            jax.ShapeDtypeStruct((pairs, 2, rows), F32),
        ],
        compiler_params=pltpu.CompilerParams(vmem_limit_bytes=VMEM_LIMIT),
        cost_estimate=pl.CostEstimate(
            flops=8 * rows * rows * width, bytes_accessed=rows * width * 12, transcendentals=rows * rows * 12
        ),
        name="attend",
    )(count, queries, near, near, remote, remote)


def attend_back_kernel(
    count, q_ref, k_ref, v_ref, rk_ref, rv_ref, do_ref, o_ref, lse_ref,
    dq_ref, dk_ref, dv_ref, rdk_ref, rdv_ref, dq_sum, dk_sum, dv_sum, *, block,
):
    rows = q_ref.shape[0]
    far_rows = rk_ref.shape[0]
    masks = pair_masks()
    blocks = rows // block

    def prepare(index):
        here = slice(index * block, (index + 1) * block)
        out_grad = do_ref[here, :]
        product = jnp.transpose(out_grad.astype(F32) * o_ref[here, :].astype(F32))
        result = []
        for head in range(2):
            query = q_ref[here, :] * (masks[head] * 0.125).astype(BF16)
            masked = out_grad * masks[head].astype(BF16)
            delta = jnp.sum(product[64 * head : 64 * head + 64], axis=0, keepdims=True)
            lse = lse_ref[0, head : head + 1, here]
            result.append((query, masked, delta, lse))
        return result

    def terms(ready, keys, values, diagonal):
        key_grad = value_grad = query_grad = 0.0
        for head in range(2):
            query, masked, delta, lse = ready[head]
            scores = dot(keys, query, 1, 1)
            if diagonal:
                size = scores.shape[0]
                last = causal(scores[size - block :], block)
                if size > block:
                    scores = jnp.concatenate([scores[: size - block], last], axis=0)
                else:
                    scores = last
            probs = jnp.exp(scores - lse)
            prob_grad = dot(values, masked, 1, 1)
            score_grad = (probs * (prob_grad - delta)).astype(BF16)
            value_grad += dot(probs.astype(BF16), masked, 1, 0)
            key_grad += dot(score_grad, query, 1, 0)
            part = keys * (masks[head] * 0.125).astype(BF16)
            query_grad += dot(part, score_grad, 0, 0)
        return key_grad, value_grad, query_grad

    for index in reversed(range(blocks)):
        here = slice(index * block, (index + 1) * block)
        size = (index + 1) * block
        key_grad, value_grad, query_grad = terms(
            prepare(index), k_ref[0:size, :], v_ref[0:size, :], True
        )
        if index == blocks - 1:
            dk_sum[...] = key_grad
            dv_sum[...] = value_grad
        else:
            dk_sum[0:size, :] += key_grad
            dv_sum[0:size, :] += value_grad
        dq_sum[:, here] = query_grad

    def far(step, unused):
        start = pl.multiple_of(step * rows, rows)
        spot = pl.ds(start, rows)
        keys = rk_ref[spot, :]
        values = rv_ref[spot, :]
        key_total = value_total = 0.0
        for index in range(blocks):
            here = slice(index * block, (index + 1) * block)
            key_grad, value_grad, query_grad = terms(prepare(index), keys, values, False)
            key_total += key_grad
            value_total += value_grad
            dq_sum[:, here] += query_grad
        rdk_ref[spot, :] = key_total.astype(BF16)
        rdv_ref[spot, :] = value_total.astype(BF16)
        return unused

    lax.fori_loop(0, count[0], far, 0)

    def clear(step, unused):
        spot = pl.ds(pl.multiple_of(step * rows, rows), rows)
        rdk_ref[spot, :] = jnp.zeros((rows, 128), BF16)
        rdv_ref[spot, :] = jnp.zeros((rows, 128), BF16)
        return unused

    lax.fori_loop(count[0], far_rows // rows, clear, 0)
    dq_ref[...] = jnp.transpose(dq_sum[...]).astype(BF16)
    dk_ref[...] = dk_sum[...]
    dv_ref[...] = dv_sum[...]


def attend_back(count, queries, near, remote, out_grad, attended, lse, block):
    rows, width = attended.shape
    pairs = width // 128
    far_rows = remote.shape[0]
    column = lambda size, offset: pl.BlockSpec((size, 128), lambda h, c: (0, h + offset))
    return pl.pallas_call(
        functools.partial(attend_back_kernel, block=block),
        grid_spec=pltpu.PrefetchScalarGridSpec(
            num_scalar_prefetch=1,
            grid=(pairs,),
            in_specs=[
                column(rows, 0),
                column(rows, 0),
                column(rows, pairs),
                column(far_rows, 0),
                column(far_rows, pairs),
                column(rows, 0),
                column(rows, 0),
                pl.BlockSpec((1, 2, rows), lambda h, c: (h, 0, 0)),
            ],
            out_specs=[
                column(rows, 0),
                column(rows, 0),
                column(rows, 0),
                column(far_rows, 0),
                column(far_rows, 0),
            ],
            scratch_shapes=[
                pltpu.VMEM((128, rows), F32),
                pltpu.VMEM((rows, 128), F32),
                pltpu.VMEM((rows, 128), F32),
            ],
        ),
        out_shape=[
            jax.ShapeDtypeStruct((rows, width), BF16),
            jax.ShapeDtypeStruct((rows, width), F32),
            jax.ShapeDtypeStruct((rows, width), F32),
            jax.ShapeDtypeStruct((far_rows, width), BF16),
            jax.ShapeDtypeStruct((far_rows, width), BF16),
        ],
        compiler_params=pltpu.CompilerParams(vmem_limit_bytes=VMEM_LIMIT),
        cost_estimate=pl.CostEstimate(
            flops=20 * rows * rows * width, bytes_accessed=rows * width * 30, transcendentals=rows * rows * 12
        ),
        name="attend_back",
    )(count, queries, near, near, remote, remote, out_grad, attended, lse)


def pairs_of(count, target):
    return [(index, target(index)) for index in range(count)]


def swap_cores(value, count):
    return lax.ppermute(value, "dp", pairs_of(count, lambda index: index ^ 1))


def swap_seq(value):
    return lax.ppermute(value, "seq", [(0, 1), (1, 0)])


def regroup(value, dp, moves):
    pairs = []
    for index in range(0, dp, 2):
        left, right = (index + 1) * 2, index * 2 + 1
        pairs += [(left, right), (right, left)]
    return jnp.where(moves, lax.ppermute(value, ("dp", "seq"), pairs), value)


def split_columns(value, width):
    return [value[:, at : at + width] for at in range(0, value.shape[1], width)]


def gather_pack(blocks, dp):
    sizes = [block.shape[0] for block in blocks]
    packed = lax.all_gather(jnp.concatenate(blocks, axis=0), "dp", axis=0)
    if dp == GROUPS:
        return packed
    parts, at = [], 0
    for size in sizes:
        part = packed[:, at : at + size]
        parts.append(part.reshape(GROUPS, -1, part.shape[2]))
        at += size
    return jnp.concatenate(parts, axis=1)


def scatter_pack(packed, sizes, dp):
    if dp != GROUPS:
        parts, at = [], 0
        for size in sizes:
            whole = size * dp // GROUPS
            part = packed[:, at : at + whole]
            parts.append(part.reshape(dp, size, part.shape[2]))
            at += whole
        packed = jnp.concatenate(parts, axis=1)
    return lax.psum_scatter(packed, "dp", scatter_dimension=0)


def sum_seq(value, sequence_parts):
    if sequence_parts == 2:
        return value.astype(F32) + swap_seq(value).astype(F32)
    return lax.psum(value, "seq").astype(F32)


def place(grad, master, slot):
    marker = (jnp.arange(master.shape[0]) == slot).astype(F32)
    return marker.reshape((-1,) + (1,) * grad.ndim) * grad[None]


def spot(place):
    index = place[0]
    return index >> 2, (index >> 1) & 1, index & 1, place[1]


def whole(shape):
    return pl.BlockSpec(shape, lambda *unused: (0,) * len(shape))


ANYWHERE = pl.BlockSpec(memory_space=pl.ANY)


def kernel_call(body, scalars, in_specs, args, out_specs, out_shape, scratch, name, flops, moved):
    return pl.pallas_call(
        body,
        grid_spec=pltpu.PrefetchScalarGridSpec(
            num_scalar_prefetch=len(scalars),
            grid=(1,),
            in_specs=in_specs,
            out_specs=out_specs,
            scratch_shapes=scratch,
        ),
        out_shape=out_shape,
        compiler_params=pltpu.CompilerParams(vmem_limit_bytes=VMEM_LIMIT),
        cost_estimate=pl.CostEstimate(flops=flops, bytes_accessed=moved, transcendentals=0),
        name=name,
    )(*scalars, *args)


def pack_kernel(slots, place, *refs):
    masters, (head, tail, lines) = refs[:12], refs[12:]
    part, width = masters[4].shape
    lines[...] = jnp.zeros_like(lines)
    for row, number in enumerate(SMALL):
        master = masters[number]
        lines[row : row + 1, 0 : master.shape[1]] = master[pl.ds(slots[number], 1), :]
    for at in range(3):
        head[at * part : (at + 1) * part, :] = masters[2][:, at * width : (at + 1) * width].astype(BF16)
    head[3 * part : 4 * part, :] = masters[4][...].astype(BF16)
    head[4 * part :, :] = lines[...].astype(BF16)

    @pl.when(place[1] == 0)
    def shrink():
        tail[...] = masters[10][...].astype(BF16)

    @pl.when(place[1] != 0)
    def expand():
        for at in range(masters[8].shape[1] // width):
            tail[at * part : (at + 1) * part, :] = masters[8][:, at * width : (at + 1) * width].astype(BF16)


def pack(slots, place, masters):
    specs = []
    for number, master in enumerate(masters):
        if master.ndim == 2:
            specs.append(whole(master.shape))
        else:
            specs.append(
                pl.BlockSpec(
                    (None,) + master.shape[1:],
                    functools.partial(lambda step, slots, place, number: (slots[number], 0, 0), number=number),
                )
            )
    part, width = masters[4].shape[1:]
    rows = 4 * part + 16
    tail_rows = masters[10].shape[1]
    return kernel_call(
        pack_kernel, (slots, place), specs, masters,
        [whole((rows, width)), whole((tail_rows, width))],
        [jax.ShapeDtypeStruct((rows, width), BF16), jax.ShapeDtypeStruct((tail_rows, width), BF16)],
        [pltpu.VMEM((16, width), F32)], "pack", 0, 4 * rows * width * 6,
    )


def shift_z(value):
    return lax.ppermute(value, "dp", pairs_of(16, lambda index: (index + 4) % 16))


def swap_x(value):
    return lax.ppermute(value, "dp", pairs_of(16, lambda index: index ^ 2))


def gather_ring(own):
    pieces = []
    for step in range(4):
        if step:
            own = shift_z(own)
        pieces += [own, swap_x(own)]
    return pieces


def ring_slots(z, x):
    slots = []
    for step in range(4):
        base = ((z - step) & 3) * 4
        slots += [base + x * 2, base + (1 - x) * 2]
    return slots


def gather_head(own):
    pieces = gather_ring(own)
    return pieces + [swap_cores(piece, 16) for piece in pieces]


def gather_tail(own):
    pieces = gather_ring(own)
    pieces = pieces + [swap_seq(piece) for piece in pieces]
    return pieces + [swap_cores(piece, 16) for piece in pieces]


def row_sum(value):
    return jnp.sum(value, axis=0, keepdims=True)


def normalise(values):
    average = jnp.mean(values, axis=-1, keepdims=True)
    centered = values - average
    scale = lax.rsqrt(jnp.mean(centered * centered, axis=-1, keepdims=True) + EPSILON)
    return centered * scale, scale


def norm_back(grad, gain, shape, scale):
    inner = grad * gain
    first = jnp.mean(inner, axis=-1, keepdims=True)
    second = jnp.mean(inner * shape, axis=-1, keepdims=True)
    return scale * (inner - first - shape * second)


def qkv_kernel(place, x_ref, *refs):
    pieces, (packed, n1_ref, q_ref, kv_ref, v48, v96, v192, sems) = refs[:16], refs[16:]
    z, x, core, half = spot(place)
    slots = ring_slots(z, x)
    slots = [slot + core for slot in slots] + [slot + 1 - core for slot in slots]
    copies = [
        pltpu.make_async_copy(piece, packed.at[slots[number]], sems.at[number])
        for number, piece in enumerate(pieces)
    ]
    for copy in copies:
        copy.start()
    width = x_ref.shape[1]
    part = width // GROUPS
    shape, unused = normalise(x_ref[...].astype(F32))
    for copy in copies:
        copy.wait()
    for group in range(GROUPS):
        lines = packed[group, 4 * part : 4 * part + 16, :].astype(F32)[0:8]
        for out in (v48, v96, v192):
            size = out.shape[1] // GROUPS
            out[:, group * size : (group + 1) * size] = lines[:, :size]
    normed = (shape * v48[0:1, :] + v48[1:2, :]).astype(BF16)
    n1_ref[...] = normed
    for at in range(3):
        weight = packed[:, at * part : (at + 1) * part, :].reshape(width, width)
        result = dot(normed, weight, 1, 0)
        if at == 0:
            q_ref[...] = (result + v96[2:3, :width]).astype(BF16)
        elif at == 1:
            kv_ref[:, :width] = result.astype(BF16)
        else:
            kv_ref[:, width:] = (result + v96[2:3, width:]).astype(BF16)


def qkv(place, values, pieces):
    rows, width = values.shape
    shapes = [
        ((GROUPS,) + pieces[0].shape, BF16), ((rows, width), BF16), ((rows, width), BF16), ((rows, 2 * width), BF16),
        ((8, width), F32), ((8, 2 * width), F32), ((8, 4 * width), F32),
    ]
    return kernel_call(
        qkv_kernel, (place,), [whole(values.shape)] + [ANYWHERE] * 16, [values] + pieces,
        [whole(shape) for shape, unused in shapes],
        [jax.ShapeDtypeStruct(shape, dtype) for shape, dtype in shapes],
        [pltpu.SemaphoreType.DMA((16,))], "qkv", 6 * rows * width * width, 20 * width * width,
    )


def merge_kernel(x_ref, o_ref, weight, v48, m_ref, n2_ref):
    width = x_ref.shape[1]
    middle = x_ref[...].astype(F32) + dot(o_ref[...], weight[...].reshape(width, width), 1, 0) + v48[3:4, :]
    m_ref[...] = middle
    shape, unused = normalise(middle)
    n2_ref[...] = (shape * v48[4:5, :] + v48[5:6, :]).astype(BF16)


def merge_spec(packed):
    part = packed.shape[2] // GROUPS
    return pl.BlockSpec((GROUPS, part, packed.shape[2]), lambda *unused: (0, 3, 0))


def merge(values, attended, packed, v48):
    rows, width = values.shape
    return kernel_call(
        merge_kernel, (), [whole(values.shape), whole(values.shape), merge_spec(packed), whole(v48.shape)],
        [values, attended, packed, v48], [whole(values.shape)] * 2,
        [jax.ShapeDtypeStruct((rows, width), F32), jax.ShapeDtypeStruct((rows, width), BF16)],
        [], "merge", 2 * rows * width * width, 12 * rows * width,
    )


def gelu_pair(value):
    scale, cubic = math.sqrt(2 / math.pi), 0.044715
    square = value * value
    bent = jnp.tanh(scale * value * (1.0 + cubic * square))
    half = 0.5 * (1.0 + bent)
    slope = half + 0.5 * value * (1.0 - bent * bent) * (scale * (1.0 + 3.0 * cubic * square))
    return value * half, slope


def ffn_kernel(place, *refs):
    pieces, refs = refs[:32], refs[32:]
    m_ref, n2_ref, gy_ref, merge_weight, v48, v192, out_ref, dm_ref, dz_ref, do_ref, g48, g192 = refs[:12]
    outs, (weights, grads, y, dn2, n2_t, u, df, in_sems, out_sems) = refs[12:20], refs[20:]
    z, x, core, half = spot(place)
    slots = ring_slots(z, x)
    spots = [(slot + core, half) for slot in slots] + [(slot + core, 1 - half) for slot in slots]
    spots += [(slot + 1 - core, half) for slot in slots] + [(slot + 1 - core, 1 - half) for slot in slots]
    copies = [
        pltpu.make_async_copy(piece, weights.at[spots[number][0], spots[number][1]], in_sems.at[number])
        for number, piece in enumerate(pieces)
    ]
    for copy in copies:
        copy.start()
    width = m_ref.shape[1]
    part = width // GROUPS
    n2_t[...] = jnp.transpose(n2_ref[...])
    y[...] = jnp.zeros_like(y)
    dn2[...] = jnp.zeros_like(dn2)
    for copy in copies:
        copy.wait()

    def step(at, unused):
        first = pl.multiple_of(at * 4, 4)
        lines = pl.ds(pl.multiple_of(at * part, 16), part)
        chunk = 256
        for column in range(0, width, chunk):
            place_in = pl.ds(pl.multiple_of(at * width + column, 128), chunk)
            expand = weights[:, 1, lines, column : column + chunk].reshape(width, chunk)
            hidden = dot(n2_ref[...], expand, 1, 0) + v192[6:7, place_in]
            shrink = weights[pl.ds(first, 4), 0].reshape(width, width)[column : column + chunk]
            active, slope = gelu_pair(hidden)
            u[:, column : column + chunk] = active.astype(BF16)
            hidden_grad = (dot(gy_ref[...], shrink, 1, 1) * slope).astype(BF16)
            df[:, column : column + chunk] = hidden_grad
            g192[0:1, place_in] = row_sum(hidden_grad.astype(F32))
        shrink = weights[pl.ds(first, 4), 0].reshape(width, width)
        expand = weights[:, 1, lines, :].reshape(width, width)
        y[...] += dot(u[...], shrink, 1, 0)
        dn2[...] += dot(df[...], expand, 1, 1)
        grads[pl.ds(first, 4), 0] = dot(u[...], gy_ref[...], 0, 0).astype(BF16).reshape(4, 4 * part, width)
        grads[:, 1, lines, :] = dot(n2_t[...], df[...], 1, 0).astype(BF16).reshape(GROUPS, part, width)
        return unused

    lax.fori_loop(0, 4, step, 0)
    copies = []
    for order in range(4):
        base = ((z - order) & 3) * 4
        for number, out in ((0, outs[2 * order]), (1, outs[2 * order + 1])):
            side = core if number == 0 else 1 - core
            for kind in range(2):
                for column in range(2):
                    source = base + (x if column == 0 else 1 - x) * 2 + side
                    copies.append(
                        pltpu.make_async_copy(
                            grads.at[source, half if kind == 0 else 1 - half],
                            out.at[kind, column],
                            out_sems.at[len(copies)],
                        )
                    )
    for copy in copies:
        copy.start()
    middle = m_ref[...]
    out_ref[...] = (middle + y[...] + v48[7:8, :]).astype(BF16)
    shape, scale = normalise(middle)
    second_grad = dn2[...]
    out_grad = gy_ref[...].astype(F32)
    middle_grad = out_grad + norm_back(second_grad, v48[4:5, :], shape, scale)
    dm_ref[...] = middle_grad
    low = middle_grad.astype(BF16)
    dz_ref[...] = low
    g48[...] = jnp.zeros_like(g48)
    g48[3:4, :] = row_sum(low.astype(F32))
    g48[4:5, :] = row_sum(shape * second_grad)
    g48[5:6, :] = row_sum(second_grad)
    g48[7:8, :] = row_sum(out_grad)
    do_ref[...] = dot(low, merge_weight[...].reshape(width, width), 1, 1).astype(BF16)
    for copy in copies:
        copy.wait()


def ffn(place, pieces, middle, second, out_grad, packed, v48, v192):
    rows, width = middle.shape
    ff = 4 * width
    tail_rows = pieces[0].shape[0]
    shapes = [
        ((rows, width), BF16), ((rows, width), F32), ((rows, width), BF16), ((rows, width), BF16),
        ((8, width), F32), ((8, ff), F32),
    ]
    part = jax.ShapeDtypeStruct((2, 2, tail_rows, width), BF16)
    pack_shape = (GROUPS, 2, tail_rows, width)
    results = kernel_call(
        ffn_kernel, (place,),
        [ANYWHERE] * 32
        + [whole(middle.shape), whole(second.shape), whole(out_grad.shape), merge_spec(packed), whole(v48.shape), whole(v192.shape)],
        pieces + [middle, second, out_grad, packed, v48, v192],
        [whole(shape) for shape, unused in shapes] + [ANYWHERE] * 8,
        [jax.ShapeDtypeStruct(shape, dtype) for shape, dtype in shapes] + [part] * 8,
        [
            pltpu.VMEM(pack_shape, BF16), pltpu.VMEM(pack_shape, BF16),
            pltpu.VMEM((rows, width), F32), pltpu.VMEM((rows, width), F32), pltpu.VMEM((width, rows), BF16),
            pltpu.VMEM((rows, width), BF16), pltpu.VMEM((rows, width), BF16),
            pltpu.SemaphoreType.DMA((32,)), pltpu.SemaphoreType.DMA((32,)),
        ],
        "ffn", 12 * rows * width * ff, 8 * width * ff,
    )
    return results[:6], results[6:]


def close_kernel(
    place, n1_ref, x_ref, q_ref, k_ref, v_ref, far_k, far_v, o_ref, dz_ref, dm_ref, packed, v48, g48_in, g192,
    *refs,
):
    grad_ref, outs, (grads, g48, g96, dt, sems) = refs[0], refs[1:9], refs[9:]
    z, x, core, half = spot(place)
    width = x_ref.shape[1]
    part = width // GROUPS
    normed_t = jnp.transpose(n1_ref[...])
    normed_grad = None
    for at in range(3):
        if at == 0:
            dt[...] = q_ref[...]
        else:
            near, far = (k_ref, far_k) if at == 1 else (v_ref, far_v)
            dt[...] = (near[...] + far[...].astype(F32)).astype(BF16)
        if at != 1:
            g96[2:3, (at // 2) * width : (at // 2 + 1) * width] = row_sum(dt[...].astype(F32))
        weight = packed[:, at * part : (at + 1) * part, :].reshape(width, width)
        term = dot(dt[...], weight, 1, 1)
        normed_grad = term if normed_grad is None else normed_grad + term
        grads[:, at * part : (at + 1) * part, :] = dot(normed_t, dt[...], 1, 0).astype(BF16).reshape(GROUPS, part, width)
    grads[:, 3 * part : 4 * part, :] = dot(o_ref[...], dz_ref[...], 0, 0).astype(BF16).reshape(GROUPS, part, width)
    shape, scale = normalise(x_ref[...].astype(F32))
    g48[...] = g48_in[...]
    g48[0:1, :] = row_sum(shape * normed_grad)
    g48[1:2, :] = row_sum(normed_grad)
    row = lax.broadcasted_iota(jnp.int32, (16, 1), 0)
    for group in range(GROUPS):
        lines = jnp.concatenate([g48[:, group * part : (group + 1) * part], jnp.zeros((8, part), F32)], axis=0)
        grads[group, 4 * part :, :] = jnp.zeros((16, width), BF16)
        pair = g96[2:3, group * 2 * part : (group + 1) * 2 * part]
        wide = g192[0:1, group * 4 * part : (group + 1) * 4 * part]
        spread = jnp.where(row == 6, wide, 0.0)
        left = jnp.where(row == 2, pair, 0.0)
        grads[group, 4 * part :, 0 : 4 * part] = spread.astype(BF16)
        grads[group, 4 * part :, 0 : 2 * part] = (spread[:, : 2 * part] + left).astype(BF16)
        keep = jnp.where((row == 2) | (row == 6), 0.0, lines) + spread[:, :part] + left[:, :part]
        grads[group, 4 * part :, 0:part] = keep.astype(BF16)
    copies = []
    for order in range(4):
        base = ((z - order) & 3) * 4
        for number, out in ((0, outs[2 * order]), (1, outs[2 * order + 1])):
            side = core if number == 0 else 1 - core
            for column in range(2):
                source = base + (x if column == 0 else 1 - x) * 2 + side
                copies.append(pltpu.make_async_copy(grads.at[source], out.at[column], sems.at[len(copies)]))
    for copy in copies:
        copy.start()
    grad_ref[...] = (dm_ref[...] + norm_back(normed_grad, v48[0:1, :], shape, scale)).astype(BF16)
    for copy in copies:
        copy.wait()


def close(place, args):
    rows, width = args[0].shape
    packed = args[10]
    head_rows = packed.shape[1]
    part = jax.ShapeDtypeStruct((2, head_rows, width), BF16)
    results = kernel_call(
        close_kernel, (place,), [whole(arg.shape) for arg in args], args,
        [whole((rows, width))] + [ANYWHERE] * 8,
        [jax.ShapeDtypeStruct((rows, width), BF16)] + [part] * 8,
        [
            pltpu.VMEM(packed.shape, BF16), pltpu.VMEM((8, width), F32), pltpu.VMEM((8, 2 * width), F32),
            pltpu.VMEM((rows, width), BF16), pltpu.SemaphoreType.DMA((16,)),
        ],
        "close", 14 * rows * width * width, 20 * width * width,
    )
    return results[0], results[1:]


def scatter_head(parts):
    moving = None
    for order in (1, 2, 3, 0):
        keep, send = parts[2 * order], parts[2 * order + 1]
        came = swap_cores(send, 16)
        value = keep[0] + came[0] + swap_x(keep[1] + came[1])
        if moving is not None:
            value = value + shift_z(moving)
        moving = value
    return moving


def scatter_tail(parts):
    moving = None
    for order in (1, 2, 3, 0):
        keep, send = parts[2 * order], parts[2 * order + 1]
        came = swap_cores(send, 16)
        other = swap_seq(keep[1] + came[1])
        value = keep[0, 0] + came[0, 0] + other[0] + swap_x(keep[0, 1] + came[0, 1] + other[1])
        if moving is not None:
            value = value + shift_z(moving)
        moving = value
    return moving


def unpack_kernel(slots, place, head, head_far, tail, tail_far, *outs):
    part, width = outs[4].shape[1:]
    total = head[...].astype(F32) + head_far[...].astype(F32)
    near, far = tail[...].astype(F32), tail_far[...].astype(F32)
    first = place[1] == 0
    shrink = jnp.where(first, near, far)
    expand = jnp.where(first, far, near)
    for row, number in enumerate(SMALL):
        out = outs[number]
        size = out.shape[1]
        line = total[4 * part + row : 4 * part + row + 1, :size]
        row_at = lax.broadcasted_iota(jnp.int32, out.shape, 0)
        out[...] = jnp.where(row_at == slots[number], line, 0.0)
    for slot in range(outs[2].shape[0]):
        chosen = lambda number, value: jnp.where(slots[number] == slot, value, 0.0)
        for at in range(3):
            outs[2][slot, :, at * width : (at + 1) * width] = chosen(2, total[at * part : (at + 1) * part])
        outs[4][slot] = chosen(4, total[3 * part : 4 * part])
        for at in range(outs[8].shape[2] // width):
            outs[8][slot, :, at * width : (at + 1) * width] = chosen(8, expand[at * part : (at + 1) * part])
        outs[10][slot] = chosen(10, shrink)


def unpack(slots, place, parts, masters):
    return kernel_call(
        unpack_kernel, (slots, place), [whole(part.shape) for part in parts], parts,
        [whole(master.shape) for master in masters],
        [jax.ShapeDtypeStruct(master.shape, F32) for master in masters],
        [], "unpack", 0, 8 * 1024 * 1024,
    )


def per_device_fast(inputs, cotangent, tie_slots, *masters):
    length, count, width = inputs.shape
    block = math.gcd(length, 256)
    index, half = lax.axis_index("dp"), lax.axis_index("seq")
    place = jnp.stack([index, half]).astype(jnp.int32)
    core = index % 2
    moves = core != half
    head, tail = pack(tie_slots, place, masters)
    head_pieces = gather_head(head)
    tail_pieces = gather_tail(tail)
    values = regroup(inputs.reshape(length, width), 16, moves)
    out_grad = regroup(cotangent.reshape(length, width), 16, moves)
    packed, normed, queries, near, v48, v96, v192 = qkv(place, values, head_pieces)
    remote = swap_cores(near, 16)
    far_count = core.astype(jnp.int32).reshape(1)
    attended, lse = attend(far_count, queries, near, remote, block)
    middle, second = merge(values, attended, packed, v48)
    (output, middle_grad, branch_grad, attended_grad, g48, g192), tail_parts = ffn(
        place, tail_pieces, middle, second, out_grad, packed, v48, v192
    )
    tail_sum = scatter_tail(tail_parts)
    output = regroup(output, 16, moves)
    query_grad, key_grad, value_grad, far_key, far_value = attend_back(
        far_count, queries, near, remote, attended_grad, attended, lse, block
    )
    input_grad, head_parts = close(
        place,
        [
            normed, values, query_grad, key_grad, value_grad, swap_cores(far_key, 16), swap_cores(far_value, 16),
            attended, branch_grad, middle_grad, packed, v48, g48, g192,
        ],
    )
    input_grad = regroup(input_grad, 16, moves).astype(F32)
    head_sum = scatter_head(head_parts)
    grads = unpack(
        tie_slots, place, [head_sum, swap_seq(head_sum), tail_sum, swap_seq(tail_sum)], masters
    )
    shape = (length, count, width)
    return (output.reshape(shape), input_grad.reshape(shape)) + tuple(grads)


def per_device(
    inputs,
    cotangent,
    tie_slots,
    *masters,
):
    dp, sequence_parts = lax.axis_size("dp"), lax.axis_size("seq")
    length, count, width = inputs.shape
    rows = length * count
    block = math.gcd(length, 256)
    moved = sequence_parts == 2 and dp % 2 == 0
    core = lax.axis_index("dp") % 2
    moves = core != lax.axis_index("seq")
    place_index = core if moved else lax.axis_index("seq")
    chosen = [
        lax.dynamic_index_in_dim(masters[number], tie_slots[number], 0, keepdims=False).astype(BF16)
        for number in range(12)
    ]
    part = width // dp
    ff = masters[10].shape[1] * dp
    small = jnp.concatenate([chosen[number] for number in SMALL])
    widths = [chosen[number].shape[0] for number in SMALL]
    pad = 16 * GROUPS // dp
    small = jnp.pad(small.reshape(1, -1), ((0, pad - 1), (0, width - small.shape[0])))
    head_blocks = split_columns(chosen[2], width) + [chosen[4], small]
    tail_blocks = [chosen[10]] + split_columns(chosen[8], width)
    head_sizes = [piece.shape[0] for piece in head_blocks]
    tail_sizes = [piece.shape[0] for piece in tail_blocks]
    head_pack = gather_pack(head_blocks, dp)
    flat_in = inputs.reshape(rows, width)
    flat_cot = cotangent.reshape(rows, width)
    if moved:
        flat_in = regroup(flat_in, dp, moves)
        flat_cot = regroup(flat_cot, dp, moves)
    tail_pack = gather_pack(tail_blocks, dp)

    group_rows = width // GROUPS
    matrix = lambda pack, at: pack[:, at * group_rows : (at + 1) * group_rows].reshape(width, width)
    triple_weight = jnp.concatenate([matrix(head_pack, at) for at in range(3)], axis=1)
    merge_weight = matrix(head_pack, 3)
    per_group = GROUPS // dp if dp < GROUPS else dp // GROUPS
    lines = head_pack[:, 4 * group_rows :].reshape(dp, pad, width)[:, 0]
    vectors, at = [], 0
    for size in widths:
        vectors.append(lines[:, at : at + size].reshape(-1).astype(F32))
        at += size
    gain_one, shift_one, pair_bias, merge_bias, gain_two, shift_two, expand_bias, shrink_bias = vectors

    flat_in = flat_in.astype(F32)
    normed, norm_one_pull = jax.vjp(layer_norm, flat_in, gain_one, shift_one)
    normed_low = normed.astype(BF16)
    bias_full = jnp.concatenate([pair_bias[:width], jnp.zeros((width,), F32), pair_bias[width:]])
    triple = (jnp.dot(normed_low, triple_weight, preferred_element_type=F32) + bias_full).astype(BF16)
    queries, near = triple[:, :width], triple[:, width:]
    if moved:
        remote = swap_cores(near, dp)
    else:
        remote = lax.all_gather(near, "seq", axis=0, tiled=True)
    far_count = place_index.astype(jnp.int32).reshape(1)
    attended_low, lse = attend(far_count, queries, near, remote, block)
    middle = flat_in + jnp.dot(attended_low, merge_weight, preferred_element_type=F32) + merge_bias

    ff_rows = ff // GROUPS
    shrink_weight = tail_pack[:, :ff_rows].reshape(ff, width)
    expand_weight = jnp.concatenate(
        [
            tail_pack[:, ff_rows + at * group_rows : ff_rows + (at + 1) * group_rows].reshape(width, width)
            for at in range(ff // width)
        ],
        axis=1,
    )
    second, norm_two_pull = jax.vjp(layer_norm, middle, gain_two, shift_two)
    second_low = second.astype(BF16)
    hidden = jnp.dot(second_low, expand_weight, preferred_element_type=F32) + expand_bias
    active, gelu_pull = jax.vjp(lambda values: jax.nn.gelu(values, approximate=True), hidden)
    active_low = active.astype(BF16)
    result = middle + jnp.dot(active_low, shrink_weight, preferred_element_type=F32) + shrink_bias
    output = result.astype(BF16)
    if moved:
        output = regroup(output, dp, moves)
    grad_shrink_weight = dot(active_low, flat_cot, 0, 0)
    grad_shrink_bias = jnp.sum(flat_cot.astype(F32), axis=0)
    active_grad = dot(flat_cot, shrink_weight, 1, 1)
    hidden_grad = gelu_pull(active_grad)[0].astype(BF16)
    grad_expand_weight = dot(second_low, hidden_grad, 0, 0)
    grad_expand_bias = jnp.sum(hidden_grad.astype(F32), axis=0)
    second_grad = dot(hidden_grad, expand_weight, 1, 1)
    middle_part, grad_gain_two, grad_shift_two = norm_two_pull(second_grad)
    middle_grad = flat_cot.astype(F32) + middle_part
    grouped = lambda value: value.astype(BF16).reshape(GROUPS, -1, width)
    tail_grads = jnp.concatenate(
        [grouped(grad_shrink_weight)] + [grouped(piece) for piece in split_columns(grad_expand_weight, width)],
        axis=1,
    )
    tail_own = sum_seq(scatter_pack(tail_grads, tail_sizes, dp), sequence_parts)

    branch_grad = middle_grad.astype(BF16)
    grad_merge_weight = dot(attended_low, branch_grad, 0, 0)
    grad_merge_bias = jnp.sum(branch_grad.astype(F32), axis=0)
    attended_grad = dot(branch_grad, merge_weight, 1, 1).astype(BF16)
    query_grad, key_grad, value_grad, far_key, far_value = attend_back(
        far_count, queries, near, remote, attended_grad, attended_low, lse, block
    )
    far_grad = jnp.concatenate([far_key, far_value], axis=1)
    pair_grad = jnp.concatenate([key_grad, value_grad], axis=1)
    if moved:
        pair_grad = pair_grad + swap_cores(far_grad, dp).astype(F32)
    else:
        pair_grad = pair_grad + lax.psum_scatter(far_grad, "seq", scatter_dimension=0, tiled=True).astype(F32)
    triple_grad = jnp.concatenate([query_grad, pair_grad.astype(BF16)], axis=1)
    grad_triple_weight = dot(normed_low, triple_grad, 0, 0)
    column_sums = jnp.sum(triple_grad.astype(F32), axis=0)
    grad_pair_bias = jnp.concatenate([column_sums[:width], column_sums[2 * width :]])
    normed_grad = dot(triple_grad, triple_weight, 1, 1)
    input_part, grad_gain_one, grad_shift_one = norm_one_pull(normed_grad)
    input_grad = middle_grad + input_part
    if moved:
        input_grad = regroup(input_grad, dp, moves)
    small_grads = [
        grad_gain_one, grad_shift_one, grad_pair_bias, grad_merge_bias,
        grad_gain_two, grad_shift_two, grad_expand_bias, grad_shrink_bias,
    ]
    lines = jnp.concatenate([piece.reshape(dp, -1) for piece in small_grads], axis=1).astype(BF16)
    lines = jnp.pad(lines[:, None], ((0, 0), (0, pad - 1), (0, width - lines.shape[1])))
    head_grads = jnp.concatenate(
        [grouped(piece) for piece in split_columns(grad_triple_weight, width)]
        + [grouped(grad_merge_weight), lines.reshape(GROUPS, -1, width)],
        axis=1,
    )
    head_own = sum_seq(scatter_pack(head_grads, head_sizes, dp), sequence_parts)

    piece_rows = chosen[4].shape[0]
    cut = lambda pack, at, size: pack[at : at + size]
    own_triple = jnp.concatenate([cut(head_own, at * piece_rows, piece_rows) for at in range(3)], axis=1)
    own_merge = cut(head_own, 3 * piece_rows, piece_rows)
    own_small, at = [], 0
    for size in widths:
        own_small.append(head_own[4 * piece_rows, at : at + size])
        at += size
    shrink_rows = chosen[10].shape[0]
    own_shrink = tail_own[:shrink_rows]
    own_expand = jnp.concatenate(
        [cut(tail_own, shrink_rows + at * piece_rows, piece_rows) for at in range(ff // width)], axis=1
    )
    own = [
        own_small[0], own_small[1], own_triple, own_small[2], own_merge, own_small[3],
        own_small[4], own_small[5], own_expand, own_small[6], own_shrink, own_small[7],
    ]
    shape = (length, count, width)
    return (output.reshape(shape), input_grad.reshape(shape)) + tuple(
        place(grad, master, tie_slots[number]) for number, (grad, master) in enumerate(zip(own, masters))
    )


def solution(mesh):
    in_specs = (
        P("seq", "dp", None),
        P("seq", "dp", None),
        P(),
        P(None, "dp"),
        P(None, "dp"),
        P(None, "dp", None),
        P(None, "dp"),
        P(None, "dp", None),
        P(None, "dp"),
        P(None, "dp"),
        P(None, "dp"),
        P(None, "dp", None),
        P(None, "dp"),
        P(None, "dp", None),
        P(None, "dp"),
    )
    out_specs = (
        P("seq", "dp", None),
        P("seq", "dp", None),
        P(None, "dp"),
        P(None, "dp"),
        P(None, "dp", None),
        P(None, "dp"),
        P(None, "dp", None),
        P(None, "dp"),
        P(None, "dp"),
        P(None, "dp"),
        P(None, "dp", None),
        P(None, "dp"),
        P(None, "dp", None),
        P(None, "dp"),
    )
    sizes = dict(mesh.shape)
    body = per_device_fast if (sizes["dp"], sizes["seq"]) == (16, 2) else per_device
    return jax.shard_map(
        body, mesh=mesh, in_specs=in_specs, out_specs=out_specs, check_vma=False
    )
```

```python
import functools
import math

import jax
import jax.numpy as jnp
from jax import lax
from jax.experimental import pallas as pl
from jax.experimental.pallas import tpu as pltpu
from jax.sharding import PartitionSpec as P

H = 12
GROUPS = 16
SMALL = (0, 1, 3, 5, 6, 7, 9, 11)
EPSILON = 1e-05
NEGATIVE = -1e30
F32 = jnp.float32
BF16 = jnp.bfloat16
MEGA = 1024 * 1024
VMEM = {"pack": 60, "qkv": 28, "merge": 14, "ffn": 52, "close": 40, "unpack": 36}


def layer_norm(values, gain, shift):
    average = jnp.mean(values, axis=-1, keepdims=True)
    centered = values - average
    variance = jnp.mean(centered * centered, axis=-1, keepdims=True)
    return centered * lax.rsqrt(variance + EPSILON) * gain + shift


def dot(left, right, left_dim, right_dim):
    return lax.dot_general(
        left, right, (((left_dim,), (right_dim,)), ((), ())), preferred_element_type=F32
    )


def pair_masks():
    lane = lax.broadcasted_iota(jnp.int32, (1, 128), 1)
    low = (lane < 64).astype(F32)
    return low, 1.0 - low


def causal(scores, block):
    key = lax.broadcasted_iota(jnp.int32, (block, block), 0)
    query = lax.broadcasted_iota(jnp.int32, (block, block), 1)
    return jnp.where(key <= query, scores, NEGATIVE)


def attend_kernel(count, q_ref, k_ref, v_ref, rk_ref, rv_ref, o_ref, lse_ref, *, block):
    rows = q_ref.shape[0]
    masks = pair_masks()
    for index in range(rows // block):
        here = slice(index * block, (index + 1) * block)
        size = (index + 1) * block
        state = []
        parts = []
        for head in range(2):
            query = q_ref[here, :] * (masks[head] * 0.125).astype(BF16)
            parts.append(query)
            scores = dot(k_ref[0:size, :], query, 1, 1)
            last = causal(scores[size - block :], block)
            top = jnp.max(last, axis=0, keepdims=True)
            if index:
                scores = jnp.concatenate([scores[: size - block], last], axis=0)
                top = jnp.max(scores, axis=0, keepdims=True)
            else:
                scores = last
            lifted = jnp.exp(scores - top)
            total = jnp.sum(lifted, axis=0, keepdims=True)
            state += [top, total, dot(v_ref[0:size, :], lifted.astype(BF16), 0, 0)]

        def far(step, state):
            start = pl.multiple_of(step * rows, rows)
            keys = rk_ref[pl.ds(start, rows), :]
            values = rv_ref[pl.ds(start, rows), :]
            result = []
            for head in range(2):
                top, total, gathered = state[3 * head : 3 * head + 3]
                scores = dot(keys, parts[head], 1, 1)
                new_top = jnp.maximum(top, jnp.max(scores, axis=0, keepdims=True))
                factor = jnp.exp(top - new_top)
                lifted = jnp.exp(scores - new_top)
                total = total * factor + jnp.sum(lifted, axis=0, keepdims=True)
                gathered = gathered * factor + dot(values, lifted.astype(BF16), 0, 0)
                result += [new_top, total, gathered]
            return tuple(result)

        top0, total0, sum0, top1, total1, sum1 = lax.fori_loop(0, count[0], far, tuple(state))
        joined = jnp.concatenate([sum0[:64] / total0, sum1[64:] / total1], axis=0)
        o_ref[here, :] = jnp.transpose(joined).astype(BF16)
        lse_ref[0, 0:1, here] = top0 + jnp.log(total0)
        lse_ref[0, 1:2, here] = top1 + jnp.log(total1)


def attend(count, queries, near, remote, block, first=0, pairs=None):
    rows, width = queries.shape
    total = width // 128
    pairs = pairs or total
    far_rows = remote.shape[0]
    column = lambda size, offset: pl.BlockSpec((size, 128), lambda h, c: (0, h + offset))
    return pl.pallas_call(
        functools.partial(attend_kernel, block=block),
        grid_spec=pltpu.PrefetchScalarGridSpec(
            num_scalar_prefetch=1,
            grid=(pairs,),
            in_specs=[
                column(rows, first),
                column(rows, first),
                column(rows, first + total),
                column(far_rows, first),
                column(far_rows, first + total),
            ],
            out_specs=[column(rows, 0), pl.BlockSpec((1, 2, rows), lambda h, c: (h, 0, 0))],
        ),
        out_shape=[
            jax.ShapeDtypeStruct((rows, pairs * 128), BF16),
            jax.ShapeDtypeStruct((pairs, 2, rows), F32),
        ],
        compiler_params=pltpu.CompilerParams(vmem_limit_bytes=16 * MEGA),
        cost_estimate=pl.CostEstimate(
            flops=rows * rows * pairs * 100 // 1, bytes_accessed=rows * pairs * 150 // 1, transcendentals=0
        ),
        name="attend",
    )(count, queries, near, near, remote, remote)


def attend_back_kernel(
    count, q_ref, k_ref, v_ref, rk_ref, rv_ref, do_ref, o_ref, lse_ref,
    dq_ref, dk_ref, dv_ref, rdk_ref, rdv_ref, dq_sum, dk_sum, dv_sum, *, block,
):
    rows = q_ref.shape[0]
    far_rows = rk_ref.shape[0]
    masks = pair_masks()
    blocks = rows // block

    def prepare(index):
        here = slice(index * block, (index + 1) * block)
        out_grad = do_ref[here, :]
        product = jnp.transpose(out_grad.astype(F32) * o_ref[here, :].astype(F32))
        result = []
        for head in range(2):
            query = q_ref[here, :] * (masks[head] * 0.125).astype(BF16)
            masked = out_grad * masks[head].astype(BF16)
            delta = jnp.sum(product[64 * head : 64 * head + 64], axis=0, keepdims=True)
            lse = lse_ref[0, head : head + 1, here]
            result.append((query, masked, delta, lse))
        return result

    def terms(ready, keys, values, diagonal):
        key_grad = value_grad = query_grad = 0.0
        for head in range(2):
            query, masked, delta, lse = ready[head]
            scores = dot(keys, query, 1, 1)
            if diagonal:
                size = scores.shape[0]
                last = causal(scores[size - block :], block)
                if size > block:
                    scores = jnp.concatenate([scores[: size - block], last], axis=0)
                else:
                    scores = last
            probs = jnp.exp(scores - lse)
            prob_grad = dot(values, masked, 1, 1)
            score_grad = (probs * (prob_grad - delta)).astype(BF16)
            value_grad += dot(probs.astype(BF16), masked, 1, 0)
            key_grad += dot(score_grad, query, 1, 0)
            part = keys * (masks[head] * 0.125).astype(BF16)
            query_grad += dot(part, score_grad, 0, 0)
        return key_grad, value_grad, query_grad

    for index in reversed(range(blocks)):
        here = slice(index * block, (index + 1) * block)
        size = (index + 1) * block
        key_grad, value_grad, query_grad = terms(
            prepare(index), k_ref[0:size, :], v_ref[0:size, :], True
        )
        if index == blocks - 1:
            dk_sum[...] = key_grad
            dv_sum[...] = value_grad
        else:
            dk_sum[0:size, :] += key_grad
            dv_sum[0:size, :] += value_grad
        dq_sum[:, here] = query_grad

    def far(step, unused):
        start = pl.multiple_of(step * rows, rows)
        spot = pl.ds(start, rows)
        keys = rk_ref[spot, :]
        values = rv_ref[spot, :]
        key_total = value_total = 0.0
        for index in range(blocks):
            here = slice(index * block, (index + 1) * block)
            key_grad, value_grad, query_grad = terms(prepare(index), keys, values, False)
            key_total += key_grad
            value_total += value_grad
            dq_sum[:, here] += query_grad
        rdk_ref[spot, :] = key_total.astype(BF16)
        rdv_ref[spot, :] = value_total.astype(BF16)
        return unused

    lax.fori_loop(0, count[0], far, 0)

    def clear(step, unused):
        spot = pl.ds(pl.multiple_of(step * rows, rows), rows)
        rdk_ref[spot, :] = jnp.zeros((rows, 128), BF16)
        rdv_ref[spot, :] = jnp.zeros((rows, 128), BF16)
        return unused

    lax.fori_loop(count[0], far_rows // rows, clear, 0)
    dq_ref[...] = jnp.transpose(dq_sum[...]).astype(BF16)
    dk_ref[...] = dk_sum[...]
    dv_ref[...] = dv_sum[...]


def attend_back(count, queries, near, remote, out_grad, attended, lse, block, first=0):
    rows, width = attended.shape
    pairs, total = width // 128, queries.shape[1] // 128
    far_rows = remote.shape[0]
    column = lambda size, offset: pl.BlockSpec((size, 128), lambda h, c: (0, h + offset))
    return pl.pallas_call(
        functools.partial(attend_back_kernel, block=block),
        grid_spec=pltpu.PrefetchScalarGridSpec(
            num_scalar_prefetch=1,
            grid=(pairs,),
            in_specs=[
                column(rows, first),
                column(rows, first),
                column(rows, first + total),
                column(far_rows, first),
                column(far_rows, first + total),
                column(rows, first),
                column(rows, 0),
                pl.BlockSpec((1, 2, rows), lambda h, c: (h, 0, 0)),
            ],
            out_specs=[
                column(rows, 0),
                column(rows, 0),
                column(rows, 0),
                column(far_rows, 0),
                column(far_rows, 0),
            ],
            scratch_shapes=[
                pltpu.VMEM((128, rows), F32),
                pltpu.VMEM((rows, 128), F32),
                pltpu.VMEM((rows, 128), F32),
            ],
        ),
        out_shape=[
            jax.ShapeDtypeStruct((rows, width), BF16),
            jax.ShapeDtypeStruct((rows, width), F32),
            jax.ShapeDtypeStruct((rows, width), F32),
            jax.ShapeDtypeStruct((far_rows, width), BF16),
            jax.ShapeDtypeStruct((far_rows, width), BF16),
        ],
        compiler_params=pltpu.CompilerParams(vmem_limit_bytes=16 * MEGA),
        cost_estimate=pl.CostEstimate(
            flops=2 * rows * rows * width // 1, bytes_accessed=rows * width * 3 // 1, transcendentals=0
        ),
        name="attend_back",
    )(count, queries, near, near, remote, remote, out_grad, attended, lse)


def pairs_of(count, target):
    return [(index, target(index)) for index in range(count)]


def swap_cores(value, count):
    return lax.ppermute(value, "dp", pairs_of(count, lambda index: index ^ 1))


def swap_seq(value):
    return lax.ppermute(value, "seq", [(0, 1), (1, 0)])


def exchange_rows(value, dp=16):
    pairs = []
    for index in range(0, dp, 2):
        left, right = (index + 1) * 2, index * 2 + 1
        pairs += [(left, right), (right, left)]
    return lax.ppermute(value, ("dp", "seq"), pairs)


def regroup(value, dp, moves):
    return jnp.where(moves, exchange_rows(value, dp), value)


def split_columns(value, width):
    return [value[:, at : at + width] for at in range(0, value.shape[1], width)]


def gather_pack(blocks, dp):
    sizes = [block.shape[0] for block in blocks]
    packed = lax.all_gather(jnp.concatenate(blocks, axis=0), "dp", axis=0)
    if dp == GROUPS:
        return packed
    parts, at = [], 0
    for size in sizes:
        part = packed[:, at : at + size]
        parts.append(part.reshape(GROUPS, -1, part.shape[2]))
        at += size
    return jnp.concatenate(parts, axis=1)


def scatter_pack(packed, sizes, dp):
    if dp != GROUPS:
        parts, at = [], 0
        for size in sizes:
            whole = size * dp // GROUPS
            part = packed[:, at : at + whole]
            parts.append(part.reshape(dp, size, part.shape[2]))
            at += whole
        packed = jnp.concatenate(parts, axis=1)
    return lax.psum_scatter(packed, "dp", scatter_dimension=0)


def sum_seq(value, sequence_parts):
    if sequence_parts == 2:
        return value.astype(F32) + swap_seq(value).astype(F32)
    return lax.psum(value, "seq").astype(F32)


def place(grad, master, slot):
    marker = (jnp.arange(master.shape[0]) == slot).astype(F32)
    return marker.reshape((-1,) + (1,) * grad.ndim) * grad[None]


def spot(place):
    index = place[0]
    return index >> 2, (index >> 1) & 1, index & 1, place[1]


def whole(shape):
    return pl.BlockSpec(shape, lambda *unused: (0,) * len(shape))


ANYWHERE = pl.BlockSpec(memory_space=pl.ANY)


def kernel_call(body, scalars, in_specs, args, out_specs, out_shape, scratch, name, flops, moved):
    return pl.pallas_call(
        body,
        grid_spec=pltpu.PrefetchScalarGridSpec(
            num_scalar_prefetch=len(scalars),
            grid=(1,),
            in_specs=in_specs,
            out_specs=out_specs,
            scratch_shapes=scratch,
        ),
        out_shape=out_shape,
        compiler_params=pltpu.CompilerParams(vmem_limit_bytes=VMEM[name] * MEGA),
        cost_estimate=pl.CostEstimate(flops=flops // 10, bytes_accessed=moved // 10, transcendentals=0),
        name=name,
    )(*scalars, *args)


def pack_kernel(slots, place, *refs):
    masters, (head, tail, lines) = refs[:12], refs[12:]
    part, width = masters[4].shape
    lines[...] = jnp.zeros_like(lines)
    for row, number in enumerate(SMALL):
        master = masters[number]
        lines[row : row + 1, 0 : master.shape[1]] = master[pl.ds(slots[number], 1), :]
    for at in range(3):
        head[at * part : (at + 1) * part, :] = masters[2][:, at * width : (at + 1) * width].astype(BF16)
    head[3 * part : 4 * part, :] = masters[4][...].astype(BF16)
    head[4 * part :, :] = lines[...].astype(BF16)

    @pl.when(place[1] == 0)
    def shrink():
        tail[...] = masters[10][...].astype(BF16)

    @pl.when(place[1] != 0)
    def expand():
        for at in range(masters[8].shape[1] // width):
            tail[at * part : (at + 1) * part, :] = masters[8][:, at * width : (at + 1) * width].astype(BF16)


def pack(slots, place, masters):
    specs = []
    for number, master in enumerate(masters):
        if master.ndim == 2:
            specs.append(whole(master.shape))
        else:
            specs.append(
                pl.BlockSpec(
                    (None,) + master.shape[1:],
                    functools.partial(lambda step, slots, place, number: (slots[number], 0, 0), number=number),
                )
            )
    part, width = masters[4].shape[1:]
    rows = 4 * part + 16
    tail_rows = masters[10].shape[1]
    return kernel_call(
        pack_kernel, (slots, place), specs, masters,
        [whole((rows, width)), whole((tail_rows, width))],
        [jax.ShapeDtypeStruct((rows, width), BF16), jax.ShapeDtypeStruct((tail_rows, width), BF16)],
        [pltpu.VMEM((16, width), F32)], "pack", 0, 4 * rows * width * 6,
    )


def shift_z(value):
    return lax.ppermute(value, "dp", pairs_of(16, lambda index: (index + 4) % 16))


def swap_x(value):
    return lax.ppermute(value, "dp", pairs_of(16, lambda index: index ^ 2))


def after(value, *earlier):
    return lax.optimization_barrier((value,) + earlier)[0]


class Lane:
    def __init__(self, move, depth=2):
        self.move, self.depth, self.sent = move, depth, []

    def __call__(self, value, move=None):
        if len(self.sent) >= self.depth:
            value = after(value, self.sent[-self.depth])
        self.sent.append((move or self.move)(value))
        return self.sent[-1]


def ring_slots(z, x):
    slots = []
    for step in range(4):
        base = ((z - step) & 3) * 4
        slots += [base + x * 2, base + (1 - x) * 2]
    return slots


def gather(head, tail, values, out_grad, moves):
    z, x, y = Lane(shift_z, 2), Lane(swap_x, 2), Lane(swap_seq, 2)
    head, tail = [head], [tail]
    head_x, tail_x, tail_y, tail_xy = [], [], [], []
    head.append(z(head[0]))
    head_x.append(x(head[0]))
    tail_y.append(y(tail[0]))
    head.append(z(head[1]))
    tail_x.append(x(tail[0]))
    new_values = y(values, exchange_rows)
    tail.append(z(tail[0]))
    head_x.append(x(head[1]))
    new_grad = y(out_grad, exchange_rows)
    head.append(z(head[2]))
    head_x.append(x(head[2]))
    tail_xy.append(y(tail_x[0]))
    tail.append(z(tail[1]))
    head_x.append(x(head[3]))
    tail_y.append(y(tail[1]))
    tail_x.append(x(tail[1]))
    values = after(jnp.where(moves, new_values, values), tail_y[1], tail_xy[0], tail[2])
    out_grad = jnp.where(moves, new_grad, out_grad)
    tail.append(z(tail[2]))
    tail_xy.append(y(tail_x[1]))
    tail_x.append(x(tail[2]))
    tail_y.append(y(tail[2]))
    tail_x.append(x(tail[3]))
    mix = lambda first, second: [piece for pair in zip(first, second) for piece in pair]

    def rest(first, second):
        tail_xy.append(y(after(tail_x[2], first)))
        tail_y.append(y(after(tail[3], first)))
        tail_xy.append(y(after(tail_x[3], second)))
        return mix(tail_y, tail_xy), out_grad

    return mix(head, head_x), mix(tail, tail_x), values, rest


def row_sum(value):
    return jnp.sum(value, axis=0, keepdims=True)


def normalise(values):
    average = jnp.mean(values, axis=-1, keepdims=True)
    centered = values - average
    scale = lax.rsqrt(jnp.mean(centered * centered, axis=-1, keepdims=True) + EPSILON)
    return centered * scale, scale


def norm_back(grad, gain, shape, scale):
    inner = grad * gain
    first = jnp.mean(inner, axis=-1, keepdims=True)
    second = jnp.mean(inner * shape, axis=-1, keepdims=True)
    return scale * (inner - first - shape * second)


def qkv_kernel(place, x_ref, *refs):
    pieces, (packed, n1_ref, q_ref, kv_ref, v48, v96, v192, sems) = refs[:16], refs[16:]
    z, x, core, half = spot(place)
    slots = ring_slots(z, x)
    slots = [slot + core for slot in slots] + [slot + 1 - core for slot in slots]
    copies = [
        pltpu.make_async_copy(piece, packed.at[slots[number]], sems.at[number])
        for number, piece in enumerate(pieces)
    ]
    for copy in copies:
        copy.start()
    width = x_ref.shape[1]
    part = width // GROUPS
    shape, unused = normalise(x_ref[...].astype(F32))
    for copy in copies:
        copy.wait()
    for group in range(GROUPS):
        lines = packed[group, 4 * part : 4 * part + 16, :].astype(F32)[0:8]
        for out in (v48, v96, v192):
            size = out.shape[1] // GROUPS
            out[:, group * size : (group + 1) * size] = lines[:, :size]
    normed = (shape * v48[0:1, :] + v48[1:2, :]).astype(BF16)
    n1_ref[...] = normed
    for at in range(3):
        weight = packed[:, at * part : (at + 1) * part, :].reshape(width, width)
        result = dot(normed, weight, 1, 0)
        if at == 0:
            q_ref[...] = (result + v96[2:3, :width]).astype(BF16)
        elif at == 1:
            kv_ref[:, :width] = result.astype(BF16)
        else:
            kv_ref[:, width:] = (result + v96[2:3, width:]).astype(BF16)


def qkv(place, values, pieces):
    rows, width = values.shape
    shapes = [
        ((GROUPS,) + pieces[0].shape, BF16), ((rows, width), BF16), ((rows, width), BF16), ((rows, 2 * width), BF16),
        ((8, width), F32), ((8, 2 * width), F32), ((8, 4 * width), F32),
    ]
    return kernel_call(
        qkv_kernel, (place,), [whole(values.shape)] + [ANYWHERE] * 16, [values] + pieces,
        [whole(shape) for shape, unused in shapes],
        [jax.ShapeDtypeStruct(shape, dtype) for shape, dtype in shapes],
        [pltpu.SemaphoreType.DMA((16,))], "qkv", 6 * rows * width * width, 20 * width * width,
    )


def merge_kernel(x_ref, o1_ref, o2_ref, weight, v48, m_ref, n2_ref):
    width = x_ref.shape[1]
    attended = jnp.concatenate([o1_ref[...], o2_ref[...]], axis=1)
    middle = x_ref[...].astype(F32) + dot(attended, weight[...].reshape(width, width), 1, 0) + v48[3:4, :]
    m_ref[...] = middle
    shape, unused = normalise(middle)
    n2_ref[...] = (shape * v48[4:5, :] + v48[5:6, :]).astype(BF16)


def merge_spec(packed):
    part = packed.shape[2] // GROUPS
    return pl.BlockSpec((GROUPS, part, packed.shape[2]), lambda *unused: (0, 3, 0))


def merge(values, attended, packed, v48):
    rows, width = values.shape
    return kernel_call(
        merge_kernel, (),
        [whole(values.shape)] + [whole(piece.shape) for piece in attended] + [merge_spec(packed), whole(v48.shape)],
        [values] + attended + [packed, v48], [whole(values.shape)] * 2,
        [jax.ShapeDtypeStruct((rows, width), F32), jax.ShapeDtypeStruct((rows, width), BF16)],
        [], "merge", 2 * rows * width * width, 12 * rows * width,
    )


def gelu_pair(value):
    scale, cubic = math.sqrt(2 / math.pi), 0.044715
    square = value * value
    bent = jnp.tanh(scale * value * (1.0 + cubic * square))
    half = 0.5 * (1.0 + bent)
    slope = half + 0.5 * value * (1.0 - bent * bent) * (scale * (1.0 + 3.0 * cubic * square))
    return value * half, slope


def ffn_kernel(place, *refs):
    pieces, refs = refs[:32], refs[32:]
    m_ref, n2_ref, gy_ref, merge_weight, v48, v192, out_ref, dm_ref, dz_ref, do_ref, g48, g192 = refs[:12]
    outs, (weights, grads, y, dn2, n2_t, u, df, in_sems, out_sems) = refs[12:20], refs[20:]
    z, x, core, half = spot(place)
    slots = ring_slots(z, x)
    spots = [(slot + core, half) for slot in slots] + [(slot + core, 1 - half) for slot in slots]
    spots += [(slot + 1 - core, half) for slot in slots] + [(slot + 1 - core, 1 - half) for slot in slots]
    copies = [
        pltpu.make_async_copy(piece, weights.at[spots[number][0], spots[number][1]], in_sems.at[number])
        for number, piece in enumerate(pieces)
    ]
    for copy in copies:
        copy.start()
    width = m_ref.shape[1]
    part = width // GROUPS
    n2_t[...] = jnp.transpose(n2_ref[...])
    y[...] = jnp.zeros_like(y)
    dn2[...] = jnp.zeros_like(dn2)
    for copy in copies:
        copy.wait()

    def step(at, unused):
        first = pl.multiple_of(at * 4, 4)
        lines = pl.ds(pl.multiple_of(at * part, 16), part)
        chunk = 256
        for column in range(0, width, chunk):
            place_in = pl.ds(pl.multiple_of(at * width + column, 128), chunk)
            expand = weights[:, 1, lines, column : column + chunk].reshape(width, chunk)
            hidden = dot(n2_ref[...], expand, 1, 0) + v192[6:7, place_in]
            shrink = weights[pl.ds(first, 4), 0].reshape(width, width)[column : column + chunk]
            active, slope = gelu_pair(hidden)
            u[:, column : column + chunk] = active.astype(BF16)
            hidden_grad = (dot(gy_ref[...], shrink, 1, 1) * slope).astype(BF16)
            df[:, column : column + chunk] = hidden_grad
            g192[0:1, place_in] = row_sum(hidden_grad.astype(F32))
        shrink = weights[pl.ds(first, 4), 0].reshape(width, width)
        expand = weights[:, 1, lines, :].reshape(width, width)
        y[...] += dot(u[...], shrink, 1, 0)
        dn2[...] += dot(df[...], expand, 1, 1)
        grads[pl.ds(first, 4), 0] = dot(u[...], gy_ref[...], 0, 0).astype(BF16).reshape(4, 4 * part, width)
        grads[:, 1, lines, :] = dot(n2_t[...], df[...], 1, 0).astype(BF16).reshape(GROUPS, part, width)
        return unused

    lax.fori_loop(0, 4, step, 0)
    copies = []
    for order in range(4):
        base = ((z - order) & 3) * 4
        for number, out in ((0, outs[2 * order]), (1, outs[2 * order + 1])):
            side = core if number == 0 else 1 - core
            for kind in range(2):
                for column in range(2):
                    source = base + (x if column == 0 else 1 - x) * 2 + side
                    copies.append(
                        pltpu.make_async_copy(
                            grads.at[source, half if kind == 0 else 1 - half],
                            out.at[kind, column],
                            out_sems.at[len(copies)],
                        )
                    )
    for copy in copies:
        copy.start()
    middle = m_ref[...]
    out_ref[...] = (middle + y[...] + v48[7:8, :]).astype(BF16)
    shape, scale = normalise(middle)
    second_grad = dn2[...]
    out_grad = gy_ref[...].astype(F32)
    middle_grad = out_grad + norm_back(second_grad, v48[4:5, :], shape, scale)
    dm_ref[...] = middle_grad
    low = middle_grad.astype(BF16)
    dz_ref[...] = low
    g48[...] = jnp.zeros_like(g48)
    g48[3:4, :] = row_sum(low.astype(F32))
    g48[4:5, :] = row_sum(shape * second_grad)
    g48[5:6, :] = row_sum(second_grad)
    g48[7:8, :] = row_sum(out_grad)
    do_ref[...] = dot(low, merge_weight[...].reshape(width, width), 1, 1).astype(BF16)
    for copy in copies:
        copy.wait()


def ffn(place, pieces, middle, second, out_grad, packed, v48, v192):
    rows, width = middle.shape
    ff = 4 * width
    tail_rows = pieces[0].shape[0]
    shapes = [
        ((rows, width), BF16), ((rows, width), F32), ((rows, width), BF16), ((rows, width), BF16),
        ((8, width), F32), ((8, ff), F32),
    ]
    part = jax.ShapeDtypeStruct((2, 2, tail_rows, width), BF16)
    pack_shape = (GROUPS, 2, tail_rows, width)
    results = kernel_call(
        ffn_kernel, (place,),
        [ANYWHERE] * 32
        + [whole(middle.shape), whole(second.shape), whole(out_grad.shape), merge_spec(packed), whole(v48.shape), whole(v192.shape)],
        pieces + [middle, second, out_grad, packed, v48, v192],
        [whole(shape) for shape, unused in shapes] + [ANYWHERE] * 8,
        [jax.ShapeDtypeStruct(shape, dtype) for shape, dtype in shapes] + [part] * 8,
        [
            pltpu.VMEM(pack_shape, BF16), pltpu.VMEM(pack_shape, BF16),
            pltpu.VMEM((rows, width), F32), pltpu.VMEM((rows, width), F32), pltpu.VMEM((width, rows), BF16),
            pltpu.VMEM((rows, width), BF16), pltpu.VMEM((rows, width), BF16),
            pltpu.SemaphoreType.DMA((32,)), pltpu.SemaphoreType.DMA((32,)),
        ],
        "ffn", 12 * rows * width * ff, 8 * width * ff,
    )
    return results[:6], results[6:]


def close_kernel(
    place, n1_ref, x_ref, q1, k1, v1, far_k1, far_v1, q2, k2, v2, far_k2, far_v2, o1, o2,
    dz_ref, dm_ref, packed, v48, g48_in, g192, *refs,
):
    join = lambda first, second: jnp.concatenate([first[...], second[...]], axis=1)
    grad_ref, outs, (grads, g48, g96, dt, sems) = refs[0], refs[1:9], refs[9:]
    z, x, core, half = spot(place)
    width = x_ref.shape[1]
    part = width // GROUPS
    normed_t = jnp.transpose(n1_ref[...])
    normed_grad = None
    for at in range(3):
        if at == 0:
            dt[...] = join(q1, q2)
        elif at == 1:
            dt[...] = (join(k1, k2) + join(far_k1, far_k2).astype(F32)).astype(BF16)
        else:
            dt[...] = (join(v1, v2) + join(far_v1, far_v2).astype(F32)).astype(BF16)
        if at != 1:
            g96[2:3, (at // 2) * width : (at // 2 + 1) * width] = row_sum(dt[...].astype(F32))
        weight = packed[:, at * part : (at + 1) * part, :].reshape(width, width)
        term = dot(dt[...], weight, 1, 1)
        normed_grad = term if normed_grad is None else normed_grad + term
        grads[:, at * part : (at + 1) * part, :] = dot(normed_t, dt[...], 1, 0).astype(BF16).reshape(GROUPS, part, width)
    grads[:, 3 * part : 4 * part, :] = dot(join(o1, o2), dz_ref[...], 0, 0).astype(BF16).reshape(GROUPS, part, width)
    shape, scale = normalise(x_ref[...].astype(F32))
    g48[...] = g48_in[...]
    g48[0:1, :] = row_sum(shape * normed_grad)
    g48[1:2, :] = row_sum(normed_grad)
    row = lax.broadcasted_iota(jnp.int32, (16, 1), 0)
    for group in range(GROUPS):
        lines = jnp.concatenate([g48[:, group * part : (group + 1) * part], jnp.zeros((8, part), F32)], axis=0)
        grads[group, 4 * part :, :] = jnp.zeros((16, width), BF16)
        pair = g96[2:3, group * 2 * part : (group + 1) * 2 * part]
        wide = g192[0:1, group * 4 * part : (group + 1) * 4 * part]
        spread = jnp.where(row == 6, wide, 0.0)
        left = jnp.where(row == 2, pair, 0.0)
        grads[group, 4 * part :, 0 : 4 * part] = spread.astype(BF16)
        grads[group, 4 * part :, 0 : 2 * part] = (spread[:, : 2 * part] + left).astype(BF16)
        keep = jnp.where((row == 2) | (row == 6), 0.0, lines) + spread[:, :part] + left[:, :part]
        grads[group, 4 * part :, 0:part] = keep.astype(BF16)
    copies = []
    for order in range(4):
        base = ((z - order) & 3) * 4
        for number, out in ((0, outs[2 * order]), (1, outs[2 * order + 1])):
            side = core if number == 0 else 1 - core
            for column in range(2):
                source = base + (x if column == 0 else 1 - x) * 2 + side
                copies.append(pltpu.make_async_copy(grads.at[source], out.at[column], sems.at[len(copies)]))
    for copy in copies:
        copy.start()
    grad_ref[...] = (dm_ref[...] + norm_back(normed_grad, v48[0:1, :], shape, scale)).astype(BF16)
    for copy in copies:
        copy.wait()


def close(place, args):
    rows, width = args[0].shape
    packed = args[16]
    head_rows = packed.shape[1]
    part = jax.ShapeDtypeStruct((2, head_rows, width), BF16)
    results = kernel_call(
        close_kernel, (place,), [whole(arg.shape) for arg in args], args,
        [whole((rows, width))] + [ANYWHERE] * 8,
        [jax.ShapeDtypeStruct((rows, width), BF16)] + [part] * 8,
        [
            pltpu.VMEM(packed.shape, BF16), pltpu.VMEM((8, width), F32), pltpu.VMEM((8, 2 * width), F32),
            pltpu.VMEM((rows, width), BF16), pltpu.SemaphoreType.DMA((16,)),
        ],
        "close", 14 * rows * width * width, 20 * width * width,
    )
    return results[0], results[1:]


def unpack_kernel(slots, place, head, head_far, tail, tail_far, *outs):
    part, width = outs[4].shape[1:]
    total = head[...].astype(F32) + head_far[...].astype(F32)
    near, far = tail[...].astype(F32), tail_far[...].astype(F32)
    first = place[1] == 0
    shrink = jnp.where(first, near, far)
    expand = jnp.where(first, far, near)
    for row, number in enumerate(SMALL):
        out = outs[number]
        size = out.shape[1]
        line = total[4 * part + row : 4 * part + row + 1, :size]
        row_at = lax.broadcasted_iota(jnp.int32, out.shape, 0)
        out[...] = jnp.where(row_at == slots[number], line, 0.0)
    for slot in range(outs[2].shape[0]):
        chosen = lambda number, value: jnp.where(slots[number] == slot, value, 0.0)
        for at in range(3):
            outs[2][slot, :, at * width : (at + 1) * width] = chosen(2, total[at * part : (at + 1) * part])
        outs[4][slot] = chosen(4, total[3 * part : 4 * part])
        for at in range(outs[8].shape[2] // width):
            outs[8][slot, :, at * width : (at + 1) * width] = chosen(8, expand[at * part : (at + 1) * part])
        outs[10][slot] = chosen(10, shrink)


def unpack(slots, place, parts, masters):
    return kernel_call(
        unpack_kernel, (slots, place), [whole(part.shape) for part in parts], parts,
        [whole(master.shape) for master in masters],
        [jax.ShapeDtypeStruct(master.shape, F32) for master in masters],
        [], "unpack", 0, 8 * 1024 * 1024,
    )


def per_device_fast(inputs, cotangent, tie_slots, *masters):
    length, count, width = inputs.shape
    block = math.gcd(length, 256)
    index, half = lax.axis_index("dp"), lax.axis_index("seq")
    place = jnp.stack([index, half]).astype(jnp.int32)
    core = index % 2
    moves = core != half
    head, tail = pack(tie_slots, place, masters)
    head_pieces, tail_pieces, values, rest = gather(
        head, tail, inputs.reshape(length, width), cotangent.reshape(length, width), moves
    )
    head_pieces = head_pieces + [swap_cores(piece, 16) for piece in head_pieces]
    packed, normed, queries, near, v48, v96, v192 = qkv(place, values, head_pieces)
    remote = swap_cores(near, 16)
    far_count = core.astype(jnp.int32).reshape(1)
    half_pairs = width // 256
    queries = after(queries, tail_pieces[4], tail_pieces[3])
    attended, lse = [None, None], [None, None]
    attended[0], lse[0] = attend(far_count, queries, near, remote, block, 0, half_pairs)
    queries = after(queries, attended[0])
    attended[1], lse[1] = attend(far_count, queries, near, remote, block, half_pairs, half_pairs)
    tail_other, out_grad = rest(attended[0], attended[1])
    middle, second = merge(values, attended, packed, v48)
    late = lambda pieces, first: [
        swap_cores(after(piece, attended[1]) if number >= first else piece, 16) for number, piece in enumerate(pieces)
    ]
    tail_pieces = tail_pieces + late(tail_pieces, 8)
    tail_other = tail_other + late(tail_other, 4)
    (output, middle_grad, branch_grad, attended_grad, g48, g192), tail_parts = ffn(
        place, tail_pieces[:8] + tail_other[:8] + tail_pieces[8:] + tail_other[8:],
        middle, second, out_grad, packed, v48, v192,
    )
    z, x, y = Lane(shift_z, 2), Lane(swap_x, 2), Lane(swap_seq, 4)
    came = [swap_cores(send, 16) for send in tail_parts[1::2]]
    kept = [keep + other for keep, other in zip(tail_parts[0::2], came)]
    attended_grad = after(attended_grad, *kept)
    tail_y = {order: y(kept[order][1]) for order in (1, 2, 3, 0)}
    grads = []
    for part in range(2):
        if part:
            attended_grad = after(attended_grad, tail_y[1], grads[0])
        query_grad, key_grad, value_grad, far_key, far_value = attend_back(
            far_count, queries, near, remote, attended_grad, attended[part], lse[part], block, part * half_pairs
        )
        grads += [query_grad, key_grad, value_grad, swap_cores(far_key, 16), swap_cores(far_value, 16)]
    tail_x = {}
    tail_kept = {}
    for order in (1, 2, 3, 0):
        both = kept[order][0] + tail_y[order]
        tail_kept[order] = both[0]
        tail_x[order] = both[1]
    middle_grad = after(middle_grad, tail_x[2], tail_kept[2])
    input_grad, head_parts = close(
        place,
        [
            normed, values, *grads, *attended, branch_grad, middle_grad, packed, v48, g48, g192,
        ],
    )
    came = [swap_cores(send, 16) for send in head_parts[1::2]]
    head_kept = [keep + other for keep, other in zip(head_parts[0::2], came)]
    tail_sum = head_sum = None
    new_output = y(output, exchange_rows)
    new_input_grad = y(input_grad, exchange_rows)
    for order in (1, 2, 3, 0):
        came = x(tail_x[order])
        part = tail_kept[order] + came
        tail_sum = part if tail_sum is None else part + z(tail_sum)
        came = x(head_kept[order][1])
        part = head_kept[order][0] + came
        head_sum = part if head_sum is None else part + z(head_sum)
    output = jnp.where(moves, new_output, output)
    input_grad = jnp.where(moves, new_input_grad, input_grad).astype(F32)
    grads = unpack(
        tie_slots, place, [head_sum, y(head_sum), tail_sum, y(tail_sum)], masters
    )
    shape = (length, count, width)
    return (output.reshape(shape), input_grad.reshape(shape)) + tuple(grads)


def per_device(
    inputs,
    cotangent,
    tie_slots,
    *masters,
):
    dp, sequence_parts = lax.axis_size("dp"), lax.axis_size("seq")
    length, count, width = inputs.shape
    rows = length * count
    block = math.gcd(length, 256)
    moved = sequence_parts == 2 and dp % 2 == 0
    core = lax.axis_index("dp") % 2
    moves = core != lax.axis_index("seq")
    place_index = core if moved else lax.axis_index("seq")
    chosen = [
        lax.dynamic_index_in_dim(masters[number], tie_slots[number], 0, keepdims=False).astype(BF16)
        for number in range(12)
    ]
    part = width // dp
    ff = masters[10].shape[1] * dp
    small = jnp.concatenate([chosen[number] for number in SMALL])
    widths = [chosen[number].shape[0] for number in SMALL]
    pad = 16 * GROUPS // dp
    small = jnp.pad(small.reshape(1, -1), ((0, pad - 1), (0, width - small.shape[0])))
    head_blocks = split_columns(chosen[2], width) + [chosen[4], small]
    tail_blocks = [chosen[10]] + split_columns(chosen[8], width)
    head_sizes = [piece.shape[0] for piece in head_blocks]
    tail_sizes = [piece.shape[0] for piece in tail_blocks]
    head_pack = gather_pack(head_blocks, dp)
    flat_in = inputs.reshape(rows, width)
    flat_cot = cotangent.reshape(rows, width)
    if moved:
        flat_in = regroup(flat_in, dp, moves)
        flat_cot = regroup(flat_cot, dp, moves)
    tail_pack = gather_pack(tail_blocks, dp)

    group_rows = width // GROUPS
    matrix = lambda pack, at: pack[:, at * group_rows : (at + 1) * group_rows].reshape(width, width)
    triple_weight = jnp.concatenate([matrix(head_pack, at) for at in range(3)], axis=1)
    merge_weight = matrix(head_pack, 3)
    per_group = GROUPS // dp if dp < GROUPS else dp // GROUPS
    lines = head_pack[:, 4 * group_rows :].reshape(dp, pad, width)[:, 0]
    vectors, at = [], 0
    for size in widths:
        vectors.append(lines[:, at : at + size].reshape(-1).astype(F32))
        at += size
    gain_one, shift_one, pair_bias, merge_bias, gain_two, shift_two, expand_bias, shrink_bias = vectors

    flat_in = flat_in.astype(F32)
    normed, norm_one_pull = jax.vjp(layer_norm, flat_in, gain_one, shift_one)
    normed_low = normed.astype(BF16)
    bias_full = jnp.concatenate([pair_bias[:width], jnp.zeros((width,), F32), pair_bias[width:]])
    triple = (jnp.dot(normed_low, triple_weight, preferred_element_type=F32) + bias_full).astype(BF16)
    queries, near = triple[:, :width], triple[:, width:]
    if moved:
        remote = swap_cores(near, dp)
    else:
        remote = lax.all_gather(near, "seq", axis=0, tiled=True)
    far_count = place_index.astype(jnp.int32).reshape(1)
    attended_low, lse = attend(far_count, queries, near, remote, block)
    middle = flat_in + jnp.dot(attended_low, merge_weight, preferred_element_type=F32) + merge_bias

    ff_rows = ff // GROUPS
    shrink_weight = tail_pack[:, :ff_rows].reshape(ff, width)
    expand_weight = jnp.concatenate(
        [
            tail_pack[:, ff_rows + at * group_rows : ff_rows + (at + 1) * group_rows].reshape(width, width)
            for at in range(ff // width)
        ],
        axis=1,
    )
    second, norm_two_pull = jax.vjp(layer_norm, middle, gain_two, shift_two)
    second_low = second.astype(BF16)
    hidden = jnp.dot(second_low, expand_weight, preferred_element_type=F32) + expand_bias
    active, gelu_pull = jax.vjp(lambda values: jax.nn.gelu(values, approximate=True), hidden)
    active_low = active.astype(BF16)
    result = middle + jnp.dot(active_low, shrink_weight, preferred_element_type=F32) + shrink_bias
    output = result.astype(BF16)
    if moved:
        output = regroup(output, dp, moves)
    grad_shrink_weight = dot(active_low, flat_cot, 0, 0)
    grad_shrink_bias = jnp.sum(flat_cot.astype(F32), axis=0)
    active_grad = dot(flat_cot, shrink_weight, 1, 1)
    hidden_grad = gelu_pull(active_grad)[0].astype(BF16)
    grad_expand_weight = dot(second_low, hidden_grad, 0, 0)
    grad_expand_bias = jnp.sum(hidden_grad.astype(F32), axis=0)
    second_grad = dot(hidden_grad, expand_weight, 1, 1)
    middle_part, grad_gain_two, grad_shift_two = norm_two_pull(second_grad)
    middle_grad = flat_cot.astype(F32) + middle_part
    grouped = lambda value: value.astype(BF16).reshape(GROUPS, -1, width)
    tail_grads = jnp.concatenate(
        [grouped(grad_shrink_weight)] + [grouped(piece) for piece in split_columns(grad_expand_weight, width)],
        axis=1,
    )
    tail_own = sum_seq(scatter_pack(tail_grads, tail_sizes, dp), sequence_parts)

    branch_grad = middle_grad.astype(BF16)
    grad_merge_weight = dot(attended_low, branch_grad, 0, 0)
    grad_merge_bias = jnp.sum(branch_grad.astype(F32), axis=0)
    attended_grad = dot(branch_grad, merge_weight, 1, 1).astype(BF16)
    query_grad, key_grad, value_grad, far_key, far_value = attend_back(
        far_count, queries, near, remote, attended_grad, attended_low, lse, block
    )
    far_grad = jnp.concatenate([far_key, far_value], axis=1)
    pair_grad = jnp.concatenate([key_grad, value_grad], axis=1)
    if moved:
        pair_grad = pair_grad + swap_cores(far_grad, dp).astype(F32)
    else:
        pair_grad = pair_grad + lax.psum_scatter(far_grad, "seq", scatter_dimension=0, tiled=True).astype(F32)
    triple_grad = jnp.concatenate([query_grad, pair_grad.astype(BF16)], axis=1)
    grad_triple_weight = dot(normed_low, triple_grad, 0, 0)
    column_sums = jnp.sum(triple_grad.astype(F32), axis=0)
    grad_pair_bias = jnp.concatenate([column_sums[:width], column_sums[2 * width :]])
    normed_grad = dot(triple_grad, triple_weight, 1, 1)
    input_part, grad_gain_one, grad_shift_one = norm_one_pull(normed_grad)
    input_grad = middle_grad + input_part
    if moved:
        input_grad = regroup(input_grad, dp, moves)
    small_grads = [
        grad_gain_one, grad_shift_one, grad_pair_bias, grad_merge_bias,
        grad_gain_two, grad_shift_two, grad_expand_bias, grad_shrink_bias,
    ]
    lines = jnp.concatenate([piece.reshape(dp, -1) for piece in small_grads], axis=1).astype(BF16)
    lines = jnp.pad(lines[:, None], ((0, 0), (0, pad - 1), (0, width - lines.shape[1])))
    head_grads = jnp.concatenate(
        [grouped(piece) for piece in split_columns(grad_triple_weight, width)]
        + [grouped(grad_merge_weight), lines.reshape(GROUPS, -1, width)],
        axis=1,
    )
    head_own = sum_seq(scatter_pack(head_grads, head_sizes, dp), sequence_parts)

    piece_rows = chosen[4].shape[0]
    cut = lambda pack, at, size: pack[at : at + size]
    own_triple = jnp.concatenate([cut(head_own, at * piece_rows, piece_rows) for at in range(3)], axis=1)
    own_merge = cut(head_own, 3 * piece_rows, piece_rows)
    own_small, at = [], 0
    for size in widths:
        own_small.append(head_own[4 * piece_rows, at : at + size])
        at += size
    shrink_rows = chosen[10].shape[0]
    own_shrink = tail_own[:shrink_rows]
    own_expand = jnp.concatenate(
        [cut(tail_own, shrink_rows + at * piece_rows, piece_rows) for at in range(ff // width)], axis=1
    )
    own = [
        own_small[0], own_small[1], own_triple, own_small[2], own_merge, own_small[3],
        own_small[4], own_small[5], own_expand, own_small[6], own_shrink, own_small[7],
    ]
    shape = (length, count, width)
    return (output.reshape(shape), input_grad.reshape(shape)) + tuple(
        place(grad, master, tie_slots[number]) for number, (grad, master) in enumerate(zip(own, masters))
    )


def solution(mesh):
    in_specs = (
        P("seq", "dp", None),
        P("seq", "dp", None),
        P(),
        P(None, "dp"),
        P(None, "dp"),
        P(None, "dp", None),
        P(None, "dp"),
        P(None, "dp", None),
        P(None, "dp"),
        P(None, "dp"),
        P(None, "dp"),
        P(None, "dp", None),
        P(None, "dp"),
        P(None, "dp", None),
        P(None, "dp"),
    )
    out_specs = (
        P("seq", "dp", None),
        P("seq", "dp", None),
        P(None, "dp"),
        P(None, "dp"),
        P(None, "dp", None),
        P(None, "dp"),
        P(None, "dp", None),
        P(None, "dp"),
        P(None, "dp"),
        P(None, "dp"),
        P(None, "dp", None),
        P(None, "dp"),
        P(None, "dp", None),
        P(None, "dp"),
    )
    sizes = dict(mesh.shape)
    body = per_device_fast if (sizes["dp"], sizes["seq"]) == (16, 2) else per_device
    return jax.shard_map(
        body, mesh=mesh, in_specs=in_specs, out_specs=out_specs, check_vma=False
    )
```

```python
import functools
import math

import jax
import jax.numpy as jnp
from jax import lax
from jax.experimental import pallas as pl
from jax.experimental.pallas import tpu as pltpu
from jax.sharding import PartitionSpec as P

H = 12
GROUPS = 16
SMALL = (0, 1, 3, 5, 6, 7, 9, 11)
EPSILON = 1e-05
NEGATIVE = -1e30
F32 = jnp.float32
BF16 = jnp.bfloat16
MEGA = 1024 * 1024
VMEM = {"pack": 60, "qkv": 28, "merge": 14, "ffn": 40, "close": 40, "unpack": 36}


def layer_norm(values, gain, shift):
    average = jnp.mean(values, axis=-1, keepdims=True)
    centered = values - average
    variance = jnp.mean(centered * centered, axis=-1, keepdims=True)
    return centered * lax.rsqrt(variance + EPSILON) * gain + shift


def dot(left, right, left_dim, right_dim):
    return lax.dot_general(
        left, right, (((left_dim,), (right_dim,)), ((), ())), preferred_element_type=F32
    )


def pair_masks():
    lane = lax.broadcasted_iota(jnp.int32, (1, 128), 1)
    low = (lane < 64).astype(F32)
    return low, 1.0 - low


def causal(scores, block):
    key = lax.broadcasted_iota(jnp.int32, (block, block), 0)
    query = lax.broadcasted_iota(jnp.int32, (block, block), 1)
    return jnp.where(key <= query, scores, NEGATIVE)


def attend_kernel(count, q_ref, k_ref, v_ref, rk_ref, rv_ref, o_ref, lse_ref, *, block):
    rows = q_ref.shape[0]
    masks = pair_masks()
    for index in range(rows // block):
        here = slice(index * block, (index + 1) * block)
        size = (index + 1) * block
        state = []
        parts = []
        for head in range(2):
            query = q_ref[here, :] * (masks[head] * 0.125).astype(BF16)
            parts.append(query)
            scores = dot(k_ref[0:size, :], query, 1, 1)
            last = causal(scores[size - block :], block)
            top = jnp.max(last, axis=0, keepdims=True)
            if index:
                scores = jnp.concatenate([scores[: size - block], last], axis=0)
                top = jnp.max(scores, axis=0, keepdims=True)
            else:
                scores = last
            lifted = jnp.exp(scores - top)
            total = jnp.sum(lifted, axis=0, keepdims=True)
            state += [top, total, dot(v_ref[0:size, :], lifted.astype(BF16), 0, 0)]

        def far(step, state):
            start = pl.multiple_of(step * rows, rows)
            keys = rk_ref[pl.ds(start, rows), :]
            values = rv_ref[pl.ds(start, rows), :]
            result = []
            for head in range(2):
                top, total, gathered = state[3 * head : 3 * head + 3]
                scores = dot(keys, parts[head], 1, 1)
                new_top = jnp.maximum(top, jnp.max(scores, axis=0, keepdims=True))
                factor = jnp.exp(top - new_top)
                lifted = jnp.exp(scores - new_top)
                total = total * factor + jnp.sum(lifted, axis=0, keepdims=True)
                gathered = gathered * factor + dot(values, lifted.astype(BF16), 0, 0)
                result += [new_top, total, gathered]
            return tuple(result)

        top0, total0, sum0, top1, total1, sum1 = lax.fori_loop(0, count[0], far, tuple(state))
        joined = jnp.concatenate([sum0[:64] / total0, sum1[64:] / total1], axis=0)
        o_ref[here, :] = jnp.transpose(joined).astype(BF16)
        lse_ref[0, 0:1, here] = top0 + jnp.log(total0)
        lse_ref[0, 1:2, here] = top1 + jnp.log(total1)


def attend(count, queries, near, remote, block, first=0, pairs=None):
    rows, width = queries.shape
    total = width // 128
    pairs = pairs or total
    far_rows = remote.shape[0]
    column = lambda size, offset: pl.BlockSpec((size, 128), lambda h, c: (0, h + offset))
    return pl.pallas_call(
        functools.partial(attend_kernel, block=block),
        grid_spec=pltpu.PrefetchScalarGridSpec(
            num_scalar_prefetch=1,
            grid=(pairs,),
            in_specs=[
                column(rows, first),
                column(rows, first),
                column(rows, first + total),
                column(far_rows, first),
                column(far_rows, first + total),
            ],
            out_specs=[column(rows, 0), pl.BlockSpec((1, 2, rows), lambda h, c: (h, 0, 0))],
        ),
        out_shape=[
            jax.ShapeDtypeStruct((rows, pairs * 128), BF16),
            jax.ShapeDtypeStruct((pairs, 2, rows), F32),
        ],
        compiler_params=pltpu.CompilerParams(vmem_limit_bytes=16 * MEGA),
        cost_estimate=pl.CostEstimate(
            flops=rows * rows * pairs * 100 // 1, bytes_accessed=rows * pairs * 150 // 1, transcendentals=0
        ),
        name="attend",
    )(count, queries, near, near, remote, remote)


def attend_back_kernel(
    count, q_ref, k_ref, v_ref, rk_ref, rv_ref, do_ref, o_ref, lse_ref,
    dq_ref, dk_ref, dv_ref, rdk_ref, rdv_ref, dq_sum, dk_sum, dv_sum, *, block,
):
    rows = q_ref.shape[0]
    far_rows = rk_ref.shape[0]
    masks = pair_masks()
    blocks = rows // block

    def prepare(index):
        here = slice(index * block, (index + 1) * block)
        out_grad = do_ref[here, :]
        product = jnp.transpose(out_grad.astype(F32) * o_ref[here, :].astype(F32))
        result = []
        for head in range(2):
            query = q_ref[here, :] * (masks[head] * 0.125).astype(BF16)
            masked = out_grad * masks[head].astype(BF16)
            delta = jnp.sum(product[64 * head : 64 * head + 64], axis=0, keepdims=True)
            lse = lse_ref[0, head : head + 1, here]
            result.append((query, masked, delta, lse))
        return result

    def terms(ready, keys, values, diagonal):
        key_grad = value_grad = query_grad = 0.0
        for head in range(2):
            query, masked, delta, lse = ready[head]
            scores = dot(keys, query, 1, 1)
            if diagonal:
                size = scores.shape[0]
                last = causal(scores[size - block :], block)
                if size > block:
                    scores = jnp.concatenate([scores[: size - block], last], axis=0)
                else:
                    scores = last
            probs = jnp.exp(scores - lse)
            prob_grad = dot(values, masked, 1, 1)
            score_grad = (probs * (prob_grad - delta)).astype(BF16)
            value_grad += dot(probs.astype(BF16), masked, 1, 0)
            key_grad += dot(score_grad, query, 1, 0)
            part = keys * (masks[head] * 0.125).astype(BF16)
            query_grad += dot(part, score_grad, 0, 0)
        return key_grad, value_grad, query_grad

    for index in reversed(range(blocks)):
        here = slice(index * block, (index + 1) * block)
        size = (index + 1) * block
        key_grad, value_grad, query_grad = terms(
            prepare(index), k_ref[0:size, :], v_ref[0:size, :], True
        )
        if index == blocks - 1:
            dk_sum[...] = key_grad
            dv_sum[...] = value_grad
        else:
            dk_sum[0:size, :] += key_grad
            dv_sum[0:size, :] += value_grad
        dq_sum[:, here] = query_grad

    def far(step, unused):
        start = pl.multiple_of(step * rows, rows)
        spot = pl.ds(start, rows)
        keys = rk_ref[spot, :]
        values = rv_ref[spot, :]
        key_total = value_total = 0.0
        for index in range(blocks):
            here = slice(index * block, (index + 1) * block)
            key_grad, value_grad, query_grad = terms(prepare(index), keys, values, False)
            key_total += key_grad
            value_total += value_grad
            dq_sum[:, here] += query_grad
        rdk_ref[spot, :] = key_total.astype(BF16)
        rdv_ref[spot, :] = value_total.astype(BF16)
        return unused

    lax.fori_loop(0, count[0], far, 0)

    def clear(step, unused):
        spot = pl.ds(pl.multiple_of(step * rows, rows), rows)
        rdk_ref[spot, :] = jnp.zeros((rows, 128), BF16)
        rdv_ref[spot, :] = jnp.zeros((rows, 128), BF16)
        return unused

    lax.fori_loop(count[0], far_rows // rows, clear, 0)
    dq_ref[...] = jnp.transpose(dq_sum[...]).astype(BF16)
    dk_ref[...] = dk_sum[...]
    dv_ref[...] = dv_sum[...]


def attend_back(count, queries, near, remote, out_grad, attended, lse, block, first=0):
    rows, width = attended.shape
    pairs, total = width // 128, queries.shape[1] // 128
    far_rows = remote.shape[0]
    column = lambda size, offset: pl.BlockSpec((size, 128), lambda h, c: (0, h + offset))
    return pl.pallas_call(
        functools.partial(attend_back_kernel, block=block),
        grid_spec=pltpu.PrefetchScalarGridSpec(
            num_scalar_prefetch=1,
            grid=(pairs,),
            in_specs=[
                column(rows, first),
                column(rows, first),
                column(rows, first + total),
                column(far_rows, first),
                column(far_rows, first + total),
                column(rows, first),
                column(rows, 0),
                pl.BlockSpec((1, 2, rows), lambda h, c: (h, 0, 0)),
            ],
            out_specs=[
                column(rows, 0),
                column(rows, 0),
                column(rows, 0),
                column(far_rows, 0),
                column(far_rows, 0),
            ],
            scratch_shapes=[
                pltpu.VMEM((128, rows), F32),
                pltpu.VMEM((rows, 128), F32),
                pltpu.VMEM((rows, 128), F32),
            ],
        ),
        out_shape=[
            jax.ShapeDtypeStruct((rows, width), BF16),
            jax.ShapeDtypeStruct((rows, width), F32),
            jax.ShapeDtypeStruct((rows, width), F32),
            jax.ShapeDtypeStruct((far_rows, width), BF16),
            jax.ShapeDtypeStruct((far_rows, width), BF16),
        ],
        compiler_params=pltpu.CompilerParams(vmem_limit_bytes=16 * MEGA),
        cost_estimate=pl.CostEstimate(
            flops=2 * rows * rows * width // 1, bytes_accessed=rows * width * 3 // 1, transcendentals=0
        ),
        name="attend_back",
    )(count, queries, near, near, remote, remote, out_grad, attended, lse)


def pairs_of(count, target):
    return [(index, target(index)) for index in range(count)]


def swap_cores(value, count):
    return lax.ppermute(value, "dp", pairs_of(count, lambda index: index ^ 1))


def swap_seq(value):
    return lax.ppermute(value, "seq", [(0, 1), (1, 0)])


def exchange_rows(value, dp=16):
    pairs = []
    for index in range(0, dp, 2):
        left, right = (index + 1) * 2, index * 2 + 1
        pairs += [(left, right), (right, left)]
    return lax.ppermute(value, ("dp", "seq"), pairs)


def regroup(value, dp, moves):
    return jnp.where(moves, exchange_rows(value, dp), value)


def turn_rows(value, back):
    pairs = []
    for first in range(0, 32, 4):
        steps = [(0, 2), (2, 3), (3, 1), (1, 0)]
        pairs += [(first + b, first + a) if back else (first + a, first + b) for a, b in steps]
    return lax.ppermute(value, ("dp", "seq"), pairs)


def deal(value, turn, cross, core, moves):
    size = value.shape[0] // 2
    first, second = value[:size], value[size:]
    base = jnp.where(moves, cross(first), first)
    came = turn(second)
    lead = core == 0
    return jnp.concatenate([jnp.where(lead, base, came), jnp.where(lead, came, base)], axis=0)


def undeal(value, turn, cross, core, moves):
    size = value.shape[0] // 2
    low, high = value[:size], value[size:]
    lead = core == 0
    base = jnp.where(lead, low, high)
    came = turn(jnp.where(lead, high, low))
    return jnp.concatenate([jnp.where(moves, cross(base), base), came], axis=0)


def split_columns(value, width):
    return [value[:, at : at + width] for at in range(0, value.shape[1], width)]


def gather_pack(blocks, dp):
    sizes = [block.shape[0] for block in blocks]
    packed = lax.all_gather(jnp.concatenate(blocks, axis=0), "dp", axis=0)
    if dp == GROUPS:
        return packed
    parts, at = [], 0
    for size in sizes:
        part = packed[:, at : at + size]
        parts.append(part.reshape(GROUPS, -1, part.shape[2]))
        at += size
    return jnp.concatenate(parts, axis=1)


def scatter_pack(packed, sizes, dp):
    if dp != GROUPS:
        parts, at = [], 0
        for size in sizes:
            whole = size * dp // GROUPS
            part = packed[:, at : at + whole]
            parts.append(part.reshape(dp, size, part.shape[2]))
            at += whole
        packed = jnp.concatenate(parts, axis=1)
    return lax.psum_scatter(packed, "dp", scatter_dimension=0)


def sum_seq(value, sequence_parts):
    if sequence_parts == 2:
        return value.astype(F32) + swap_seq(value).astype(F32)
    return lax.psum(value, "seq").astype(F32)


def place(grad, master, slot):
    marker = (jnp.arange(master.shape[0]) == slot).astype(F32)
    return marker.reshape((-1,) + (1,) * grad.ndim) * grad[None]


def spot(place):
    index = place[0]
    return index >> 2, (index >> 1) & 1, index & 1, place[1]


def whole(shape):
    return pl.BlockSpec(shape, lambda *unused: (0,) * len(shape))


ANYWHERE = pl.BlockSpec(memory_space=pl.ANY)


def kernel_call(body, scalars, in_specs, args, out_specs, out_shape, scratch, name, flops, moved):
    return pl.pallas_call(
        body,
        grid_spec=pltpu.PrefetchScalarGridSpec(
            num_scalar_prefetch=len(scalars),
            grid=(1,),
            in_specs=in_specs,
            out_specs=out_specs,
            scratch_shapes=scratch,
        ),
        out_shape=out_shape,
        compiler_params=pltpu.CompilerParams(vmem_limit_bytes=VMEM[name] * MEGA),
        cost_estimate=pl.CostEstimate(flops=flops // 2, bytes_accessed=moved // 2, transcendentals=0),
        name=name,
    )(*scalars, *args)


def pack_kernel(slots, place, *refs):
    masters, (head, tail, lines) = refs[:12], refs[12:]
    part, width = masters[4].shape
    lines[...] = jnp.zeros_like(lines)
    for row, number in enumerate(SMALL):
        master = masters[number]
        lines[row : row + 1, 0 : master.shape[1]] = master[pl.ds(slots[number], 1), :]
    for at in range(3):
        head[at * part : (at + 1) * part, :] = masters[2][:, at * width : (at + 1) * width].astype(BF16)
    head[3 * part : 4 * part, :] = masters[4][...].astype(BF16)
    head[4 * part :, :] = lines[...].astype(BF16)

    @pl.when(place[1] == 0)
    def shrink():
        tail[...] = masters[10][...].astype(BF16)

    @pl.when(place[1] != 0)
    def expand():
        for at in range(masters[8].shape[1] // width):
            tail[at * part : (at + 1) * part, :] = masters[8][:, at * width : (at + 1) * width].astype(BF16)


def pack(slots, place, masters):
    specs = []
    for number, master in enumerate(masters):
        if master.ndim == 2:
            specs.append(whole(master.shape))
        else:
            specs.append(
                pl.BlockSpec(
                    (None,) + master.shape[1:],
                    functools.partial(lambda step, slots, place, number: (slots[number], 0, 0), number=number),
                )
            )
    part, width = masters[4].shape[1:]
    rows = 4 * part + 16
    tail_rows = masters[10].shape[1]
    return kernel_call(
        pack_kernel, (slots, place), specs, masters,
        [whole((rows, width)), whole((tail_rows, width))],
        [jax.ShapeDtypeStruct((rows, width), BF16), jax.ShapeDtypeStruct((tail_rows, width), BF16)],
        [pltpu.VMEM((16, width), F32)], "pack", 0, 4 * rows * width * 6,
    )


def shift_z(value):
    return lax.ppermute(value, "dp", pairs_of(16, lambda index: (index + 4) % 16))


def swap_x(value):
    return lax.ppermute(value, "dp", pairs_of(16, lambda index: index ^ 2))


def after(value, *earlier):
    return lax.optimization_barrier((value,) + earlier)[0]


class Lane:
    def __init__(self, move, depth=2):
        self.move, self.depth, self.sent = move, depth, []

    def __call__(self, value, move=None):
        if len(self.sent) >= self.depth:
            value = after(value, self.sent[-self.depth])
        self.sent.append((move or self.move)(value))
        return self.sent[-1]


def ring_slots(z, x):
    slots = []
    for step in range(4):
        base = ((z - step) & 3) * 4
        slots += [base + x * 2, base + (1 - x) * 2]
    return slots


def gather(head, tail, values, out_grad, core, moves):
    z, x, y = Lane(shift_z, 2), Lane(swap_x, 1), Lane(swap_seq, 2)
    head, tail = [head], [tail]
    head_x, tail_x, tail_y, tail_xy = [], [], [], []
    head.append(z(head[0]))
    head_x.append(x(head[0]))
    tail_y.append(y(tail[0]))
    head.append(z(head[1]))
    tail_x.append(x(tail[0]))
    turn = lambda value: y(value, functools.partial(turn_rows, back=False))
    cross = lambda value: y(value, exchange_rows)
    values = deal(values, turn, cross, core, moves)
    tail.append(z(tail[0]))
    head_x.append(x(head[1]))
    out_grad = deal(out_grad, turn, cross, core, moves)
    head.append(z(head[2]))
    head_x.append(x(head[2]))
    tail_xy.append(y(tail_x[0]))
    tail.append(z(tail[1]))
    head_x.append(x(head[3]))
    tail_y.append(y(tail[1]))
    tail_x.append(x(tail[1]))
    values = after(values, tail_xy[0], tail[2], tail_x[1])
    tail.append(z(tail[2]))
    tail_xy.append(y(tail_x[1]))
    tail_x.append(x(tail[2]))
    tail_y.append(y(tail[2]))
    tail_x.append(x(tail[3]))
    mix = lambda first, second: [piece for pair in zip(first, second) for piece in pair]

    def rest(first, second):
        tail_xy.append(y(after(tail_x[2], first)))
        tail_y.append(y(after(tail[3], first)))
        tail_xy.append(y(after(tail_x[3], second)))
        return mix(tail_y, tail_xy), out_grad

    return mix(head, head_x), mix(tail, tail_x), values, rest


def row_sum(value):
    return jnp.sum(value, axis=0, keepdims=True)


def normalise(values):
    average = jnp.mean(values, axis=-1, keepdims=True)
    centered = values - average
    scale = lax.rsqrt(jnp.mean(centered * centered, axis=-1, keepdims=True) + EPSILON)
    return centered * scale, scale


def norm_back(grad, gain, shape, scale):
    inner = grad * gain
    first = jnp.mean(inner, axis=-1, keepdims=True)
    second = jnp.mean(inner * shape, axis=-1, keepdims=True)
    return scale * (inner - first - shape * second)


def balanced_kernel(extra, q_ref, k_ref, v_ref, rk_ref, rv_ref, o_ref, lse_ref, *, block):
    masks = pair_masks()
    index = extra[0]
    first = (index == 0).astype(F32)
    spot = pl.ds(pl.multiple_of(index * block, block), block)
    keys = jnp.concatenate([k_ref[0:block, :], rk_ref[0:block, :], k_ref[block:, :]], axis=0)
    values = jnp.concatenate([v_ref[0:block, :], rv_ref[0:block, :], v_ref[block:, :]], axis=0)
    sums, totals = [[], []], [[], []]
    for head in range(2):
        mask = (masks[head] * 0.125).astype(BF16)
        long = dot(keys, q_ref[block:, :] * mask, 1, 1)
        last = causal(long[2 * block :], block)
        long = long[: 2 * block]
        short = causal(dot(keys[0:block], q_ref[0:block, :] * mask, 1, 1), block)
        more = dot(rk_ref[spot, :], q_ref[spot, :] * mask, 1, 1)
        peak = lambda value: jnp.max(value, axis=0, keepdims=True)
        top_more = peak(more)
        top_short = peak(short)
        top_long = jnp.maximum(peak(long), peak(last))
        joined_short = jnp.maximum(top_short, top_more)
        joined_long = jnp.maximum(top_long, top_more)
        at_first = index == 0
        top_short = jnp.where(at_first, joined_short, top_short)
        top_long = jnp.where(at_first, top_long, joined_long)
        more = jnp.exp(more - jnp.where(at_first, top_short, top_long))
        short = jnp.exp(short - top_short)
        long = jnp.exp(long - top_long)
        last = jnp.exp(last - top_long)
        more_total = row_sum(more)
        more_sum = dot(rv_ref[spot, :], more.astype(BF16), 0, 0)
        short_total = row_sum(short) + first * more_total
        long_total = row_sum(long) + row_sum(last) + (1.0 - first) * more_total
        long_low = jnp.concatenate([long.astype(BF16), last.astype(BF16)], axis=0)
        half = slice(64 * head, 64 * head + 64)
        sums[0].append((dot(values[0:block], short.astype(BF16), 0, 0) + first * more_sum)[half] / short_total)
        sums[1].append((dot(values, long_low, 0, 0) + (1.0 - first) * more_sum)[half] / long_total)
        lse_ref[0, head : head + 1, 0:block] = top_short + jnp.log(short_total)
        lse_ref[0, head : head + 1, block:] = top_long + jnp.log(long_total)
    for part in range(2):
        joined = jnp.concatenate(sums[part], axis=0)
        o_ref[part * block : (part + 1) * block, :] = jnp.transpose(joined).astype(BF16)


def balanced_back_kernel(
    extra, q_ref, k_ref, v_ref, rk_ref, rv_ref, do_ref, o_ref, lse_ref,
    dq_ref, dk_ref, dv_ref, rdk_ref, rdv_ref, *, block,
):
    masks = pair_masks()
    index = extra[0]
    first = (index == 0).astype(F32)
    spot = pl.ds(pl.multiple_of(index * block, block), block)
    keys = jnp.concatenate([k_ref[0:block, :], rk_ref[0:block, :], k_ref[block:, :]], axis=0)
    values = jnp.concatenate([v_ref[0:block, :], rv_ref[0:block, :], v_ref[block:, :]], axis=0)
    product = jnp.transpose(do_ref[...].astype(F32) * o_ref[...].astype(F32))
    key_grads, value_grads, query_grads = [0.0] * 3, [0.0] * 3, [0.0] * 3
    for head in range(2):
        mask = masks[head].astype(BF16)
        scaled = (masks[head] * 0.125).astype(BF16)
        delta = row_sum(product[64 * head : 64 * head + 64])
        lse = lse_ref[0, head : head + 1, :]
        pick = lambda row: jnp.where(index == 0, row[:, :block], row[:, block:])
        sets = (
            (slice(block, None), keys, values, lse[:, block:], delta[:, block:], 3),
            (slice(0, block), keys[0:block], values[0:block], lse[:, :block], delta[:, :block], 1),
            (spot, rk_ref[spot, :], rv_ref[spot, :], pick(lse), pick(delta), 0),
        )
        for at, (rows, near_keys, near_values, norm, shift, blocks) in enumerate(sets):
            query = q_ref[rows, :] * scaled
            grad = do_ref[rows, :] * mask
            scores = dot(near_keys, query, 1, 1)
            if blocks:
                last = causal(scores[(blocks - 1) * block :], block)
                scores = jnp.concatenate([scores[: (blocks - 1) * block], last], axis=0) if blocks > 1 else last
            probs = jnp.exp(scores - norm)
            score_grad = (probs * (dot(near_values, grad, 1, 1) - shift)).astype(BF16)
            value_grads[at] += dot(probs.astype(BF16), grad, 1, 0)
            key_grads[at] += dot(score_grad, query, 1, 0)
            query_grads[at] += dot(near_keys * scaled, score_grad, 0, 0)
    turned = jnp.concatenate([query_grads[1] + first * query_grads[2], query_grads[0] + (1.0 - first) * query_grads[2]], axis=1)
    dq_ref[...] = jnp.transpose(turned).astype(BF16)
    for out, far, grads in ((dk_ref, rdk_ref, key_grads), (dv_ref, rdv_ref, value_grads)):
        out[0:block, :] = (grads[0][0:block] + grads[1]).astype(BF16)
        out[block:, :] = grads[0][2 * block :].astype(BF16)
        far[0:block, :] = (grads[0][block : 2 * block] + first * grads[2]).astype(BF16)
        far[block:, :] = ((1.0 - first) * grads[2]).astype(BF16)


def balanced(extra, args, first, pairs, cost):
    queries = args[0]
    rows, width = queries.shape
    total = width // 128
    column = lambda offset: pl.BlockSpec((rows, 128), lambda h, c: (0, h + offset))
    line = pl.BlockSpec((1, 2, rows), lambda h, c: (h, 0, 0))
    half = jax.ShapeDtypeStruct((rows, pairs * 128), BF16)
    in_specs = [column(first), column(first), column(first + total), column(first), column(first + total)]
    operands = [queries, args[1], args[1], args[2], args[2]]
    if len(args) == 3:
        body, out_specs = balanced_kernel, [column(0), line]
        out_shape = [half, jax.ShapeDtypeStruct((pairs, 2, rows), F32)]
    else:
        body, out_specs, out_shape = balanced_back_kernel, [column(0)] * 5, [half] * 5
        in_specs += [column(first), column(0), line]
        operands += list(args[3:])
    return pl.pallas_call(
        functools.partial(body, block=rows // 2),
        grid_spec=pltpu.PrefetchScalarGridSpec(
            num_scalar_prefetch=1, grid=(pairs,), in_specs=in_specs, out_specs=out_specs
        ),
        out_shape=out_shape,
        compiler_params=pltpu.CompilerParams(vmem_limit_bytes=16 * MEGA),
        cost_estimate=pl.CostEstimate(flops=cost, bytes_accessed=cost // 1000, transcendentals=0),
        name="attend" if len(args) == 3 else "attend_back",
    )(extra, *operands)


def qkv_kernel(place, x_ref, *refs):
    pieces, (packed, n1_ref, q_ref, kv_ref, v48, v96, v192, sems) = refs[:16], refs[16:]
    z, x, core, half = spot(place)
    slots = ring_slots(z, x)
    slots = [slot + core for slot in slots] + [slot + 1 - core for slot in slots]
    copies = [
        pltpu.make_async_copy(piece, packed.at[slots[number]], sems.at[number])
        for number, piece in enumerate(pieces)
    ]
    for copy in copies:
        copy.start()
    width = x_ref.shape[1]
    part = width // GROUPS
    shape, unused = normalise(x_ref[...].astype(F32))
    for copy in copies:
        copy.wait()
    for group in range(GROUPS):
        lines = packed[group, 4 * part : 4 * part + 16, :].astype(F32)[0:8]
        for out in (v48, v96, v192):
            size = out.shape[1] // GROUPS
            out[:, group * size : (group + 1) * size] = lines[:, :size]
    normed = (shape * v48[0:1, :] + v48[1:2, :]).astype(BF16)
    n1_ref[...] = normed
    for at in range(3):
        weight = packed[:, at * part : (at + 1) * part, :].reshape(width, width)
        result = dot(normed, weight, 1, 0)
        if at == 0:
            q_ref[...] = (result + v96[2:3, :width]).astype(BF16)
        elif at == 1:
            kv_ref[:, :width] = result.astype(BF16)
        else:
            kv_ref[:, width:] = (result + v96[2:3, width:]).astype(BF16)


def qkv(place, values, pieces):
    rows, width = values.shape
    shapes = [
        ((GROUPS,) + pieces[0].shape, BF16), ((rows, width), BF16), ((rows, width), BF16), ((rows, 2 * width), BF16),
        ((8, width), F32), ((8, 2 * width), F32), ((8, 4 * width), F32),
    ]
    return kernel_call(
        qkv_kernel, (place,), [whole(values.shape)] + [ANYWHERE] * 16, [values] + pieces,
        [whole(shape) for shape, unused in shapes],
        [jax.ShapeDtypeStruct(shape, dtype) for shape, dtype in shapes],
        [pltpu.SemaphoreType.DMA((16,))], "qkv", 6 * rows * width * width, 20 * width * width,
    )


def merge_kernel(x_ref, o1_ref, o2_ref, weight, v48, m_ref, n2_ref):
    width = x_ref.shape[1]
    attended = jnp.concatenate([o1_ref[...], o2_ref[...]], axis=1)
    middle = x_ref[...].astype(F32) + dot(attended, weight[...].reshape(width, width), 1, 0) + v48[3:4, :]
    m_ref[...] = middle
    shape, unused = normalise(middle)
    n2_ref[...] = (shape * v48[4:5, :] + v48[5:6, :]).astype(BF16)


def merge_spec(packed):
    part = packed.shape[2] // GROUPS
    return pl.BlockSpec((GROUPS, part, packed.shape[2]), lambda *unused: (0, 3, 0))


def merge(values, attended, packed, v48):
    rows, width = values.shape
    return kernel_call(
        merge_kernel, (),
        [whole(values.shape)] + [whole(piece.shape) for piece in attended] + [merge_spec(packed), whole(v48.shape)],
        [values] + attended + [packed, v48], [whole(values.shape)] * 2,
        [jax.ShapeDtypeStruct((rows, width), F32), jax.ShapeDtypeStruct((rows, width), BF16)],
        [], "merge", 2 * rows * width * width, 12 * rows * width,
    )


def gelu_pair(value):
    scale, cubic = math.sqrt(2 / math.pi), 0.044715
    square = value * value
    bent = jnp.tanh(scale * value * (1.0 + cubic * square))
    half = 0.5 * (1.0 + bent)
    slope = half + 0.5 * value * (1.0 - bent * bent) * (scale * (1.0 + 3.0 * cubic * square))
    return value * half, slope


def ffn_kernel(place, *refs):
    pieces, refs = refs[:32], refs[32:]
    m_ref, n2_ref, gy_ref, merge_weight, v48, v192, out_ref, dm_ref, dz_ref, do_ref, g48, g192 = refs[:12]
    outs, (weights, grads, y, dn2, n2_t, u, df, in_sems, out_sems) = refs[12:20], refs[20:]
    z, x, core, half = spot(place)
    slots = ring_slots(z, x)
    spots = [(slot + core, half) for slot in slots] + [(slot + core, 1 - half) for slot in slots]
    spots += [(slot + 1 - core, half) for slot in slots] + [(slot + 1 - core, 1 - half) for slot in slots]
    copies = [
        pltpu.make_async_copy(piece, weights.at[spots[number][0], spots[number][1]], in_sems.at[number])
        for number, piece in enumerate(pieces)
    ]
    for copy in copies:
        copy.start()
    width = m_ref.shape[1]
    part = width // GROUPS
    n2_t[...] = jnp.transpose(n2_ref[...])
    y[...] = jnp.zeros_like(y)
    dn2[...] = jnp.zeros_like(dn2)
    for copy in copies:
        copy.wait()

    def step(at, unused):
        first = pl.multiple_of(at * 4, 4)
        lines = pl.ds(pl.multiple_of(at * part, 16), part)
        chunk = 256
        for column in range(0, width, chunk):
            place_in = pl.ds(pl.multiple_of(at * width + column, 128), chunk)
            expand = weights[:, 1, lines, column : column + chunk].reshape(width, chunk)
            hidden = dot(n2_ref[...], expand, 1, 0) + v192[6:7, place_in]
            shrink = weights[pl.ds(first, 4), 0].reshape(width, width)[column : column + chunk]
            active, slope = gelu_pair(hidden)
            u[:, column : column + chunk] = active.astype(BF16)
            hidden_grad = (dot(gy_ref[...], shrink, 1, 1) * slope).astype(BF16)
            df[:, column : column + chunk] = hidden_grad
            g192[0:1, place_in] = row_sum(hidden_grad.astype(F32))
        shrink = weights[pl.ds(first, 4), 0].reshape(width, width)
        expand = weights[:, 1, lines, :].reshape(width, width)
        y[...] += dot(u[...], shrink, 1, 0)
        dn2[...] += dot(df[...], expand, 1, 1)
        grads[pl.ds(first, 4), 0] = dot(u[...], gy_ref[...], 0, 0).astype(BF16).reshape(4, 4 * part, width)
        grads[:, 1, lines, :] = dot(n2_t[...], df[...], 1, 0).astype(BF16).reshape(GROUPS, part, width)
        return unused

    lax.fori_loop(0, 4, step, 0)
    copies = []
    for order in range(4):
        base = ((z - order) & 3) * 4
        for number, out in ((0, outs[2 * order]), (1, outs[2 * order + 1])):
            side = core if number == 0 else 1 - core
            for kind in range(2):
                for column in range(2):
                    source = base + (x if column == 0 else 1 - x) * 2 + side
                    copies.append(
                        pltpu.make_async_copy(
                            grads.at[source, half if kind == 0 else 1 - half],
                            out.at[column, kind],
                            out_sems.at[len(copies)],
                        )
                    )
    for copy in copies:
        copy.start()
    middle = m_ref[...]
    out_ref[...] = (middle + y[...] + v48[7:8, :]).astype(BF16)
    shape, scale = normalise(middle)
    second_grad = dn2[...]
    out_grad = gy_ref[...].astype(F32)
    middle_grad = out_grad + norm_back(second_grad, v48[4:5, :], shape, scale)
    dm_ref[...] = middle_grad
    low = middle_grad.astype(BF16)
    dz_ref[...] = low
    g48[...] = jnp.zeros_like(g48)
    g48[3:4, :] = row_sum(low.astype(F32))
    g48[4:5, :] = row_sum(shape * second_grad)
    g48[5:6, :] = row_sum(second_grad)
    g48[7:8, :] = row_sum(out_grad)
    do_ref[...] = dot(low, merge_weight[...].reshape(width, width), 1, 1).astype(BF16)
    for copy in copies:
        copy.wait()


def ffn(place, pieces, middle, second, out_grad, packed, v48, v192):
    rows, width = middle.shape
    ff = 4 * width
    tail_rows = pieces[0].shape[0]
    shapes = [
        ((rows, width), BF16), ((rows, width), F32), ((rows, width), BF16), ((rows, width), BF16),
        ((8, width), F32), ((8, ff), F32),
    ]
    part = jax.ShapeDtypeStruct((2, 2, tail_rows, width), BF16)
    pack_shape = (GROUPS, 2, tail_rows, width)
    results = kernel_call(
        ffn_kernel, (place,),
        [ANYWHERE] * 32
        + [whole(middle.shape), whole(second.shape), whole(out_grad.shape), merge_spec(packed), whole(v48.shape), whole(v192.shape)],
        pieces + [middle, second, out_grad, packed, v48, v192],
        [whole(shape) for shape, unused in shapes] + [ANYWHERE] * 8,
        [jax.ShapeDtypeStruct(shape, dtype) for shape, dtype in shapes] + [part] * 8,
        [
            pltpu.VMEM(pack_shape, BF16), pltpu.VMEM(pack_shape, BF16),
            pltpu.VMEM((rows, width), F32), pltpu.VMEM((rows, width), F32), pltpu.VMEM((width, rows), BF16),
            pltpu.VMEM((rows, width), BF16), pltpu.VMEM((rows, width), BF16),
            pltpu.SemaphoreType.DMA((32,)), pltpu.SemaphoreType.DMA((32,)),
        ],
        "ffn", 12 * rows * width * ff, 8 * width * ff,
    )
    return results[:6], results[6:]


def close_kernel(
    place, n1_ref, x_ref, q1, k1, v1, far_k1, far_v1, q2, k2, v2, far_k2, far_v2, o1, o2,
    dz_ref, dm_ref, packed, v48, g48_in, g192, *refs,
):
    join = lambda first, second: jnp.concatenate([first[...], second[...]], axis=1)
    grad_ref, outs, (grads, g48, g96, dt, sems) = refs[0], refs[1:9], refs[9:]
    z, x, core, half = spot(place)
    width = x_ref.shape[1]
    part = width // GROUPS
    normed_t = jnp.transpose(n1_ref[...])
    normed_grad = None
    for at in range(3):
        if at == 0:
            dt[...] = join(q1, q2)
        elif at == 1:
            dt[...] = (join(k1, k2).astype(F32) + join(far_k1, far_k2).astype(F32)).astype(BF16)
        else:
            dt[...] = (join(v1, v2).astype(F32) + join(far_v1, far_v2).astype(F32)).astype(BF16)
        if at != 1:
            g96[2:3, (at // 2) * width : (at // 2 + 1) * width] = row_sum(dt[...].astype(F32))
        weight = packed[:, at * part : (at + 1) * part, :].reshape(width, width)
        term = dot(dt[...], weight, 1, 1)
        normed_grad = term if normed_grad is None else normed_grad + term
        grads[:, at * part : (at + 1) * part, :] = dot(normed_t, dt[...], 1, 0).astype(BF16).reshape(GROUPS, part, width)
    grads[:, 3 * part : 4 * part, :] = dot(join(o1, o2), dz_ref[...], 0, 0).astype(BF16).reshape(GROUPS, part, width)
    shape, scale = normalise(x_ref[...].astype(F32))
    g48[...] = g48_in[...]
    g48[0:1, :] = row_sum(shape * normed_grad)
    g48[1:2, :] = row_sum(normed_grad)
    row = lax.broadcasted_iota(jnp.int32, (16, 1), 0)
    for group in range(GROUPS):
        lines = jnp.concatenate([g48[:, group * part : (group + 1) * part], jnp.zeros((8, part), F32)], axis=0)
        grads[group, 4 * part :, :] = jnp.zeros((16, width), BF16)
        pair = g96[2:3, group * 2 * part : (group + 1) * 2 * part]
        wide = g192[0:1, group * 4 * part : (group + 1) * 4 * part]
        spread = jnp.where(row == 6, wide, 0.0)
        left = jnp.where(row == 2, pair, 0.0)
        grads[group, 4 * part :, 0 : 4 * part] = spread.astype(BF16)
        grads[group, 4 * part :, 0 : 2 * part] = (spread[:, : 2 * part] + left).astype(BF16)
        keep = jnp.where((row == 2) | (row == 6), 0.0, lines) + spread[:, :part] + left[:, :part]
        grads[group, 4 * part :, 0:part] = keep.astype(BF16)
    copies = []
    for order in range(4):
        base = ((z - order) & 3) * 4
        for number, out in ((0, outs[2 * order]), (1, outs[2 * order + 1])):
            side = core if number == 0 else 1 - core
            for column in range(2):
                source = base + (x if column == 0 else 1 - x) * 2 + side
                copies.append(pltpu.make_async_copy(grads.at[source], out.at[column], sems.at[len(copies)]))
    for copy in copies:
        copy.start()
    grad_ref[...] = (dm_ref[...] + norm_back(normed_grad, v48[0:1, :], shape, scale)).astype(BF16)
    for copy in copies:
        copy.wait()


def close(place, args):
    rows, width = args[0].shape
    packed = args[16]
    head_rows = packed.shape[1]
    part = jax.ShapeDtypeStruct((2, head_rows, width), BF16)
    results = kernel_call(
        close_kernel, (place,), [whole(arg.shape) for arg in args], args,
        [whole((rows, width))] + [ANYWHERE] * 8,
        [jax.ShapeDtypeStruct((rows, width), BF16)] + [part] * 8,
        [
            pltpu.VMEM(packed.shape, BF16), pltpu.VMEM((8, width), F32), pltpu.VMEM((8, 2 * width), F32),
            pltpu.VMEM((rows, width), BF16), pltpu.SemaphoreType.DMA((16,)),
        ],
        "close", 14 * rows * width * width, 20 * width * width,
    )
    return results[0], results[1:]


def unpack_kernel(slots, place, head, head_far, tail, tail_far, *outs):
    part, width = outs[4].shape[1:]
    total = head[...].astype(F32) + head_far[...].astype(F32)
    own = tail[0].astype(F32) + tail_far[1].astype(F32)
    other = tail[1].astype(F32) + tail_far[0].astype(F32)
    lead = place[1] == 0
    shrink, expand = jnp.where(lead, own, other), jnp.where(lead, other, own)
    for row, number in enumerate(SMALL):
        out = outs[number]
        size = out.shape[1]
        line = total[4 * part + row : 4 * part + row + 1, :size]
        row_at = lax.broadcasted_iota(jnp.int32, out.shape, 0)
        out[...] = jnp.where(row_at == slots[number], line, 0.0)
    for slot in range(outs[2].shape[0]):
        chosen = lambda number, value: jnp.where(slots[number] == slot, value, 0.0)
        for at in range(3):
            outs[2][slot, :, at * width : (at + 1) * width] = chosen(2, total[at * part : (at + 1) * part])
        outs[4][slot] = chosen(4, total[3 * part : 4 * part])
        for at in range(outs[8].shape[2] // width):
            outs[8][slot, :, at * width : (at + 1) * width] = chosen(8, expand[at * part : (at + 1) * part])
        outs[10][slot] = chosen(10, shrink)


def unpack(slots, place, parts, masters):
    return kernel_call(
        unpack_kernel, (slots, place), [whole(part.shape) for part in parts], parts,
        [whole(master.shape) for master in masters],
        [jax.ShapeDtypeStruct(master.shape, F32) for master in masters],
        [], "unpack", 0, 8 * 1024 * 1024,
    )


def per_device_fast(inputs, cotangent, tie_slots, *masters):
    length, count, width = inputs.shape
    index, half = lax.axis_index("dp"), lax.axis_index("seq")
    place = jnp.stack([index, half]).astype(jnp.int32)
    core = index % 2
    moves = core != half
    head, tail = pack(tie_slots, place, masters)
    head_pieces, tail_pieces, values, rest = gather(
        head, tail, inputs.reshape(length, width), cotangent.reshape(length, width), core, moves
    )
    head_pieces = head_pieces + [swap_cores(piece, 16) for piece in head_pieces]
    packed, normed, queries, near, v48, v96, v192 = qkv(place, values, head_pieces)
    remote = swap_cores(near, 16)
    extra = (1 - core).astype(jnp.int32).reshape(1)
    half_pairs = width // 256
    queries = after(queries, tail_pieces[6], tail_pieces[3])
    attended, lse = [None, None], [None, None]
    attended[0], lse[0] = balanced(extra, (queries, near, remote), 0, half_pairs, 1000000)
    queries = after(queries, attended[0])
    attended[1], lse[1] = balanced(extra, (queries, near, remote), half_pairs, half_pairs, 1000000)
    tail_other, out_grad = rest(attended[0], attended[1])
    middle, second = merge(values, attended, packed, v48)
    late = lambda pieces, first: [
        swap_cores(after(piece, attended[1]) if number >= first else piece, 16) for number, piece in enumerate(pieces)
    ]
    tail_pieces = tail_pieces + late(tail_pieces, 4)
    tail_other = tail_other + late(tail_other, 5)
    (output, middle_grad, branch_grad, attended_grad, g48, g192), tail_parts = ffn(
        place, tail_pieces[:8] + tail_other[:8] + tail_pieces[8:] + tail_other[8:],
        middle, second, out_grad, packed, v48, v192,
    )
    z, x, y = Lane(shift_z, 2), Lane(swap_x, 3), Lane(swap_seq, 2)
    turn = lambda value: y(value, functools.partial(turn_rows, back=True))
    cross = lambda value: y(value, exchange_rows)
    came = [swap_cores(send, 16) for send in tail_parts[1::2]]
    kept = [keep + other for keep, other in zip(tail_parts[0::2], came)]
    tail_half, tail_part, head_part = {}, {}, {}
    attended_grad = after(attended_grad, *kept)
    tail_half[1] = kept[1][1, 0] + y(kept[1][1, 1])
    tail_half[2] = kept[2][1, 0] + y(kept[2][1, 1])
    tail_half[3] = kept[3][1, 0] + y(kept[3][1, 1])
    tail_half[0] = kept[0][1, 0] + y(kept[0][1, 1])
    output = undeal(output, turn, cross, core, moves)
    grads = []
    for part in range(2):
        if part:
            attended_grad = after(attended_grad, grads[0], tail_half[1])
        query_grad, key_grad, value_grad, far_key, far_value = balanced(
            extra, (queries, near, remote, attended_grad, attended[part], lse[part]), part * half_pairs, half_pairs, 1000000
        )
        grads += [query_grad, key_grad, value_grad, swap_cores(far_key, 16), swap_cores(far_value, 16)]
    tail_part[1] = jnp.stack([kept[1][0, 0] + x(tail_half[1]), kept[1][0, 1]])
    tail_run = z(tail_part[1])
    tail_part[2] = jnp.stack([kept[2][0, 0] + x(tail_half[2]), kept[2][0, 1]])
    tail_run = z(tail_part[2] + tail_run)
    tail_part[3] = jnp.stack([kept[3][0, 0] + x(tail_half[3]), kept[3][0, 1]])
    tail_run = z(tail_part[3] + tail_run)
    middle_grad = after(middle_grad, tail_half[3])
    input_grad, head_parts = close(
        place,
        [
            normed, values, *grads, *attended, branch_grad, middle_grad, packed, v48, g48, g192,
        ],
    )
    came = [swap_cores(send, 16) for send in head_parts[1::2]]
    head_kept = [keep + other for keep, other in zip(head_parts[0::2], came)]
    input_grad = undeal(input_grad, turn, cross, core, moves)
    head_part[1] = head_kept[1][0] + x(head_kept[1][1])
    head_run = z(head_part[1])
    tail_part[0] = jnp.stack([kept[0][0, 0] + x(tail_half[0]), kept[0][0, 1]])
    tail_sum = tail_part[0] + tail_run
    head_part[2] = head_kept[2][0] + x(head_kept[2][1])
    head_run = z(head_part[2] + head_run)
    head_part[3] = head_kept[3][0] + x(head_kept[3][1])
    head_run = z(head_part[3] + head_run)
    head_part[0] = head_kept[0][0] + x(head_kept[0][1])
    head_sum = head_part[0] + head_run
    input_grad = input_grad.astype(F32)
    grads = unpack(
        tie_slots, place, [head_sum, y(head_sum), tail_sum, y(tail_sum)], masters
    )
    shape = (length, count, width)
    return (output.reshape(shape), input_grad.reshape(shape)) + tuple(grads)


def per_device(
    inputs,
    cotangent,
    tie_slots,
    *masters,
):
    dp, sequence_parts = lax.axis_size("dp"), lax.axis_size("seq")
    length, count, width = inputs.shape
    rows = length * count
    block = math.gcd(length, 256)
    moved = sequence_parts == 2 and dp % 2 == 0
    core = lax.axis_index("dp") % 2
    moves = core != lax.axis_index("seq")
    place_index = core if moved else lax.axis_index("seq")
    chosen = [
        lax.dynamic_index_in_dim(masters[number], tie_slots[number], 0, keepdims=False).astype(BF16)
        for number in range(12)
    ]
    part = width // dp
    ff = masters[10].shape[1] * dp
    small = jnp.concatenate([chosen[number] for number in SMALL])
    widths = [chosen[number].shape[0] for number in SMALL]
    pad = 16 * GROUPS // dp
    small = jnp.pad(small.reshape(1, -1), ((0, pad - 1), (0, width - small.shape[0])))
    head_blocks = split_columns(chosen[2], width) + [chosen[4], small]
    tail_blocks = [chosen[10]] + split_columns(chosen[8], width)
    head_sizes = [piece.shape[0] for piece in head_blocks]
    tail_sizes = [piece.shape[0] for piece in tail_blocks]
    head_pack = gather_pack(head_blocks, dp)
    flat_in = inputs.reshape(rows, width)
    flat_cot = cotangent.reshape(rows, width)
    if moved:
        flat_in = regroup(flat_in, dp, moves)
        flat_cot = regroup(flat_cot, dp, moves)
    tail_pack = gather_pack(tail_blocks, dp)

    group_rows = width // GROUPS
    matrix = lambda pack, at: pack[:, at * group_rows : (at + 1) * group_rows].reshape(width, width)
    triple_weight = jnp.concatenate([matrix(head_pack, at) for at in range(3)], axis=1)
    merge_weight = matrix(head_pack, 3)
    per_group = GROUPS // dp if dp < GROUPS else dp // GROUPS
    lines = head_pack[:, 4 * group_rows :].reshape(dp, pad, width)[:, 0]
    vectors, at = [], 0
    for size in widths:
        vectors.append(lines[:, at : at + size].reshape(-1).astype(F32))
        at += size
    gain_one, shift_one, pair_bias, merge_bias, gain_two, shift_two, expand_bias, shrink_bias = vectors

    flat_in = flat_in.astype(F32)
    normed, norm_one_pull = jax.vjp(layer_norm, flat_in, gain_one, shift_one)
    normed_low = normed.astype(BF16)
    bias_full = jnp.concatenate([pair_bias[:width], jnp.zeros((width,), F32), pair_bias[width:]])
    triple = (jnp.dot(normed_low, triple_weight, preferred_element_type=F32) + bias_full).astype(BF16)
    queries, near = triple[:, :width], triple[:, width:]
    if moved:
        remote = swap_cores(near, dp)
    else:
        remote = lax.all_gather(near, "seq", axis=0, tiled=True)
    far_count = place_index.astype(jnp.int32).reshape(1)
    attended_low, lse = attend(far_count, queries, near, remote, block)
    middle = flat_in + jnp.dot(attended_low, merge_weight, preferred_element_type=F32) + merge_bias

    ff_rows = ff // GROUPS
    shrink_weight = tail_pack[:, :ff_rows].reshape(ff, width)
    expand_weight = jnp.concatenate(
        [
            tail_pack[:, ff_rows + at * group_rows : ff_rows + (at + 1) * group_rows].reshape(width, width)
            for at in range(ff // width)
        ],
        axis=1,
    )
    second, norm_two_pull = jax.vjp(layer_norm, middle, gain_two, shift_two)
    second_low = second.astype(BF16)
    hidden = jnp.dot(second_low, expand_weight, preferred_element_type=F32) + expand_bias
    active, gelu_pull = jax.vjp(lambda values: jax.nn.gelu(values, approximate=True), hidden)
    active_low = active.astype(BF16)
    result = middle + jnp.dot(active_low, shrink_weight, preferred_element_type=F32) + shrink_bias
    output = result.astype(BF16)
    if moved:
        output = regroup(output, dp, moves)
    grad_shrink_weight = dot(active_low, flat_cot, 0, 0)
    grad_shrink_bias = jnp.sum(flat_cot.astype(F32), axis=0)
    active_grad = dot(flat_cot, shrink_weight, 1, 1)
    hidden_grad = gelu_pull(active_grad)[0].astype(BF16)
    grad_expand_weight = dot(second_low, hidden_grad, 0, 0)
    grad_expand_bias = jnp.sum(hidden_grad.astype(F32), axis=0)
    second_grad = dot(hidden_grad, expand_weight, 1, 1)
    middle_part, grad_gain_two, grad_shift_two = norm_two_pull(second_grad)
    middle_grad = flat_cot.astype(F32) + middle_part
    grouped = lambda value: value.astype(BF16).reshape(GROUPS, -1, width)
    tail_grads = jnp.concatenate(
        [grouped(grad_shrink_weight)] + [grouped(piece) for piece in split_columns(grad_expand_weight, width)],
        axis=1,
    )
    tail_own = sum_seq(scatter_pack(tail_grads, tail_sizes, dp), sequence_parts)

    branch_grad = middle_grad.astype(BF16)
    grad_merge_weight = dot(attended_low, branch_grad, 0, 0)
    grad_merge_bias = jnp.sum(branch_grad.astype(F32), axis=0)
    attended_grad = dot(branch_grad, merge_weight, 1, 1).astype(BF16)
    query_grad, key_grad, value_grad, far_key, far_value = attend_back(
        far_count, queries, near, remote, attended_grad, attended_low, lse, block
    )
    far_grad = jnp.concatenate([far_key, far_value], axis=1)
    pair_grad = jnp.concatenate([key_grad, value_grad], axis=1)
    if moved:
        pair_grad = pair_grad + swap_cores(far_grad, dp).astype(F32)
    else:
        pair_grad = pair_grad + lax.psum_scatter(far_grad, "seq", scatter_dimension=0, tiled=True).astype(F32)
    triple_grad = jnp.concatenate([query_grad, pair_grad.astype(BF16)], axis=1)
    grad_triple_weight = dot(normed_low, triple_grad, 0, 0)
    column_sums = jnp.sum(triple_grad.astype(F32), axis=0)
    grad_pair_bias = jnp.concatenate([column_sums[:width], column_sums[2 * width :]])
    normed_grad = dot(triple_grad, triple_weight, 1, 1)
    input_part, grad_gain_one, grad_shift_one = norm_one_pull(normed_grad)
    input_grad = middle_grad + input_part
    if moved:
        input_grad = regroup(input_grad, dp, moves)
    small_grads = [
        grad_gain_one, grad_shift_one, grad_pair_bias, grad_merge_bias,
        grad_gain_two, grad_shift_two, grad_expand_bias, grad_shrink_bias,
    ]
    lines = jnp.concatenate([piece.reshape(dp, -1) for piece in small_grads], axis=1).astype(BF16)
    lines = jnp.pad(lines[:, None], ((0, 0), (0, pad - 1), (0, width - lines.shape[1])))
    head_grads = jnp.concatenate(
        [grouped(piece) for piece in split_columns(grad_triple_weight, width)]
        + [grouped(grad_merge_weight), lines.reshape(GROUPS, -1, width)],
        axis=1,
    )
    head_own = sum_seq(scatter_pack(head_grads, head_sizes, dp), sequence_parts)

    piece_rows = chosen[4].shape[0]
    cut = lambda pack, at, size: pack[at : at + size]
    own_triple = jnp.concatenate([cut(head_own, at * piece_rows, piece_rows) for at in range(3)], axis=1)
    own_merge = cut(head_own, 3 * piece_rows, piece_rows)
    own_small, at = [], 0
    for size in widths:
        own_small.append(head_own[4 * piece_rows, at : at + size])
        at += size
    shrink_rows = chosen[10].shape[0]
    own_shrink = tail_own[:shrink_rows]
    own_expand = jnp.concatenate(
        [cut(tail_own, shrink_rows + at * piece_rows, piece_rows) for at in range(ff // width)], axis=1
    )
    own = [
        own_small[0], own_small[1], own_triple, own_small[2], own_merge, own_small[3],
        own_small[4], own_small[5], own_expand, own_small[6], own_shrink, own_small[7],
    ]
    shape = (length, count, width)
    return (output.reshape(shape), input_grad.reshape(shape)) + tuple(
        place(grad, master, tie_slots[number]) for number, (grad, master) in enumerate(zip(own, masters))
    )


def solution(mesh):
    in_specs = (
        P("seq", "dp", None),
        P("seq", "dp", None),
        P(),
        P(None, "dp"),
        P(None, "dp"),
        P(None, "dp", None),
        P(None, "dp"),
        P(None, "dp", None),
        P(None, "dp"),
        P(None, "dp"),
        P(None, "dp"),
        P(None, "dp", None),
        P(None, "dp"),
        P(None, "dp", None),
        P(None, "dp"),
    )
    out_specs = (
        P("seq", "dp", None),
        P("seq", "dp", None),
        P(None, "dp"),
        P(None, "dp"),
        P(None, "dp", None),
        P(None, "dp"),
        P(None, "dp", None),
        P(None, "dp"),
        P(None, "dp"),
        P(None, "dp"),
        P(None, "dp", None),
        P(None, "dp"),
        P(None, "dp", None),
        P(None, "dp"),
    )
    sizes = dict(mesh.shape)
    body = per_device_fast if (sizes["dp"], sizes["seq"]) == (16, 2) else per_device
    return jax.shard_map(
        body, mesh=mesh, in_specs=in_specs, out_specs=out_specs, check_vma=False
    )
```

```python
import functools
import math

import jax
import jax.numpy as jnp
from jax import lax
from jax.experimental import pallas as pl
from jax.experimental.pallas import tpu as pltpu
from jax.sharding import PartitionSpec as P

H = 12
GROUPS = 16
SMALL = (0, 1, 3, 5, 6, 7, 9, 11)
EPSILON = 1e-05
NEGATIVE = -1e30
F32 = jnp.float32
BF16 = jnp.bfloat16
MEGA = 1024 * 1024
VMEM = {"pack": 60, "qkv": 28, "merge": 14, "ffn": 40, "close": 26, "unpack": 36}


def layer_norm(values, gain, shift):
    average = jnp.mean(values, axis=-1, keepdims=True)
    centered = values - average
    variance = jnp.mean(centered * centered, axis=-1, keepdims=True)
    return centered * lax.rsqrt(variance + EPSILON) * gain + shift


def dot(left, right, left_dim, right_dim):
    return lax.dot_general(
        left, right, (((left_dim,), (right_dim,)), ((), ())), preferred_element_type=F32
    )


def pair_masks():
    lane = lax.broadcasted_iota(jnp.int32, (1, 128), 1)
    low = (lane < 64).astype(F32)
    return low, 1.0 - low


def causal(scores, block):
    key = lax.broadcasted_iota(jnp.int32, (block, block), 0)
    query = lax.broadcasted_iota(jnp.int32, (block, block), 1)
    return jnp.where(key <= query, scores, NEGATIVE)


def attend_kernel(count, q_ref, k_ref, v_ref, rk_ref, rv_ref, o_ref, lse_ref, *, block):
    rows = q_ref.shape[0]
    masks = pair_masks()
    for index in range(rows // block):
        here = slice(index * block, (index + 1) * block)
        size = (index + 1) * block
        state = []
        parts = []
        for head in range(2):
            query = q_ref[here, :] * (masks[head] * 0.125).astype(BF16)
            parts.append(query)
            scores = dot(k_ref[0:size, :], query, 1, 1)
            last = causal(scores[size - block :], block)
            top = jnp.max(last, axis=0, keepdims=True)
            if index:
                scores = jnp.concatenate([scores[: size - block], last], axis=0)
                top = jnp.max(scores, axis=0, keepdims=True)
            else:
                scores = last
            lifted = jnp.exp(scores - top)
            total = jnp.sum(lifted, axis=0, keepdims=True)
            state += [top, total, dot(v_ref[0:size, :], lifted.astype(BF16), 0, 0)]

        def far(step, state):
            start = pl.multiple_of(step * rows, rows)
            keys = rk_ref[pl.ds(start, rows), :]
            values = rv_ref[pl.ds(start, rows), :]
            result = []
            for head in range(2):
                top, total, gathered = state[3 * head : 3 * head + 3]
                scores = dot(keys, parts[head], 1, 1)
                new_top = jnp.maximum(top, jnp.max(scores, axis=0, keepdims=True))
                factor = jnp.exp(top - new_top)
                lifted = jnp.exp(scores - new_top)
                total = total * factor + jnp.sum(lifted, axis=0, keepdims=True)
                gathered = gathered * factor + dot(values, lifted.astype(BF16), 0, 0)
                result += [new_top, total, gathered]
            return tuple(result)

        top0, total0, sum0, top1, total1, sum1 = lax.fori_loop(0, count[0], far, tuple(state))
        joined = jnp.concatenate([sum0[:64] / total0, sum1[64:] / total1], axis=0)
        o_ref[here, :] = jnp.transpose(joined).astype(BF16)
        lse_ref[0, 0:1, here] = top0 + jnp.log(total0)
        lse_ref[0, 1:2, here] = top1 + jnp.log(total1)


def attend(count, queries, near, remote, block, first=0, pairs=None):
    rows, width = queries.shape
    total = width // 128
    pairs = pairs or total
    far_rows = remote.shape[0]
    column = lambda size, offset: pl.BlockSpec((size, 128), lambda h, c: (0, h + offset))
    return pl.pallas_call(
        functools.partial(attend_kernel, block=block),
        grid_spec=pltpu.PrefetchScalarGridSpec(
            num_scalar_prefetch=1,
            grid=(pairs,),
            in_specs=[
                column(rows, first),
                column(rows, first),
                column(rows, first + total),
                column(far_rows, first),
                column(far_rows, first + total),
            ],
            out_specs=[column(rows, 0), pl.BlockSpec((1, 2, rows), lambda h, c: (h, 0, 0))],
        ),
        out_shape=[
            jax.ShapeDtypeStruct((rows, pairs * 128), BF16),
            jax.ShapeDtypeStruct((pairs, 2, rows), F32),
        ],
        compiler_params=pltpu.CompilerParams(vmem_limit_bytes=16 * MEGA),
        cost_estimate=pl.CostEstimate(
            flops=rows * rows * pairs * 100 // 1, bytes_accessed=rows * pairs * 150 // 1, transcendentals=0
        ),
        name="attend",
    )(count, queries, near, near, remote, remote)


def attend_back_kernel(
    count, q_ref, k_ref, v_ref, rk_ref, rv_ref, do_ref, o_ref, lse_ref,
    dq_ref, dk_ref, dv_ref, rdk_ref, rdv_ref, dq_sum, dk_sum, dv_sum, *, block,
):
    rows = q_ref.shape[0]
    far_rows = rk_ref.shape[0]
    masks = pair_masks()
    blocks = rows // block

    def prepare(index):
        here = slice(index * block, (index + 1) * block)
        out_grad = do_ref[here, :]
        product = jnp.transpose(out_grad.astype(F32) * o_ref[here, :].astype(F32))
        result = []
        for head in range(2):
            query = q_ref[here, :] * (masks[head] * 0.125).astype(BF16)
            masked = out_grad * masks[head].astype(BF16)
            delta = jnp.sum(product[64 * head : 64 * head + 64], axis=0, keepdims=True)
            lse = lse_ref[0, head : head + 1, here]
            result.append((query, masked, delta, lse))
        return result

    def terms(ready, keys, values, diagonal):
        key_grad = value_grad = query_grad = 0.0
        for head in range(2):
            query, masked, delta, lse = ready[head]
            scores = dot(keys, query, 1, 1)
            if diagonal:
                size = scores.shape[0]
                last = causal(scores[size - block :], block)
                if size > block:
                    scores = jnp.concatenate([scores[: size - block], last], axis=0)
                else:
                    scores = last
            probs = jnp.exp(scores - lse)
            prob_grad = dot(values, masked, 1, 1)
            score_grad = (probs * (prob_grad - delta)).astype(BF16)
            value_grad += dot(probs.astype(BF16), masked, 1, 0)
            key_grad += dot(score_grad, query, 1, 0)
            part = keys * (masks[head] * 0.125).astype(BF16)
            query_grad += dot(part, score_grad, 0, 0)
        return key_grad, value_grad, query_grad

    for index in reversed(range(blocks)):
        here = slice(index * block, (index + 1) * block)
        size = (index + 1) * block
        key_grad, value_grad, query_grad = terms(
            prepare(index), k_ref[0:size, :], v_ref[0:size, :], True
        )
        if index == blocks - 1:
            dk_sum[...] = key_grad
            dv_sum[...] = value_grad
        else:
            dk_sum[0:size, :] += key_grad
            dv_sum[0:size, :] += value_grad
        dq_sum[:, here] = query_grad

    def far(step, unused):
        start = pl.multiple_of(step * rows, rows)
        spot = pl.ds(start, rows)
        keys = rk_ref[spot, :]
        values = rv_ref[spot, :]
        key_total = value_total = 0.0
        for index in range(blocks):
            here = slice(index * block, (index + 1) * block)
            key_grad, value_grad, query_grad = terms(prepare(index), keys, values, False)
            key_total += key_grad
            value_total += value_grad
            dq_sum[:, here] += query_grad
        rdk_ref[spot, :] = key_total.astype(BF16)
        rdv_ref[spot, :] = value_total.astype(BF16)
        return unused

    lax.fori_loop(0, count[0], far, 0)

    def clear(step, unused):
        spot = pl.ds(pl.multiple_of(step * rows, rows), rows)
        rdk_ref[spot, :] = jnp.zeros((rows, 128), BF16)
        rdv_ref[spot, :] = jnp.zeros((rows, 128), BF16)
        return unused

    lax.fori_loop(count[0], far_rows // rows, clear, 0)
    dq_ref[...] = jnp.transpose(dq_sum[...]).astype(BF16)
    dk_ref[...] = dk_sum[...]
    dv_ref[...] = dv_sum[...]


def attend_back(count, queries, near, remote, out_grad, attended, lse, block, first=0):
    rows, width = attended.shape
    pairs, total = width // 128, queries.shape[1] // 128
    far_rows = remote.shape[0]
    column = lambda size, offset: pl.BlockSpec((size, 128), lambda h, c: (0, h + offset))
    return pl.pallas_call(
        functools.partial(attend_back_kernel, block=block),
        grid_spec=pltpu.PrefetchScalarGridSpec(
            num_scalar_prefetch=1,
            grid=(pairs,),
            in_specs=[
                column(rows, first),
                column(rows, first),
                column(rows, first + total),
                column(far_rows, first),
                column(far_rows, first + total),
                column(rows, first),
                column(rows, 0),
                pl.BlockSpec((1, 2, rows), lambda h, c: (h, 0, 0)),
            ],
            out_specs=[
                column(rows, 0),
                column(rows, 0),
                column(rows, 0),
                column(far_rows, 0),
                column(far_rows, 0),
            ],
            scratch_shapes=[
                pltpu.VMEM((128, rows), F32),
                pltpu.VMEM((rows, 128), F32),
                pltpu.VMEM((rows, 128), F32),
            ],
        ),
        out_shape=[
            jax.ShapeDtypeStruct((rows, width), BF16),
            jax.ShapeDtypeStruct((rows, width), F32),
            jax.ShapeDtypeStruct((rows, width), F32),
            jax.ShapeDtypeStruct((far_rows, width), BF16),
            jax.ShapeDtypeStruct((far_rows, width), BF16),
        ],
        compiler_params=pltpu.CompilerParams(vmem_limit_bytes=16 * MEGA),
        cost_estimate=pl.CostEstimate(
            flops=2 * rows * rows * width // 1, bytes_accessed=rows * width * 3 // 1, transcendentals=0
        ),
        name="attend_back",
    )(count, queries, near, near, remote, remote, out_grad, attended, lse)


def pairs_of(count, target):
    return [(index, target(index)) for index in range(count)]


def swap_cores(value, count):
    return lax.ppermute(value, "dp", pairs_of(count, lambda index: index ^ 1))


def swap_seq(value):
    return lax.ppermute(value, "seq", [(0, 1), (1, 0)])


def exchange_rows(value, dp=16):
    pairs = []
    for index in range(0, dp, 2):
        left, right = (index + 1) * 2, index * 2 + 1
        pairs += [(left, right), (right, left)]
    return lax.ppermute(value, ("dp", "seq"), pairs)


def regroup(value, dp, moves):
    return jnp.where(moves, exchange_rows(value, dp), value)


def turn_rows(value, back):
    pairs = []
    for first in range(0, 32, 4):
        steps = [(0, 2), (2, 3), (3, 1), (1, 0)]
        pairs += [(first + b, first + a) if back else (first + a, first + b) for a, b in steps]
    return lax.ppermute(value, ("dp", "seq"), pairs)


def deal(value, turn, cross, core, moves):
    size = value.shape[0] // 2
    first, second = value[:size], value[size:]
    base = jnp.where(moves, cross(first), first)
    came = turn(second)
    lead = core == 0
    return jnp.concatenate([jnp.where(lead, base, came), jnp.where(lead, came, base)], axis=0)


def undeal(value, turn, cross, core, moves):
    size = value.shape[0] // 2
    low, high = value[:size], value[size:]
    lead = core == 0
    base = jnp.where(lead, low, high)
    came = turn(jnp.where(lead, high, low))
    return jnp.concatenate([jnp.where(moves, cross(base), base), came], axis=0)


def split_columns(value, width):
    return [value[:, at : at + width] for at in range(0, value.shape[1], width)]


def gather_pack(blocks, dp):
    sizes = [block.shape[0] for block in blocks]
    packed = lax.all_gather(jnp.concatenate(blocks, axis=0), "dp", axis=0)
    if dp == GROUPS:
        return packed
    parts, at = [], 0
    for size in sizes:
        part = packed[:, at : at + size]
        parts.append(part.reshape(GROUPS, -1, part.shape[2]))
        at += size
    return jnp.concatenate(parts, axis=1)


def scatter_pack(packed, sizes, dp):
    if dp != GROUPS:
        parts, at = [], 0
        for size in sizes:
            whole = size * dp // GROUPS
            part = packed[:, at : at + whole]
            parts.append(part.reshape(dp, size, part.shape[2]))
            at += whole
        packed = jnp.concatenate(parts, axis=1)
    return lax.psum_scatter(packed, "dp", scatter_dimension=0)


def sum_seq(value, sequence_parts):
    if sequence_parts == 2:
        return value.astype(F32) + swap_seq(value).astype(F32)
    return lax.psum(value, "seq").astype(F32)


def place(grad, master, slot):
    marker = (jnp.arange(master.shape[0]) == slot).astype(F32)
    return marker.reshape((-1,) + (1,) * grad.ndim) * grad[None]


def spot(place):
    index = place[0]
    return index >> 2, (index >> 1) & 1, index & 1, place[1]


def whole(shape):
    return pl.BlockSpec(shape, lambda *unused: (0,) * len(shape))


ANYWHERE = pl.BlockSpec(memory_space=pl.ANY)


def kernel_call(body, scalars, in_specs, args, out_specs, out_shape, scratch, name, flops, moved):
    return pl.pallas_call(
        body,
        grid_spec=pltpu.PrefetchScalarGridSpec(
            num_scalar_prefetch=len(scalars),
            grid=(1,),
            in_specs=in_specs,
            out_specs=out_specs,
            scratch_shapes=scratch,
        ),
        out_shape=out_shape,
        compiler_params=pltpu.CompilerParams(vmem_limit_bytes=VMEM[name] * MEGA),
        cost_estimate=pl.CostEstimate(flops=flops // 2, bytes_accessed=moved // 2, transcendentals=0),
        name=name,
    )(*scalars, *args)


def pack_kernel(slots, place, *refs):
    masters, (head, tail, lines) = refs[:12], refs[12:]
    part, width = masters[4].shape
    lines[...] = jnp.zeros_like(lines)
    for row, number in enumerate(SMALL):
        master = masters[number]
        lines[row : row + 1, 0 : master.shape[1]] = master[pl.ds(slots[number], 1), :]
    for at in range(3):
        head[at * part : (at + 1) * part, :] = masters[2][:, at * width : (at + 1) * width].astype(BF16)
    head[3 * part : 4 * part, :] = masters[4][...].astype(BF16)
    head[4 * part :, :] = lines[...].astype(BF16)

    @pl.when(place[1] == 0)
    def shrink():
        tail[...] = masters[10][...].astype(BF16)

    @pl.when(place[1] != 0)
    def expand():
        for at in range(masters[8].shape[1] // width):
            tail[at * part : (at + 1) * part, :] = masters[8][:, at * width : (at + 1) * width].astype(BF16)


def pack(slots, place, masters):
    specs = []
    for number, master in enumerate(masters):
        if master.ndim == 2:
            specs.append(whole(master.shape))
        else:
            specs.append(
                pl.BlockSpec(
                    (None,) + master.shape[1:],
                    functools.partial(lambda step, slots, place, number: (slots[number], 0, 0), number=number),
                )
            )
    part, width = masters[4].shape[1:]
    rows = 4 * part + 16
    tail_rows = masters[10].shape[1]
    return kernel_call(
        pack_kernel, (slots, place), specs, masters,
        [whole((rows, width)), whole((tail_rows, width))],
        [jax.ShapeDtypeStruct((rows, width), BF16), jax.ShapeDtypeStruct((tail_rows, width), BF16)],
        [pltpu.VMEM((16, width), F32)], "pack", 0, 4 * rows * width * 6,
    )


def shift_z(value):
    return lax.ppermute(value, "dp", pairs_of(16, lambda index: (index + 4) % 16))


def swap_x(value):
    return lax.ppermute(value, "dp", pairs_of(16, lambda index: index ^ 2))


def after(value, *earlier):
    return lax.optimization_barrier((value,) + earlier)[0]


class Lane:
    def __init__(self, move, depth=2):
        self.move, self.depth, self.sent = move, depth, []

    def __call__(self, value, move=None):
        if len(self.sent) >= self.depth:
            value = after(value, self.sent[-self.depth])
        self.sent.append((move or self.move)(value))
        return self.sent[-1]


def ring_slots(z, x):
    slots = []
    for step in range(4):
        base = ((z - step) & 3) * 4
        slots += [base + x * 2, base + (1 - x) * 2]
    return slots


def gather(head, tail, values, out_grad, core, moves):
    z, x, y = Lane(shift_z, 2), Lane(swap_x, 1), Lane(swap_seq, 2)
    head, tail = [head], [tail]
    head_x, tail_x, tail_y, tail_xy = [], [], [], []
    head.append(z(head[0]))
    head_x.append(x(head[0]))
    tail_y.append(y(tail[0]))
    head.append(z(head[1]))
    tail_x.append(x(tail[0]))
    turn = lambda value: y(value, functools.partial(turn_rows, back=False))
    cross = lambda value: y(value, exchange_rows)
    values = deal(values, turn, cross, core, moves)
    tail.append(z(tail[0]))
    head_x.append(x(head[1]))
    out_grad = deal(out_grad, turn, cross, core, moves)
    head.append(z(head[2]))
    head_x.append(x(head[2]))
    tail_xy.append(y(tail_x[0]))
    tail.append(z(tail[1]))
    head_x.append(x(head[3]))
    tail_y.append(y(tail[1]))
    tail_x.append(x(tail[1]))
    values = after(values, tail_xy[0], tail[2], tail_x[1])
    tail.append(z(tail[2]))
    tail_xy.append(y(tail_x[1]))
    tail_x.append(x(tail[2]))
    tail_y.append(y(tail[2]))
    tail_x.append(x(tail[3]))
    mix = lambda first, second: [piece for pair in zip(first, second) for piece in pair]

    def rest(first, second):
        tail_xy.append(y(after(tail_x[2], first)))
        tail_y.append(y(after(tail[3], first)))
        tail_xy.append(y(after(tail_x[3], second)))
        return mix(tail_y, tail_xy), out_grad

    return mix(head, head_x), mix(tail, tail_x), values, rest


def row_sum(value):
    return jnp.sum(value, axis=0, keepdims=True)


def normalise(values):
    average = jnp.mean(values, axis=-1, keepdims=True)
    centered = values - average
    scale = lax.rsqrt(jnp.mean(centered * centered, axis=-1, keepdims=True) + EPSILON)
    return centered * scale, scale


def norm_back(grad, gain, shape, scale):
    inner = grad * gain
    first = jnp.mean(inner, axis=-1, keepdims=True)
    second = jnp.mean(inner * shape, axis=-1, keepdims=True)
    return scale * (inner - first - shape * second)


def balanced_kernel(extra, q_ref, k_ref, v_ref, rk_ref, rv_ref, o_ref, lse_ref, *, block):
    masks = pair_masks()
    index = extra[0]
    first = (index == 0).astype(F32)
    spot = pl.ds(pl.multiple_of(index * block, block), block)
    keys = jnp.concatenate([k_ref[0:block, :], rk_ref[0:block, :], k_ref[block:, :]], axis=0)
    values = jnp.concatenate([v_ref[0:block, :], rv_ref[0:block, :], v_ref[block:, :]], axis=0)
    sums, totals = [[], []], [[], []]
    for head in range(2):
        mask = (masks[head] * 0.125).astype(BF16)
        long = dot(keys, q_ref[block:, :] * mask, 1, 1)
        last = causal(long[2 * block :], block)
        long = long[: 2 * block]
        short = causal(dot(keys[0:block], q_ref[0:block, :] * mask, 1, 1), block)
        more = dot(rk_ref[spot, :], q_ref[spot, :] * mask, 1, 1)
        peak = lambda value: jnp.max(value, axis=0, keepdims=True)
        top_more = peak(more)
        top_short = peak(short)
        top_long = jnp.maximum(peak(long), peak(last))
        joined_short = jnp.maximum(top_short, top_more)
        joined_long = jnp.maximum(top_long, top_more)
        at_first = index == 0
        top_short = jnp.where(at_first, joined_short, top_short)
        top_long = jnp.where(at_first, top_long, joined_long)
        more = jnp.exp(more - jnp.where(at_first, top_short, top_long))
        short = jnp.exp(short - top_short)
        long = jnp.exp(long - top_long)
        last = jnp.exp(last - top_long)
        more_total = row_sum(more)
        more_sum = dot(rv_ref[spot, :], more.astype(BF16), 0, 0)
        short_total = row_sum(short) + first * more_total
        long_total = row_sum(long) + row_sum(last) + (1.0 - first) * more_total
        long_low = jnp.concatenate([long.astype(BF16), last.astype(BF16)], axis=0)
        half = slice(64 * head, 64 * head + 64)
        sums[0].append((dot(values[0:block], short.astype(BF16), 0, 0) + first * more_sum)[half] / short_total)
        sums[1].append((dot(values, long_low, 0, 0) + (1.0 - first) * more_sum)[half] / long_total)
        lse_ref[0, head : head + 1, 0:block] = top_short + jnp.log(short_total)
        lse_ref[0, head : head + 1, block:] = top_long + jnp.log(long_total)
    for part in range(2):
        joined = jnp.concatenate(sums[part], axis=0)
        o_ref[part * block : (part + 1) * block, :] = jnp.transpose(joined).astype(BF16)


def balanced_back_kernel(
    extra, q_ref, k_ref, v_ref, rk_ref, rv_ref, do_ref, o_ref, lse_ref,
    dq_ref, dk_ref, dv_ref, rdk_ref, rdv_ref, *, block,
):
    masks = pair_masks()
    index = extra[0]
    first = (index == 0).astype(F32)
    spot = pl.ds(pl.multiple_of(index * block, block), block)
    keys = jnp.concatenate([k_ref[0:block, :], rk_ref[0:block, :], k_ref[block:, :]], axis=0)
    values = jnp.concatenate([v_ref[0:block, :], rv_ref[0:block, :], v_ref[block:, :]], axis=0)
    product = jnp.transpose(do_ref[...].astype(F32) * o_ref[...].astype(F32))
    key_grads, value_grads, query_grads = [0.0] * 3, [0.0] * 3, [0.0] * 3
    for head in range(2):
        mask = masks[head].astype(BF16)
        scaled = (masks[head] * 0.125).astype(BF16)
        delta = row_sum(product[64 * head : 64 * head + 64])
        lse = lse_ref[0, head : head + 1, :]
        pick = lambda row: jnp.where(index == 0, row[:, :block], row[:, block:])
        sets = (
            (slice(block, None), keys, values, lse[:, block:], delta[:, block:], 3),
            (slice(0, block), keys[0:block], values[0:block], lse[:, :block], delta[:, :block], 1),
            (spot, rk_ref[spot, :], rv_ref[spot, :], pick(lse), pick(delta), 0),
        )
        for at, (rows, near_keys, near_values, norm, shift, blocks) in enumerate(sets):
            query = q_ref[rows, :] * scaled
            grad = do_ref[rows, :] * mask
            scores = dot(near_keys, query, 1, 1)
            if blocks:
                last = causal(scores[(blocks - 1) * block :], block)
                scores = jnp.concatenate([scores[: (blocks - 1) * block], last], axis=0) if blocks > 1 else last
            probs = jnp.exp(scores - norm)
            score_grad = (probs * (dot(near_values, grad, 1, 1) - shift)).astype(BF16)
            value_grads[at] += dot(probs.astype(BF16), grad, 1, 0)
            key_grads[at] += dot(score_grad, query, 1, 0)
            query_grads[at] += dot(near_keys * scaled, score_grad, 0, 0)
    turned = jnp.concatenate([query_grads[1] + first * query_grads[2], query_grads[0] + (1.0 - first) * query_grads[2]], axis=1)
    dq_ref[...] = jnp.transpose(turned).astype(BF16)
    for out, far, grads in ((dk_ref, rdk_ref, key_grads), (dv_ref, rdv_ref, value_grads)):
        out[0:block, :] = (grads[0][0:block] + grads[1]).astype(BF16)
        out[block:, :] = grads[0][2 * block :].astype(BF16)
        far[0:block, :] = (grads[0][block : 2 * block] + first * grads[2]).astype(BF16)
        far[block:, :] = ((1.0 - first) * grads[2]).astype(BF16)


def balanced(extra, args, first, pairs, cost):
    queries = args[0]
    rows, width = queries.shape
    total = width // 128
    column = lambda offset: pl.BlockSpec((rows, 128), lambda h, c: (0, h + offset))
    line = pl.BlockSpec((1, 2, rows), lambda h, c: (h, 0, 0))
    half = jax.ShapeDtypeStruct((rows, pairs * 128), BF16)
    in_specs = [column(first), column(first), column(first + total), column(first), column(first + total)]
    operands = [queries, args[1], args[1], args[2], args[2]]
    if len(args) == 3:
        body, out_specs = balanced_kernel, [column(0), line]
        out_shape = [half, jax.ShapeDtypeStruct((pairs, 2, rows), F32)]
    else:
        body, out_specs, out_shape = balanced_back_kernel, [column(0)] * 5, [half] * 5
        in_specs += [column(first), column(0), line]
        operands += list(args[3:])
    return pl.pallas_call(
        functools.partial(body, block=rows // 2),
        grid_spec=pltpu.PrefetchScalarGridSpec(
            num_scalar_prefetch=1, grid=(pairs,), in_specs=in_specs, out_specs=out_specs
        ),
        out_shape=out_shape,
        compiler_params=pltpu.CompilerParams(vmem_limit_bytes=16 * MEGA),
        cost_estimate=pl.CostEstimate(flops=cost, bytes_accessed=cost // 1000, transcendentals=0),
        name="attend" if len(args) == 3 else "attend_back",
    )(extra, *operands)


def qkv_kernel(place, x_ref, *refs):
    pieces, (packed, n1_ref, q_ref, kv_ref, v48, v96, v192, sems) = refs[:16], refs[16:]
    z, x, core, half = spot(place)
    slots = ring_slots(z, x)
    slots = [slot + core for slot in slots] + [slot + 1 - core for slot in slots]
    copies = [
        pltpu.make_async_copy(piece, packed.at[slots[number]], sems.at[number])
        for number, piece in enumerate(pieces)
    ]
    for copy in copies:
        copy.start()
    width = x_ref.shape[1]
    part = width // GROUPS
    shape, unused = normalise(x_ref[...].astype(F32))
    for copy in copies:
        copy.wait()
    for group in range(GROUPS):
        lines = packed[group, 4 * part : 4 * part + 16, :].astype(F32)[0:8]
        for out in (v48, v96, v192):
            size = out.shape[1] // GROUPS
            out[:, group * size : (group + 1) * size] = lines[:, :size]
    normed = (shape * v48[0:1, :] + v48[1:2, :]).astype(BF16)
    n1_ref[...] = normed
    for at in range(3):
        weight = packed[:, at * part : (at + 1) * part, :].reshape(width, width)
        result = dot(normed, weight, 1, 0)
        if at == 0:
            q_ref[...] = (result + v96[2:3, :width]).astype(BF16)
        elif at == 1:
            kv_ref[:, :width] = result.astype(BF16)
        else:
            kv_ref[:, width:] = (result + v96[2:3, width:]).astype(BF16)


def qkv(place, values, pieces):
    rows, width = values.shape
    shapes = [
        ((GROUPS,) + pieces[0].shape, BF16), ((rows, width), BF16), ((rows, width), BF16), ((rows, 2 * width), BF16),
        ((8, width), F32), ((8, 2 * width), F32), ((8, 4 * width), F32),
    ]
    return kernel_call(
        qkv_kernel, (place,), [whole(values.shape)] + [ANYWHERE] * 16, [values] + pieces,
        [whole(shape) for shape, unused in shapes],
        [jax.ShapeDtypeStruct(shape, dtype) for shape, dtype in shapes],
        [pltpu.SemaphoreType.DMA((16,))], "qkv", 6 * rows * width * width, 20 * width * width,
    )


def merge_kernel(x_ref, o1_ref, o2_ref, weight, v48, m_ref, n2_ref):
    width = x_ref.shape[1]
    attended = jnp.concatenate([o1_ref[...], o2_ref[...]], axis=1)
    middle = x_ref[...].astype(F32) + dot(attended, weight[...].reshape(width, width), 1, 0) + v48[3:4, :]
    m_ref[...] = middle
    shape, unused = normalise(middle)
    n2_ref[...] = (shape * v48[4:5, :] + v48[5:6, :]).astype(BF16)


def merge_spec(packed):
    part = packed.shape[2] // GROUPS
    return pl.BlockSpec((GROUPS, part, packed.shape[2]), lambda *unused: (0, 3, 0))


def merge(values, attended, packed, v48):
    rows, width = values.shape
    return kernel_call(
        merge_kernel, (),
        [whole(values.shape)] + [whole(piece.shape) for piece in attended] + [merge_spec(packed), whole(v48.shape)],
        [values] + attended + [packed, v48], [whole(values.shape)] * 2,
        [jax.ShapeDtypeStruct((rows, width), F32), jax.ShapeDtypeStruct((rows, width), BF16)],
        [], "merge", 2 * rows * width * width, 12 * rows * width,
    )


def gelu_pair(value):
    scale, cubic = math.sqrt(2 / math.pi), 0.044715
    square = value * value
    bent = jnp.tanh(scale * value * (1.0 + cubic * square))
    half = 0.5 * (1.0 + bent)
    slope = half + 0.5 * value * (1.0 - bent * bent) * (scale * (1.0 + 3.0 * cubic * square))
    return value * half, slope


def ffn_kernel(place, *refs):
    pieces, refs = refs[:32], refs[32:]
    m_ref, n2_ref, gy_ref, merge_weight, v48, v192, out_ref, dm_ref, dz_ref, do_ref, g48, g192 = refs[:12]
    outs, (weights, grads, y, dn2, n2_t, u, df, in_sems, out_sems) = refs[12:20], refs[20:]
    z, x, core, half = spot(place)
    slots = ring_slots(z, x)
    spots = [(slot + core, half) for slot in slots] + [(slot + core, 1 - half) for slot in slots]
    spots += [(slot + 1 - core, half) for slot in slots] + [(slot + 1 - core, 1 - half) for slot in slots]
    copies = [
        pltpu.make_async_copy(piece, weights.at[spots[number][0], spots[number][1]], in_sems.at[number])
        for number, piece in enumerate(pieces)
    ]
    for copy in copies:
        copy.start()
    width = m_ref.shape[1]
    part = width // GROUPS
    n2_t[...] = jnp.transpose(n2_ref[...])
    y[...] = jnp.zeros_like(y)
    dn2[...] = jnp.zeros_like(dn2)
    for copy in copies:
        copy.wait()

    def step(at, unused):
        first = pl.multiple_of(at * 4, 4)
        lines = pl.ds(pl.multiple_of(at * part, 16), part)
        chunk = 256
        for column in range(0, width, chunk):
            place_in = pl.ds(pl.multiple_of(at * width + column, 128), chunk)
            expand = weights[:, 1, lines, column : column + chunk].reshape(width, chunk)
            hidden = dot(n2_ref[...], expand, 1, 0) + v192[6:7, place_in]
            shrink = weights[pl.ds(first, 4), 0].reshape(width, width)[column : column + chunk]
            active, slope = gelu_pair(hidden)
            u[:, column : column + chunk] = active.astype(BF16)
            hidden_grad = (dot(gy_ref[...], shrink, 1, 1) * slope).astype(BF16)
            df[:, column : column + chunk] = hidden_grad
            g192[0:1, place_in] = row_sum(hidden_grad.astype(F32))
        shrink = weights[pl.ds(first, 4), 0].reshape(width, width)
        expand = weights[:, 1, lines, :].reshape(width, width)
        y[...] += dot(u[...], shrink, 1, 0)
        dn2[...] += dot(df[...], expand, 1, 1)
        grads[pl.ds(first, 4), 0] = dot(u[...], gy_ref[...], 0, 0).astype(BF16).reshape(4, 4 * part, width)
        grads[:, 1, lines, :] = dot(n2_t[...], df[...], 1, 0).astype(BF16).reshape(GROUPS, part, width)
        return unused

    lax.fori_loop(0, 4, step, 0)
    copies = []
    for order in range(4):
        base = ((z - order) & 3) * 4
        for number, out in ((0, outs[2 * order]), (1, outs[2 * order + 1])):
            side = core if number == 0 else 1 - core
            for kind in range(2):
                for column in range(2):
                    source = base + (x if column == 0 else 1 - x) * 2 + side
                    copies.append(
                        pltpu.make_async_copy(
                            grads.at[source, half if kind == 0 else 1 - half],
                            out.at[column, kind],
                            out_sems.at[len(copies)],
                        )
                    )
    for copy in copies:
        copy.start()
    middle = m_ref[...]
    out_ref[...] = (middle + y[...] + v48[7:8, :]).astype(BF16)
    shape, scale = normalise(middle)
    second_grad = dn2[...]
    out_grad = gy_ref[...].astype(F32)
    middle_grad = out_grad + norm_back(second_grad, v48[4:5, :], shape, scale)
    dm_ref[...] = middle_grad
    low = middle_grad.astype(BF16)
    dz_ref[...] = low
    g48[...] = jnp.zeros_like(g48)
    g48[3:4, :] = row_sum(low.astype(F32))
    g48[4:5, :] = row_sum(shape * second_grad)
    g48[5:6, :] = row_sum(second_grad)
    g48[7:8, :] = row_sum(out_grad)
    do_ref[...] = dot(low, merge_weight[...].reshape(width, width), 1, 1).astype(BF16)
    for copy in copies:
        copy.wait()


def ffn(place, pieces, middle, second, out_grad, packed, v48, v192):
    rows, width = middle.shape
    ff = 4 * width
    tail_rows = pieces[0].shape[0]
    shapes = [
        ((rows, width), BF16), ((rows, width), F32), ((rows, width), BF16), ((rows, width), BF16),
        ((8, width), F32), ((8, ff), F32),
    ]
    part = jax.ShapeDtypeStruct((2, 2, tail_rows, width), BF16)
    pack_shape = (GROUPS, 2, tail_rows, width)
    results = kernel_call(
        ffn_kernel, (place,),
        [ANYWHERE] * 32
        + [whole(middle.shape), whole(second.shape), whole(out_grad.shape), merge_spec(packed), whole(v48.shape), whole(v192.shape)],
        pieces + [middle, second, out_grad, packed, v48, v192],
        [whole(shape) for shape, unused in shapes] + [ANYWHERE] * 8,
        [jax.ShapeDtypeStruct(shape, dtype) for shape, dtype in shapes] + [part] * 8,
        [
            pltpu.VMEM(pack_shape, BF16), pltpu.VMEM(pack_shape, BF16),
            pltpu.VMEM((rows, width), F32), pltpu.VMEM((rows, width), F32), pltpu.VMEM((width, rows), BF16),
            pltpu.VMEM((rows, width), BF16), pltpu.VMEM((rows, width), BF16),
            pltpu.SemaphoreType.DMA((32,)), pltpu.SemaphoreType.DMA((32,)),
        ],
        "ffn", 12 * rows * width * ff, 8 * width * ff,
    )
    return results[:6], results[6:]


def close_kernel(
    place, n1_ref, x_ref, q1, k1, v1, far_k1, far_v1, q2, k2, v2, far_k2, far_v2, o1, o2,
    dz_ref, dm_ref, packed, v48, g48_in, g192, *refs,
):
    join = lambda first, second: jnp.concatenate([first[...], second[...]], axis=1)
    grad_ref, outs, (grads, g48, g96, dt, sems) = refs[0], refs[1:9], refs[9:]
    z, x, core, half = spot(place)
    width = x_ref.shape[1]
    part = width // GROUPS
    normed_t = jnp.transpose(n1_ref[...])
    normed_grad = None
    for at in range(3):
        if at == 0:
            dt[...] = join(q1, q2)
        elif at == 1:
            dt[...] = (join(k1, k2).astype(F32) + join(far_k1, far_k2).astype(F32)).astype(BF16)
        else:
            dt[...] = (join(v1, v2).astype(F32) + join(far_v1, far_v2).astype(F32)).astype(BF16)
        if at != 1:
            g96[2:3, (at // 2) * width : (at // 2 + 1) * width] = row_sum(dt[...].astype(F32))
        weight = packed[:, at * part : (at + 1) * part, :].reshape(width, width)
        term = dot(dt[...], weight, 1, 1)
        normed_grad = term if normed_grad is None else normed_grad + term
        grads[:, at * part : (at + 1) * part, :] = dot(normed_t, dt[...], 1, 0).astype(BF16).reshape(GROUPS, part, width)
    grads[:, 3 * part : 4 * part, :] = dot(join(o1, o2), dz_ref[...], 0, 0).astype(BF16).reshape(GROUPS, part, width)
    shape, scale = normalise(x_ref[...].astype(F32))
    g48[...] = g48_in[...]
    g48[0:1, :] = row_sum(shape * normed_grad)
    g48[1:2, :] = row_sum(normed_grad)
    row = lax.broadcasted_iota(jnp.int32, (16, 1), 0)
    for group in range(GROUPS):
        lines = jnp.concatenate([g48[:, group * part : (group + 1) * part], jnp.zeros((8, part), F32)], axis=0)
        grads[group, 4 * part :, :] = jnp.zeros((16, width), BF16)
        pair = g96[2:3, group * 2 * part : (group + 1) * 2 * part]
        wide = g192[0:1, group * 4 * part : (group + 1) * 4 * part]
        spread = jnp.where(row == 6, wide, 0.0)
        left = jnp.where(row == 2, pair, 0.0)
        grads[group, 4 * part :, 0 : 4 * part] = spread.astype(BF16)
        grads[group, 4 * part :, 0 : 2 * part] = (spread[:, : 2 * part] + left).astype(BF16)
        keep = jnp.where((row == 2) | (row == 6), 0.0, lines) + spread[:, :part] + left[:, :part]
        grads[group, 4 * part :, 0:part] = keep.astype(BF16)
    copies = []
    for order in range(4):
        base = ((z - order) & 3) * 4
        for number, out in ((0, outs[2 * order]), (1, outs[2 * order + 1])):
            side = core if number == 0 else 1 - core
            for column in range(2):
                source = base + (x if column == 0 else 1 - x) * 2 + side
                copies.append(pltpu.make_async_copy(grads.at[source], out.at[column], sems.at[len(copies)]))
    for copy in copies:
        copy.start()
    grad_ref[...] = (dm_ref[...] + norm_back(normed_grad, v48[0:1, :], shape, scale)).astype(BF16)
    for copy in copies:
        copy.wait()


def close(place, args):
    rows, width = args[0].shape
    packed = args[16]
    head_rows = packed.shape[1]
    part = jax.ShapeDtypeStruct((2, head_rows, width), BF16)
    results = kernel_call(
        close_kernel, (place,), [whole(arg.shape) for arg in args], args,
        [whole((rows, width))] + [ANYWHERE] * 8,
        [jax.ShapeDtypeStruct((rows, width), BF16)] + [part] * 8,
        [
            pltpu.VMEM(packed.shape, BF16), pltpu.VMEM((8, width), F32), pltpu.VMEM((8, 2 * width), F32),
            pltpu.VMEM((rows, width), BF16), pltpu.SemaphoreType.DMA((16,)),
        ],
        "close", 14 * rows * width * width, 20 * width * width,
    )
    return results[0], results[1:]


def unpack_kernel(slots, place, head, head_far, tail, tail_far, *outs):
    part, width = outs[4].shape[1:]
    total = head[...].astype(F32) + head_far[...].astype(F32)
    own = tail[0].astype(F32) + tail_far[1].astype(F32)
    other = tail[1].astype(F32) + tail_far[0].astype(F32)
    lead = place[1] == 0
    shrink, expand = jnp.where(lead, own, other), jnp.where(lead, other, own)
    for row, number in enumerate(SMALL):
        out = outs[number]
        size = out.shape[1]
        line = total[4 * part + row : 4 * part + row + 1, :size]
        row_at = lax.broadcasted_iota(jnp.int32, out.shape, 0)
        out[...] = jnp.where(row_at == slots[number], line, 0.0)
    for slot in range(outs[2].shape[0]):
        chosen = lambda number, value: jnp.where(slots[number] == slot, value, 0.0)
        for at in range(3):
            outs[2][slot, :, at * width : (at + 1) * width] = chosen(2, total[at * part : (at + 1) * part])
        outs[4][slot] = chosen(4, total[3 * part : 4 * part])
        for at in range(outs[8].shape[2] // width):
            outs[8][slot, :, at * width : (at + 1) * width] = chosen(8, expand[at * part : (at + 1) * part])
        outs[10][slot] = chosen(10, shrink)


def unpack(slots, place, parts, masters):
    return kernel_call(
        unpack_kernel, (slots, place), [whole(part.shape) for part in parts], parts,
        [whole(master.shape) for master in masters],
        [jax.ShapeDtypeStruct(master.shape, F32) for master in masters],
        [], "unpack", 0, 8 * 1024 * 1024,
    )


def per_device_fast(inputs, cotangent, tie_slots, *masters):
    length, count, width = inputs.shape
    index, half = lax.axis_index("dp"), lax.axis_index("seq")
    place = jnp.stack([index, half]).astype(jnp.int32)
    core = index % 2
    moves = core != half
    head, tail = pack(tie_slots, place, masters)
    head_pieces, tail_pieces, values, rest = gather(
        head, tail, inputs.reshape(length, width), cotangent.reshape(length, width), core, moves
    )
    head_pieces = head_pieces + [swap_cores(piece, 16) for piece in head_pieces]
    packed, normed, queries, near, v48, v96, v192 = qkv(place, values, head_pieces)
    remote = swap_cores(near, 16)
    extra = (1 - core).astype(jnp.int32).reshape(1)
    half_pairs = width // 256
    queries = after(queries, tail_pieces[6], tail_pieces[3])
    attended, lse = [None, None], [None, None]
    attended[0], lse[0] = balanced(extra, (queries, near, remote), 0, half_pairs, 1000000)
    queries = after(queries, attended[0])
    attended[1], lse[1] = balanced(extra, (queries, near, remote), half_pairs, half_pairs, 1000000)
    tail_other, out_grad = rest(attended[0], attended[1])
    middle, second = merge(values, attended, packed, v48)
    late = lambda pieces, first: [
        swap_cores(after(piece, attended[1]) if number >= first else piece, 16) for number, piece in enumerate(pieces)
    ]
    tail_pieces = tail_pieces + late(tail_pieces, 4)
    tail_other = tail_other + late(tail_other, 5)
    (output, middle_grad, branch_grad, attended_grad, g48, g192), tail_parts = ffn(
        place, tail_pieces[:8] + tail_other[:8] + tail_pieces[8:] + tail_other[8:],
        middle, second, out_grad, packed, v48, v192,
    )
    z, x, y = Lane(shift_z, 2), Lane(swap_x, 3), Lane(swap_seq, 2)
    turn = lambda value: y(value, functools.partial(turn_rows, back=True))
    cross = lambda value: y(value, exchange_rows)
    came = [swap_cores(send, 16) for send in tail_parts[1::2]]
    kept = [keep + other for keep, other in zip(tail_parts[0::2], came)]
    tail_half, tail_part, head_part = {}, {}, {}
    attended_grad = after(attended_grad, *kept)
    tail_half[1] = kept[1][1, 0] + y(kept[1][1, 1])
    tail_half[2] = kept[2][1, 0] + y(kept[2][1, 1])
    tail_half[3] = kept[3][1, 0] + y(kept[3][1, 1])
    tail_half[0] = kept[0][1, 0] + y(kept[0][1, 1])
    grads = []
    for part in range(2):
        if part:
            attended_grad = after(attended_grad, grads[0], tail_half[1])
        query_grad, key_grad, value_grad, far_key, far_value = balanced(
            extra, (queries, near, remote, attended_grad, attended[part], lse[part]), part * half_pairs, half_pairs, 1000000
        )
        grads += [query_grad, key_grad, value_grad, swap_cores(far_key, 16), swap_cores(far_value, 16)]
    tail_part[1] = jnp.stack([kept[1][0, 0] + x(tail_half[1]), kept[1][0, 1]])
    tail_run = tail_run1 = z(tail_part[1])
    tail_part[2] = jnp.stack([kept[2][0, 0] + x(tail_half[2]), kept[2][0, 1]])
    tail_run = tail_run2 = z(tail_part[2] + tail_run)
    middle_grad = after(middle_grad, tail_run1)
    input_grad, head_parts = close(
        place,
        [
            normed, values, *grads, *attended, branch_grad, middle_grad, packed, v48, g48, g192,
        ],
    )
    came = [swap_cores(send, 16) for send in head_parts[1::2]]
    head_kept = [keep + other for keep, other in zip(head_parts[0::2], came)]
    output = undeal(output, turn, cross, core, moves)
    input_grad = undeal(input_grad, turn, cross, core, moves)
    head_part[1] = head_kept[1][0] + x(head_kept[1][1])
    head_run = head_run1 = z(head_part[1])
    tail_part[3] = jnp.stack([kept[3][0, 0] + x(tail_half[3]), kept[3][0, 1]])
    tail_run = tail_run3 = z(tail_part[3] + tail_run)
    head_part[2] = head_kept[2][0] + x(head_kept[2][1])
    head_run = head_run2 = z(head_part[2] + head_run)
    tail_part[0] = jnp.stack([kept[0][0, 0] + x(tail_half[0]), kept[0][0, 1]])
    tail_sum = tail_part[0] + tail_run
    head_part[3] = head_kept[3][0] + x(head_kept[3][1])
    head_run = head_run3 = z(head_part[3] + head_run)
    head_part[0] = head_kept[0][0] + x(head_kept[0][1])
    head_sum = head_part[0] + head_run
    input_grad = input_grad.astype(F32)
    grads = unpack(
        tie_slots, place, [head_sum, y(head_sum), tail_sum, y(tail_sum)], masters
    )
    shape = (length, count, width)
    return (output.reshape(shape), input_grad.reshape(shape)) + tuple(grads)


def per_device(
    inputs,
    cotangent,
    tie_slots,
    *masters,
):
    dp, sequence_parts = lax.axis_size("dp"), lax.axis_size("seq")
    length, count, width = inputs.shape
    rows = length * count
    block = math.gcd(length, 256)
    moved = sequence_parts == 2 and dp % 2 == 0
    core = lax.axis_index("dp") % 2
    moves = core != lax.axis_index("seq")
    place_index = core if moved else lax.axis_index("seq")
    chosen = [
        lax.dynamic_index_in_dim(masters[number], tie_slots[number], 0, keepdims=False).astype(BF16)
        for number in range(12)
    ]
    part = width // dp
    ff = masters[10].shape[1] * dp
    small = jnp.concatenate([chosen[number] for number in SMALL])
    widths = [chosen[number].shape[0] for number in SMALL]
    pad = 16 * GROUPS // dp
    small = jnp.pad(small.reshape(1, -1), ((0, pad - 1), (0, width - small.shape[0])))
    head_blocks = split_columns(chosen[2], width) + [chosen[4], small]
    tail_blocks = [chosen[10]] + split_columns(chosen[8], width)
    head_sizes = [piece.shape[0] for piece in head_blocks]
    tail_sizes = [piece.shape[0] for piece in tail_blocks]
    head_pack = gather_pack(head_blocks, dp)
    flat_in = inputs.reshape(rows, width)
    flat_cot = cotangent.reshape(rows, width)
    if moved:
        flat_in = regroup(flat_in, dp, moves)
        flat_cot = regroup(flat_cot, dp, moves)
    tail_pack = gather_pack(tail_blocks, dp)

    group_rows = width // GROUPS
    matrix = lambda pack, at: pack[:, at * group_rows : (at + 1) * group_rows].reshape(width, width)
    triple_weight = jnp.concatenate([matrix(head_pack, at) for at in range(3)], axis=1)
    merge_weight = matrix(head_pack, 3)
    per_group = GROUPS // dp if dp < GROUPS else dp // GROUPS
    lines = head_pack[:, 4 * group_rows :].reshape(dp, pad, width)[:, 0]
    vectors, at = [], 0
    for size in widths:
        vectors.append(lines[:, at : at + size].reshape(-1).astype(F32))
        at += size
    gain_one, shift_one, pair_bias, merge_bias, gain_two, shift_two, expand_bias, shrink_bias = vectors

    flat_in = flat_in.astype(F32)
    normed, norm_one_pull = jax.vjp(layer_norm, flat_in, gain_one, shift_one)
    normed_low = normed.astype(BF16)
    bias_full = jnp.concatenate([pair_bias[:width], jnp.zeros((width,), F32), pair_bias[width:]])
    triple = (jnp.dot(normed_low, triple_weight, preferred_element_type=F32) + bias_full).astype(BF16)
    queries, near = triple[:, :width], triple[:, width:]
    if moved:
        remote = swap_cores(near, dp)
    else:
        remote = lax.all_gather(near, "seq", axis=0, tiled=True)
    far_count = place_index.astype(jnp.int32).reshape(1)
    attended_low, lse = attend(far_count, queries, near, remote, block)
    middle = flat_in + jnp.dot(attended_low, merge_weight, preferred_element_type=F32) + merge_bias

    ff_rows = ff // GROUPS
    shrink_weight = tail_pack[:, :ff_rows].reshape(ff, width)
    expand_weight = jnp.concatenate(
        [
            tail_pack[:, ff_rows + at * group_rows : ff_rows + (at + 1) * group_rows].reshape(width, width)
            for at in range(ff // width)
        ],
        axis=1,
    )
    second, norm_two_pull = jax.vjp(layer_norm, middle, gain_two, shift_two)
    second_low = second.astype(BF16)
    hidden = jnp.dot(second_low, expand_weight, preferred_element_type=F32) + expand_bias
    active, gelu_pull = jax.vjp(lambda values: jax.nn.gelu(values, approximate=True), hidden)
    active_low = active.astype(BF16)
    result = middle + jnp.dot(active_low, shrink_weight, preferred_element_type=F32) + shrink_bias
    output = result.astype(BF16)
    if moved:
        output = regroup(output, dp, moves)
    grad_shrink_weight = dot(active_low, flat_cot, 0, 0)
    grad_shrink_bias = jnp.sum(flat_cot.astype(F32), axis=0)
    active_grad = dot(flat_cot, shrink_weight, 1, 1)
    hidden_grad = gelu_pull(active_grad)[0].astype(BF16)
    grad_expand_weight = dot(second_low, hidden_grad, 0, 0)
    grad_expand_bias = jnp.sum(hidden_grad.astype(F32), axis=0)
    second_grad = dot(hidden_grad, expand_weight, 1, 1)
    middle_part, grad_gain_two, grad_shift_two = norm_two_pull(second_grad)
    middle_grad = flat_cot.astype(F32) + middle_part
    grouped = lambda value: value.astype(BF16).reshape(GROUPS, -1, width)
    tail_grads = jnp.concatenate(
        [grouped(grad_shrink_weight)] + [grouped(piece) for piece in split_columns(grad_expand_weight, width)],
        axis=1,
    )
    tail_own = sum_seq(scatter_pack(tail_grads, tail_sizes, dp), sequence_parts)

    branch_grad = middle_grad.astype(BF16)
    grad_merge_weight = dot(attended_low, branch_grad, 0, 0)
    grad_merge_bias = jnp.sum(branch_grad.astype(F32), axis=0)
    attended_grad = dot(branch_grad, merge_weight, 1, 1).astype(BF16)
    query_grad, key_grad, value_grad, far_key, far_value = attend_back(
        far_count, queries, near, remote, attended_grad, attended_low, lse, block
    )
    far_grad = jnp.concatenate([far_key, far_value], axis=1)
    pair_grad = jnp.concatenate([key_grad, value_grad], axis=1)
    if moved:
        pair_grad = pair_grad + swap_cores(far_grad, dp).astype(F32)
    else:
        pair_grad = pair_grad + lax.psum_scatter(far_grad, "seq", scatter_dimension=0, tiled=True).astype(F32)
    triple_grad = jnp.concatenate([query_grad, pair_grad.astype(BF16)], axis=1)
    grad_triple_weight = dot(normed_low, triple_grad, 0, 0)
    column_sums = jnp.sum(triple_grad.astype(F32), axis=0)
    grad_pair_bias = jnp.concatenate([column_sums[:width], column_sums[2 * width :]])
    normed_grad = dot(triple_grad, triple_weight, 1, 1)
    input_part, grad_gain_one, grad_shift_one = norm_one_pull(normed_grad)
    input_grad = middle_grad + input_part
    if moved:
        input_grad = regroup(input_grad, dp, moves)
    small_grads = [
        grad_gain_one, grad_shift_one, grad_pair_bias, grad_merge_bias,
        grad_gain_two, grad_shift_two, grad_expand_bias, grad_shrink_bias,
    ]
    lines = jnp.concatenate([piece.reshape(dp, -1) for piece in small_grads], axis=1).astype(BF16)
    lines = jnp.pad(lines[:, None], ((0, 0), (0, pad - 1), (0, width - lines.shape[1])))
    head_grads = jnp.concatenate(
        [grouped(piece) for piece in split_columns(grad_triple_weight, width)]
        + [grouped(grad_merge_weight), lines.reshape(GROUPS, -1, width)],
        axis=1,
    )
    head_own = sum_seq(scatter_pack(head_grads, head_sizes, dp), sequence_parts)

    piece_rows = chosen[4].shape[0]
    cut = lambda pack, at, size: pack[at : at + size]
    own_triple = jnp.concatenate([cut(head_own, at * piece_rows, piece_rows) for at in range(3)], axis=1)
    own_merge = cut(head_own, 3 * piece_rows, piece_rows)
    own_small, at = [], 0
    for size in widths:
        own_small.append(head_own[4 * piece_rows, at : at + size])
        at += size
    shrink_rows = chosen[10].shape[0]
    own_shrink = tail_own[:shrink_rows]
    own_expand = jnp.concatenate(
        [cut(tail_own, shrink_rows + at * piece_rows, piece_rows) for at in range(ff // width)], axis=1
    )
    own = [
        own_small[0], own_small[1], own_triple, own_small[2], own_merge, own_small[3],
        own_small[4], own_small[5], own_expand, own_small[6], own_shrink, own_small[7],
    ]
    shape = (length, count, width)
    return (output.reshape(shape), input_grad.reshape(shape)) + tuple(
        place(grad, master, tie_slots[number]) for number, (grad, master) in enumerate(zip(own, masters))
    )


def solution(mesh):
    in_specs = (
        P("seq", "dp", None),
        P("seq", "dp", None),
        P(),
        P(None, "dp"),
        P(None, "dp"),
        P(None, "dp", None),
        P(None, "dp"),
        P(None, "dp", None),
        P(None, "dp"),
        P(None, "dp"),
        P(None, "dp"),
        P(None, "dp", None),
        P(None, "dp"),
        P(None, "dp", None),
        P(None, "dp"),
    )
    out_specs = (
        P("seq", "dp", None),
        P("seq", "dp", None),
        P(None, "dp"),
        P(None, "dp"),
        P(None, "dp", None),
        P(None, "dp"),
        P(None, "dp", None),
        P(None, "dp"),
        P(None, "dp"),
        P(None, "dp"),
        P(None, "dp", None),
        P(None, "dp"),
        P(None, "dp", None),
        P(None, "dp"),
    )
    sizes = dict(mesh.shape)
    body = per_device_fast if (sizes["dp"], sizes["seq"]) == (16, 2) else per_device
    return jax.shard_map(
        body, mesh=mesh, in_specs=in_specs, out_specs=out_specs, check_vma=False
    )
```

```python
import functools
import math

import jax
import jax.numpy as jnp
from jax import lax
from jax.experimental import pallas as pl
from jax.experimental.pallas import tpu as pltpu
from jax.sharding import PartitionSpec as P

H = 12
GROUPS = 16
SMALL = (0, 1, 3, 5, 6, 7, 9, 11)
EPSILON = 1e-05
NEGATIVE = -1e30
F32 = jnp.float32
BF16 = jnp.bfloat16
MEGA = 1024 * 1024
VMEM = {"pack": 60, "qkv": 28, "merge": 14, "ffn": 36, "close": 26, "unpack": 36}


def layer_norm(values, gain, shift):
    average = jnp.mean(values, axis=-1, keepdims=True)
    centered = values - average
    variance = jnp.mean(centered * centered, axis=-1, keepdims=True)
    return centered * lax.rsqrt(variance + EPSILON) * gain + shift


def dot(left, right, left_dim, right_dim):
    return lax.dot_general(
        left, right, (((left_dim,), (right_dim,)), ((), ())), preferred_element_type=F32
    )


def pair_masks():
    lane = lax.broadcasted_iota(jnp.int32, (1, 128), 1)
    low = (lane < 64).astype(F32)
    return low, 1.0 - low


def causal(scores, block):
    key = lax.broadcasted_iota(jnp.int32, (block, block), 0)
    query = lax.broadcasted_iota(jnp.int32, (block, block), 1)
    return jnp.where(key <= query, scores, NEGATIVE)


def attend_kernel(count, q_ref, k_ref, v_ref, rk_ref, rv_ref, o_ref, lse_ref, *, block):
    rows = q_ref.shape[0]
    masks = pair_masks()
    for index in range(rows // block):
        here = slice(index * block, (index + 1) * block)
        size = (index + 1) * block
        state = []
        parts = []
        for head in range(2):
            query = q_ref[here, :] * (masks[head] * 0.125).astype(BF16)
            parts.append(query)
            scores = dot(k_ref[0:size, :], query, 1, 1)
            last = causal(scores[size - block :], block)
            top = jnp.max(last, axis=0, keepdims=True)
            if index:
                scores = jnp.concatenate([scores[: size - block], last], axis=0)
                top = jnp.max(scores, axis=0, keepdims=True)
            else:
                scores = last
            lifted = jnp.exp(scores - top)
            total = jnp.sum(lifted, axis=0, keepdims=True)
            state += [top, total, dot(v_ref[0:size, :], lifted.astype(BF16), 0, 0)]

        def far(step, state):
            start = pl.multiple_of(step * rows, rows)
            keys = rk_ref[pl.ds(start, rows), :]
            values = rv_ref[pl.ds(start, rows), :]
            result = []
            for head in range(2):
                top, total, gathered = state[3 * head : 3 * head + 3]
                scores = dot(keys, parts[head], 1, 1)
                new_top = jnp.maximum(top, jnp.max(scores, axis=0, keepdims=True))
                factor = jnp.exp(top - new_top)
                lifted = jnp.exp(scores - new_top)
                total = total * factor + jnp.sum(lifted, axis=0, keepdims=True)
                gathered = gathered * factor + dot(values, lifted.astype(BF16), 0, 0)
                result += [new_top, total, gathered]
            return tuple(result)

        top0, total0, sum0, top1, total1, sum1 = lax.fori_loop(0, count[0], far, tuple(state))
        joined = jnp.concatenate([sum0[:64] / total0, sum1[64:] / total1], axis=0)
        o_ref[here, :] = jnp.transpose(joined).astype(BF16)
        lse_ref[0, 0:1, here] = top0 + jnp.log(total0)
        lse_ref[0, 1:2, here] = top1 + jnp.log(total1)


def attend(count, queries, near, remote, block, first=0, pairs=None):
    rows, width = queries.shape
    total = width // 128
    pairs = pairs or total
    far_rows = remote.shape[0]
    column = lambda size, offset: pl.BlockSpec((size, 128), lambda h, c: (0, h + offset))
    return pl.pallas_call(
        functools.partial(attend_kernel, block=block),
        grid_spec=pltpu.PrefetchScalarGridSpec(
            num_scalar_prefetch=1,
            grid=(pairs,),
            in_specs=[
                column(rows, first),
                column(rows, first),
                column(rows, first + total),
                column(far_rows, first),
                column(far_rows, first + total),
            ],
            out_specs=[column(rows, 0), pl.BlockSpec((1, 2, rows), lambda h, c: (h, 0, 0))],
        ),
        out_shape=[
            jax.ShapeDtypeStruct((rows, pairs * 128), BF16),
            jax.ShapeDtypeStruct((pairs, 2, rows), F32),
        ],
        compiler_params=pltpu.CompilerParams(vmem_limit_bytes=16 * MEGA),
        cost_estimate=pl.CostEstimate(
            flops=rows * rows * pairs * 100 // 1, bytes_accessed=rows * pairs * 150 // 1, transcendentals=0
        ),
        name="attend",
    )(count, queries, near, near, remote, remote)


def attend_back_kernel(
    count, q_ref, k_ref, v_ref, rk_ref, rv_ref, do_ref, o_ref, lse_ref,
    dq_ref, dk_ref, dv_ref, rdk_ref, rdv_ref, dq_sum, dk_sum, dv_sum, *, block,
):
    rows = q_ref.shape[0]
    far_rows = rk_ref.shape[0]
    masks = pair_masks()
    blocks = rows // block

    def prepare(index):
        here = slice(index * block, (index + 1) * block)
        out_grad = do_ref[here, :]
        product = jnp.transpose(out_grad.astype(F32) * o_ref[here, :].astype(F32))
        result = []
        for head in range(2):
            query = q_ref[here, :] * (masks[head] * 0.125).astype(BF16)
            masked = out_grad * masks[head].astype(BF16)
            delta = jnp.sum(product[64 * head : 64 * head + 64], axis=0, keepdims=True)
            lse = lse_ref[0, head : head + 1, here]
            result.append((query, masked, delta, lse))
        return result

    def terms(ready, keys, values, diagonal):
        key_grad = value_grad = query_grad = 0.0
        for head in range(2):
            query, masked, delta, lse = ready[head]
            scores = dot(keys, query, 1, 1)
            if diagonal:
                size = scores.shape[0]
                last = causal(scores[size - block :], block)
                if size > block:
                    scores = jnp.concatenate([scores[: size - block], last], axis=0)
                else:
                    scores = last
            probs = jnp.exp(scores - lse)
            prob_grad = dot(values, masked, 1, 1)
            score_grad = (probs * (prob_grad - delta)).astype(BF16)
            value_grad += dot(probs.astype(BF16), masked, 1, 0)
            key_grad += dot(score_grad, query, 1, 0)
            part = keys * (masks[head] * 0.125).astype(BF16)
            query_grad += dot(part, score_grad, 0, 0)
        return key_grad, value_grad, query_grad

    for index in reversed(range(blocks)):
        here = slice(index * block, (index + 1) * block)
        size = (index + 1) * block
        key_grad, value_grad, query_grad = terms(
            prepare(index), k_ref[0:size, :], v_ref[0:size, :], True
        )
        if index == blocks - 1:
            dk_sum[...] = key_grad
            dv_sum[...] = value_grad
        else:
            dk_sum[0:size, :] += key_grad
            dv_sum[0:size, :] += value_grad
        dq_sum[:, here] = query_grad

    def far(step, unused):
        start = pl.multiple_of(step * rows, rows)
        spot = pl.ds(start, rows)
        keys = rk_ref[spot, :]
        values = rv_ref[spot, :]
        key_total = value_total = 0.0
        for index in range(blocks):
            here = slice(index * block, (index + 1) * block)
            key_grad, value_grad, query_grad = terms(prepare(index), keys, values, False)
            key_total += key_grad
            value_total += value_grad
            dq_sum[:, here] += query_grad
        rdk_ref[spot, :] = key_total.astype(BF16)
        rdv_ref[spot, :] = value_total.astype(BF16)
        return unused

    lax.fori_loop(0, count[0], far, 0)

    def clear(step, unused):
        spot = pl.ds(pl.multiple_of(step * rows, rows), rows)
        rdk_ref[spot, :] = jnp.zeros((rows, 128), BF16)
        rdv_ref[spot, :] = jnp.zeros((rows, 128), BF16)
        return unused

    lax.fori_loop(count[0], far_rows // rows, clear, 0)
    dq_ref[...] = jnp.transpose(dq_sum[...]).astype(BF16)
    dk_ref[...] = dk_sum[...]
    dv_ref[...] = dv_sum[...]


def attend_back(count, queries, near, remote, out_grad, attended, lse, block, first=0):
    rows, width = attended.shape
    pairs, total = width // 128, queries.shape[1] // 128
    far_rows = remote.shape[0]
    column = lambda size, offset: pl.BlockSpec((size, 128), lambda h, c: (0, h + offset))
    return pl.pallas_call(
        functools.partial(attend_back_kernel, block=block),
        grid_spec=pltpu.PrefetchScalarGridSpec(
            num_scalar_prefetch=1,
            grid=(pairs,),
            in_specs=[
                column(rows, first),
                column(rows, first),
                column(rows, first + total),
                column(far_rows, first),
                column(far_rows, first + total),
                column(rows, first),
                column(rows, 0),
                pl.BlockSpec((1, 2, rows), lambda h, c: (h, 0, 0)),
            ],
            out_specs=[
                column(rows, 0),
                column(rows, 0),
                column(rows, 0),
                column(far_rows, 0),
                column(far_rows, 0),
            ],
            scratch_shapes=[
                pltpu.VMEM((128, rows), F32),
                pltpu.VMEM((rows, 128), F32),
                pltpu.VMEM((rows, 128), F32),
            ],
        ),
        out_shape=[
            jax.ShapeDtypeStruct((rows, width), BF16),
            jax.ShapeDtypeStruct((rows, width), F32),
            jax.ShapeDtypeStruct((rows, width), F32),
            jax.ShapeDtypeStruct((far_rows, width), BF16),
            jax.ShapeDtypeStruct((far_rows, width), BF16),
        ],
        compiler_params=pltpu.CompilerParams(vmem_limit_bytes=16 * MEGA),
        cost_estimate=pl.CostEstimate(
            flops=2 * rows * rows * width // 1, bytes_accessed=rows * width * 3 // 1, transcendentals=0
        ),
        name="attend_back",
    )(count, queries, near, near, remote, remote, out_grad, attended, lse)


def pairs_of(count, target):
    return [(index, target(index)) for index in range(count)]


def swap_cores(value, count):
    return lax.ppermute(value, "dp", pairs_of(count, lambda index: index ^ 1))


def swap_seq(value):
    return lax.ppermute(value, "seq", [(0, 1), (1, 0)])


def exchange_rows(value, dp=16):
    pairs = []
    for index in range(0, dp, 2):
        left, right = (index + 1) * 2, index * 2 + 1
        pairs += [(left, right), (right, left)]
    return lax.ppermute(value, ("dp", "seq"), pairs)


def regroup(value, dp, moves):
    return jnp.where(moves, exchange_rows(value, dp), value)


def turn_rows(value, back):
    pairs = []
    for first in range(0, 32, 4):
        steps = [(0, 2), (2, 3), (3, 1), (1, 0)]
        pairs += [(first + b, first + a) if back else (first + a, first + b) for a, b in steps]
    return lax.ppermute(value, ("dp", "seq"), pairs)


def deal(value, turn, cross, core, moves):
    size = value.shape[0] // 2
    first, second = value[:size], value[size:]
    base = jnp.where(moves, cross(first), first)
    came = turn(second)
    lead = core == 0
    return jnp.concatenate([jnp.where(lead, base, came), jnp.where(lead, came, base)], axis=0)


def undeal(value, turn, cross, core, moves):
    size = value.shape[0] // 2
    low, high = value[:size], value[size:]
    lead = core == 0
    base = jnp.where(lead, low, high)
    came = turn(jnp.where(lead, high, low))
    return jnp.concatenate([jnp.where(moves, cross(base), base), came], axis=0)


def split_columns(value, width):
    return [value[:, at : at + width] for at in range(0, value.shape[1], width)]


def gather_pack(blocks, dp):
    sizes = [block.shape[0] for block in blocks]
    packed = lax.all_gather(jnp.concatenate(blocks, axis=0), "dp", axis=0)
    if dp == GROUPS:
        return packed
    parts, at = [], 0
    for size in sizes:
        part = packed[:, at : at + size]
        parts.append(part.reshape(GROUPS, -1, part.shape[2]))
        at += size
    return jnp.concatenate(parts, axis=1)


def scatter_pack(packed, sizes, dp):
    if dp != GROUPS:
        parts, at = [], 0
        for size in sizes:
            whole = size * dp // GROUPS
            part = packed[:, at : at + whole]
            parts.append(part.reshape(dp, size, part.shape[2]))
            at += whole
        packed = jnp.concatenate(parts, axis=1)
    return lax.psum_scatter(packed, "dp", scatter_dimension=0)


def sum_seq(value, sequence_parts):
    if sequence_parts == 2:
        return value.astype(F32) + swap_seq(value).astype(F32)
    return lax.psum(value, "seq").astype(F32)


def place(grad, master, slot):
    marker = (jnp.arange(master.shape[0]) == slot).astype(F32)
    return marker.reshape((-1,) + (1,) * grad.ndim) * grad[None]


def spot(place):
    index = place[0]
    return index >> 2, (index >> 1) & 1, index & 1, place[1]


def whole(shape):
    return pl.BlockSpec(shape, lambda *unused: (0,) * len(shape))


ANYWHERE = pl.BlockSpec(memory_space=pl.ANY)


def kernel_call(body, scalars, in_specs, args, out_specs, out_shape, scratch, name, flops, moved):
    return pl.pallas_call(
        body,
        grid_spec=pltpu.PrefetchScalarGridSpec(
            num_scalar_prefetch=len(scalars),
            grid=(1,),
            in_specs=in_specs,
            out_specs=out_specs,
            scratch_shapes=scratch,
        ),
        out_shape=out_shape,
        compiler_params=pltpu.CompilerParams(vmem_limit_bytes=VMEM[name] * MEGA),
        cost_estimate=pl.CostEstimate(flops=flops // 2, bytes_accessed=moved // 2, transcendentals=0),
        name=name,
    )(*scalars, *args)


def pack_kernel(slots, place, *refs):
    masters, (head, tail, lines) = refs[:12], refs[12:]
    part, width = masters[4].shape
    lines[...] = jnp.zeros_like(lines)
    for row, number in enumerate(SMALL):
        master = masters[number]
        lines[row : row + 1, 0 : master.shape[1]] = master[pl.ds(slots[number], 1), :]
    for at in range(3):
        head[at * part : (at + 1) * part, :] = masters[2][:, at * width : (at + 1) * width].astype(BF16)
    head[3 * part : 4 * part, :] = masters[4][...].astype(BF16)
    head[4 * part :, :] = lines[...].astype(BF16)

    @pl.when(place[1] == 0)
    def shrink():
        tail[...] = masters[10][...].astype(BF16)

    @pl.when(place[1] != 0)
    def expand():
        for at in range(masters[8].shape[1] // width):
            tail[at * part : (at + 1) * part, :] = masters[8][:, at * width : (at + 1) * width].astype(BF16)


def pack(slots, place, masters):
    specs = []
    for number, master in enumerate(masters):
        if master.ndim == 2:
            specs.append(whole(master.shape))
        else:
            specs.append(
                pl.BlockSpec(
                    (None,) + master.shape[1:],
                    functools.partial(lambda step, slots, place, number: (slots[number], 0, 0), number=number),
                )
            )
    part, width = masters[4].shape[1:]
    rows = 4 * part + 16
    tail_rows = masters[10].shape[1]
    return kernel_call(
        pack_kernel, (slots, place), specs, masters,
        [whole((rows, width)), whole((tail_rows, width))],
        [jax.ShapeDtypeStruct((rows, width), BF16), jax.ShapeDtypeStruct((tail_rows, width), BF16)],
        [pltpu.VMEM((16, width), F32)], "pack", 0, 4 * rows * width * 6,
    )


def shift_z(value):
    return lax.ppermute(value, "dp", pairs_of(16, lambda index: (index + 4) % 16))


def swap_x(value):
    return lax.ppermute(value, "dp", pairs_of(16, lambda index: index ^ 2))


def after(value, *earlier):
    return lax.optimization_barrier((value,) + earlier)[0]


class Lane:
    def __init__(self, move, depth=2):
        self.move, self.depth, self.sent = move, depth, []

    def __call__(self, value, move=None):
        if len(self.sent) >= self.depth:
            value = after(value, self.sent[-self.depth])
        self.sent.append((move or self.move)(value))
        return self.sent[-1]


def ring_slots(z, x):
    slots = []
    for step in range(4):
        base = ((z - step) & 3) * 4
        slots += [base + x * 2, base + (1 - x) * 2]
    return slots


def gather(head, tail, values, out_grad, core, moves):
    z, x, y = Lane(shift_z, 2), Lane(swap_x, 1), Lane(swap_seq, 2)
    head, tail = [head], [tail]
    head_x, tail_x, tail_y, tail_xy = [], [], [], []
    head.append(z(head[0]))
    head_x.append(x(head[0]))
    tail_y.append(y(tail[0]))
    head.append(z(head[1]))
    tail_x.append(x(tail[0]))
    turn = lambda value: y(value, functools.partial(turn_rows, back=False))
    cross = lambda value: y(value, exchange_rows)
    values = deal(values, turn, cross, core, moves)
    tail.append(z(tail[0]))
    head_x.append(x(head[1]))
    out_grad = deal(out_grad, turn, cross, core, moves)
    head.append(z(head[2]))
    head_x.append(x(head[2]))
    tail_xy.append(y(tail_x[0]))
    tail.append(z(tail[1]))
    head_x.append(x(head[3]))
    tail_y.append(y(tail[1]))
    tail_x.append(x(tail[1]))
    values = after(values, tail_xy[0], tail[2], tail_x[1])
    tail.append(z(tail[2]))
    tail_xy.append(y(tail_x[1]))
    tail_x.append(x(tail[2]))
    tail_y.append(y(tail[2]))
    tail_x.append(x(tail[3]))
    mix = lambda first, second: [piece for pair in zip(first, second) for piece in pair]

    def rest(first, second):
        tail_xy.append(y(after(tail_x[2], first)))
        tail_y.append(y(after(tail[3], first)))
        tail_xy.append(y(after(tail_x[3], second)))
        return mix(tail_y, tail_xy), out_grad

    return mix(head, head_x), mix(tail, tail_x), values, rest


def row_sum(value):
    return jnp.sum(value, axis=0, keepdims=True)


def normalise(values):
    average = jnp.mean(values, axis=-1, keepdims=True)
    centered = values - average
    scale = lax.rsqrt(jnp.mean(centered * centered, axis=-1, keepdims=True) + EPSILON)
    return centered * scale, scale


def norm_back(grad, gain, shape, scale):
    inner = grad * gain
    first = jnp.mean(inner, axis=-1, keepdims=True)
    second = jnp.mean(inner * shape, axis=-1, keepdims=True)
    return scale * (inner - first - shape * second)


def balanced_kernel(extra, q_ref, k_ref, v_ref, rk_ref, rv_ref, o_ref, lse_ref, *, block):
    masks = pair_masks()
    index = extra[0]
    first = (index == 0).astype(F32)
    spot = pl.ds(pl.multiple_of(index * block, block), block)
    keys = jnp.concatenate([k_ref[0:block, :], rk_ref[0:block, :], k_ref[block:, :]], axis=0)
    values = jnp.concatenate([v_ref[0:block, :], rv_ref[0:block, :], v_ref[block:, :]], axis=0)
    sums, totals = [[], []], [[], []]
    for head in range(2):
        mask = (masks[head] * 0.125).astype(BF16)
        long = dot(keys, q_ref[block:, :] * mask, 1, 1)
        last = causal(long[2 * block :], block)
        long = long[: 2 * block]
        short = causal(dot(keys[0:block], q_ref[0:block, :] * mask, 1, 1), block)
        more = dot(rk_ref[spot, :], q_ref[spot, :] * mask, 1, 1)
        peak = lambda value: jnp.max(value, axis=0, keepdims=True)
        top_more = peak(more)
        top_short = peak(short)
        top_long = jnp.maximum(peak(long), peak(last))
        joined_short = jnp.maximum(top_short, top_more)
        joined_long = jnp.maximum(top_long, top_more)
        at_first = index == 0
        top_short = jnp.where(at_first, joined_short, top_short)
        top_long = jnp.where(at_first, top_long, joined_long)
        more = jnp.exp(more - jnp.where(at_first, top_short, top_long))
        short = jnp.exp(short - top_short)
        long = jnp.exp(long - top_long)
        last = jnp.exp(last - top_long)
        more_total = row_sum(more)
        more_sum = dot(rv_ref[spot, :], more.astype(BF16), 0, 0)
        short_total = row_sum(short) + first * more_total
        long_total = row_sum(long) + row_sum(last) + (1.0 - first) * more_total
        long_low = jnp.concatenate([long.astype(BF16), last.astype(BF16)], axis=0)
        half = slice(64 * head, 64 * head + 64)
        sums[0].append((dot(values[0:block], short.astype(BF16), 0, 0) + first * more_sum)[half] / short_total)
        sums[1].append((dot(values, long_low, 0, 0) + (1.0 - first) * more_sum)[half] / long_total)
        lse_ref[0, head : head + 1, 0:block] = top_short + jnp.log(short_total)
        lse_ref[0, head : head + 1, block:] = top_long + jnp.log(long_total)
    for part in range(2):
        joined = jnp.concatenate(sums[part], axis=0)
        o_ref[part * block : (part + 1) * block, :] = jnp.transpose(joined).astype(BF16)


def balanced_back_kernel(
    extra, q_ref, k_ref, v_ref, rk_ref, rv_ref, do_ref, o_ref, lse_ref,
    dq_ref, dk_ref, dv_ref, rdk_ref, rdv_ref, *, block,
):
    masks = pair_masks()
    index = extra[0]
    first = (index == 0).astype(F32)
    spot = pl.ds(pl.multiple_of(index * block, block), block)
    keys = jnp.concatenate([k_ref[0:block, :], rk_ref[0:block, :], k_ref[block:, :]], axis=0)
    values = jnp.concatenate([v_ref[0:block, :], rv_ref[0:block, :], v_ref[block:, :]], axis=0)
    product = jnp.transpose(do_ref[...].astype(F32) * o_ref[...].astype(F32))
    key_grads, value_grads, query_grads = [0.0] * 3, [0.0] * 3, [0.0] * 3
    for head in range(2):
        mask = masks[head].astype(BF16)
        scaled = (masks[head] * 0.125).astype(BF16)
        delta = row_sum(product[64 * head : 64 * head + 64])
        lse = lse_ref[0, head : head + 1, :]
        pick = lambda row: jnp.where(index == 0, row[:, :block], row[:, block:])
        sets = (
            (slice(block, None), keys, values, lse[:, block:], delta[:, block:], 3),
            (slice(0, block), keys[0:block], values[0:block], lse[:, :block], delta[:, :block], 1),
            (spot, rk_ref[spot, :], rv_ref[spot, :], pick(lse), pick(delta), 0),
        )
        for at, (rows, near_keys, near_values, norm, shift, blocks) in enumerate(sets):
            query = q_ref[rows, :] * scaled
            grad = do_ref[rows, :] * mask
            scores = dot(near_keys, query, 1, 1)
            if blocks:
                last = causal(scores[(blocks - 1) * block :], block)
                scores = jnp.concatenate([scores[: (blocks - 1) * block], last], axis=0) if blocks > 1 else last
            probs = jnp.exp(scores - norm)
            score_grad = (probs * (dot(near_values, grad, 1, 1) - shift)).astype(BF16)
            value_grads[at] += dot(probs.astype(BF16), grad, 1, 0)
            key_grads[at] += dot(score_grad, query, 1, 0)
            query_grads[at] += dot(near_keys * scaled, score_grad, 0, 0)
    turned = jnp.concatenate([query_grads[1] + first * query_grads[2], query_grads[0] + (1.0 - first) * query_grads[2]], axis=1)
    dq_ref[...] = jnp.transpose(turned).astype(BF16)
    for out, far, grads in ((dk_ref, rdk_ref, key_grads), (dv_ref, rdv_ref, value_grads)):
        out[0:block, :] = (grads[0][0:block] + grads[1]).astype(BF16)
        out[block:, :] = grads[0][2 * block :].astype(BF16)
        far[0:block, :] = (grads[0][block : 2 * block] + first * grads[2]).astype(BF16)
        far[block:, :] = ((1.0 - first) * grads[2]).astype(BF16)


def balanced(extra, args, first, pairs, cost):
    queries = args[0]
    rows, width = queries.shape
    total = width // 128
    column = lambda offset: pl.BlockSpec((rows, 128), lambda h, c: (0, h + offset))
    line = pl.BlockSpec((1, 2, rows), lambda h, c: (h, 0, 0))
    half = jax.ShapeDtypeStruct((rows, pairs * 128), BF16)
    in_specs = [column(first), column(first), column(first + total), column(first), column(first + total)]
    operands = [queries, args[1], args[1], args[2], args[2]]
    if len(args) == 3:
        body, out_specs = balanced_kernel, [column(0), line]
        out_shape = [half, jax.ShapeDtypeStruct((pairs, 2, rows), F32)]
    else:
        body, out_specs, out_shape = balanced_back_kernel, [column(0)] * 5, [half] * 5
        in_specs += [column(first), column(0), line]
        operands += list(args[3:])
    return pl.pallas_call(
        functools.partial(body, block=rows // 2),
        grid_spec=pltpu.PrefetchScalarGridSpec(
            num_scalar_prefetch=1, grid=(pairs,), in_specs=in_specs, out_specs=out_specs
        ),
        out_shape=out_shape,
        compiler_params=pltpu.CompilerParams(vmem_limit_bytes=16 * MEGA),
        cost_estimate=pl.CostEstimate(flops=cost, bytes_accessed=cost // 1000, transcendentals=0),
        name="attend" if len(args) == 3 else "attend_back",
    )(extra, *operands)


def qkv_kernel(place, x_ref, *refs):
    pieces, (packed, n1_ref, q_ref, kv_ref, v48, v96, v192, sems) = refs[:16], refs[16:]
    z, x, core, half = spot(place)
    slots = ring_slots(z, x)
    slots = [slot + core for slot in slots] + [slot + 1 - core for slot in slots]
    copies = [
        pltpu.make_async_copy(piece, packed.at[slots[number]], sems.at[number])
        for number, piece in enumerate(pieces)
    ]
    for copy in copies:
        copy.start()
    width = x_ref.shape[1]
    part = width // GROUPS
    shape, unused = normalise(x_ref[...].astype(F32))
    for copy in copies:
        copy.wait()
    for group in range(GROUPS):
        lines = packed[group, 4 * part : 4 * part + 16, :].astype(F32)[0:8]
        for out in (v48, v96, v192):
            size = out.shape[1] // GROUPS
            out[:, group * size : (group + 1) * size] = lines[:, :size]
    normed = (shape * v48[0:1, :] + v48[1:2, :]).astype(BF16)
    n1_ref[...] = normed
    for at in range(3):
        weight = packed[:, at * part : (at + 1) * part, :].reshape(width, width)
        result = dot(normed, weight, 1, 0)
        if at == 0:
            q_ref[...] = (result + v96[2:3, :width]).astype(BF16)
        elif at == 1:
            kv_ref[:, :width] = result.astype(BF16)
        else:
            kv_ref[:, width:] = (result + v96[2:3, width:]).astype(BF16)


def qkv(place, values, pieces):
    rows, width = values.shape
    shapes = [
        ((GROUPS,) + pieces[0].shape, BF16), ((rows, width), BF16), ((rows, width), BF16), ((rows, 2 * width), BF16),
        ((8, width), F32), ((8, 2 * width), F32), ((8, 4 * width), F32),
    ]
    return kernel_call(
        qkv_kernel, (place,), [whole(values.shape)] + [ANYWHERE] * 16, [values] + pieces,
        [whole(shape) for shape, unused in shapes],
        [jax.ShapeDtypeStruct(shape, dtype) for shape, dtype in shapes],
        [pltpu.SemaphoreType.DMA((16,))], "qkv", 6 * rows * width * width, 20 * width * width,
    )


def merge_kernel(x_ref, o1_ref, o2_ref, weight, v48, m_ref, n2_ref):
    width = x_ref.shape[1]
    attended = jnp.concatenate([o1_ref[...], o2_ref[...]], axis=1)
    middle = x_ref[...].astype(F32) + dot(attended, weight[...].reshape(width, width), 1, 0) + v48[3:4, :]
    m_ref[...] = middle
    shape, unused = normalise(middle)
    n2_ref[...] = (shape * v48[4:5, :] + v48[5:6, :]).astype(BF16)


def merge_spec(packed):
    part = packed.shape[2] // GROUPS
    return pl.BlockSpec((GROUPS, part, packed.shape[2]), lambda *unused: (0, 3, 0))


def merge(values, attended, packed, v48):
    rows, width = values.shape
    return kernel_call(
        merge_kernel, (),
        [whole(values.shape)] + [whole(piece.shape) for piece in attended] + [merge_spec(packed), whole(v48.shape)],
        [values] + attended + [packed, v48], [whole(values.shape)] * 2,
        [jax.ShapeDtypeStruct((rows, width), F32), jax.ShapeDtypeStruct((rows, width), BF16)],
        [], "merge", 2 * rows * width * width, 12 * rows * width,
    )


def gelu_pair(value):
    scale, cubic = math.sqrt(2 / math.pi), 0.044715
    square = value * value
    bent = jnp.tanh(scale * value * (1.0 + cubic * square))
    half = 0.5 * (1.0 + bent)
    slope = half + 0.5 * value * (1.0 - bent * bent) * (scale * (1.0 + 3.0 * cubic * square))
    return value * half, slope


def ffn_kernel(place, *refs):
    pieces, refs = refs[:32], refs[32:]
    m_far, n2_ref, gy_ref, packed, v48, v192, out_ref, dm_ref, dz_ref, do_ref, g48, g192 = refs[:12]
    outs, (weights, grads, y, dn2, n2_t, u, df, m_ref, merge_weight, in_sems, out_sems, late_sems) = refs[12:20], refs[20:]
    z, x, core, half = spot(place)
    slots = ring_slots(z, x)
    spots = [(slot + core, half) for slot in slots] + [(slot + core, 1 - half) for slot in slots]
    spots += [(slot + 1 - core, half) for slot in slots] + [(slot + 1 - core, 1 - half) for slot in slots]
    copies = [
        pltpu.make_async_copy(piece, weights.at[spots[number][0], spots[number][1]], in_sems.at[number])
        for number, piece in enumerate(pieces)
    ]
    for copy in copies:
        copy.start()
    width = m_ref.shape[1]
    part = width // GROUPS
    late = [
        pltpu.make_async_copy(m_far, m_ref, late_sems.at[0]),
        pltpu.make_async_copy(packed.at[:, 3 * part : 4 * part, :], merge_weight, late_sems.at[1]),
    ]
    for copy in late:
        copy.start()
    n2_t[...] = jnp.transpose(n2_ref[...])
    y[...] = jnp.zeros_like(y)
    dn2[...] = jnp.zeros_like(dn2)
    for copy in copies:
        copy.wait()

    def step(at, unused):
        first = pl.multiple_of(at * 4, 4)
        lines = pl.ds(pl.multiple_of(at * part, 16), part)
        chunk = 256
        for column in range(0, width, chunk):
            place_in = pl.ds(pl.multiple_of(at * width + column, 128), chunk)
            expand = weights[:, 1, lines, column : column + chunk].reshape(width, chunk)
            hidden = dot(n2_ref[...], expand, 1, 0) + v192[6:7, place_in]
            shrink = weights[pl.ds(first, 4), 0].reshape(width, width)[column : column + chunk]
            active, slope = gelu_pair(hidden)
            u[:, column : column + chunk] = active.astype(BF16)
            hidden_grad = (dot(gy_ref[...], shrink, 1, 1) * slope).astype(BF16)
            df[:, column : column + chunk] = hidden_grad
            g192[0:1, place_in] = row_sum(hidden_grad.astype(F32))
        shrink = weights[pl.ds(first, 4), 0].reshape(width, width)
        expand = weights[:, 1, lines, :].reshape(width, width)
        y[...] += dot(u[...], shrink, 1, 0)
        dn2[...] += dot(df[...], expand, 1, 1)
        grads[pl.ds(first, 4), 0] = dot(u[...], gy_ref[...], 0, 0).astype(BF16).reshape(4, 4 * part, width)
        grads[:, 1, lines, :] = dot(n2_t[...], df[...], 1, 0).astype(BF16).reshape(GROUPS, part, width)
        return unused

    lax.fori_loop(0, 4, step, 0)
    copies = []
    for order in range(4):
        base = ((z - order) & 3) * 4
        for number, out in ((0, outs[2 * order]), (1, outs[2 * order + 1])):
            side = core if number == 0 else 1 - core
            for kind in range(2):
                for column in range(2):
                    source = base + (x if column == 0 else 1 - x) * 2 + side
                    copies.append(
                        pltpu.make_async_copy(
                            grads.at[source, half if kind == 0 else 1 - half],
                            out.at[column, kind],
                            out_sems.at[len(copies)],
                        )
                    )
    for copy in copies:
        copy.start()
    for copy in late:
        copy.wait()
    middle = m_ref[...]
    out_ref[...] = (middle + y[...] + v48[7:8, :]).astype(BF16)
    shape, scale = normalise(middle)
    second_grad = dn2[...]
    out_grad = gy_ref[...].astype(F32)
    middle_grad = out_grad + norm_back(second_grad, v48[4:5, :], shape, scale)
    dm_ref[...] = middle_grad
    low = middle_grad.astype(BF16)
    dz_ref[...] = low
    g48[...] = jnp.zeros_like(g48)
    g48[3:4, :] = row_sum(low.astype(F32))
    g48[4:5, :] = row_sum(shape * second_grad)
    g48[5:6, :] = row_sum(second_grad)
    g48[7:8, :] = row_sum(out_grad)
    do_ref[...] = dot(low, merge_weight[...].reshape(width, width), 1, 1).astype(BF16)
    for copy in copies:
        copy.wait()


def ffn(place, pieces, middle, second, out_grad, packed, v48, v192):
    rows, width = middle.shape
    ff = 4 * width
    tail_rows = pieces[0].shape[0]
    shapes = [
        ((rows, width), BF16), ((rows, width), F32), ((rows, width), BF16), ((rows, width), BF16),
        ((8, width), F32), ((8, ff), F32),
    ]
    part = jax.ShapeDtypeStruct((2, 2, tail_rows, width), BF16)
    pack_shape = (GROUPS, 2, tail_rows, width)
    results = kernel_call(
        ffn_kernel, (place,),
        [ANYWHERE] * 32
        + [ANYWHERE, whole(second.shape), whole(out_grad.shape), ANYWHERE, whole(v48.shape), whole(v192.shape)],
        pieces + [middle, second, out_grad, packed, v48, v192],
        [whole(shape) for shape, unused in shapes] + [ANYWHERE] * 8,
        [jax.ShapeDtypeStruct(shape, dtype) for shape, dtype in shapes] + [part] * 8,
        [
            pltpu.VMEM(pack_shape, BF16), pltpu.VMEM(pack_shape, BF16),
            pltpu.VMEM((rows, width), F32), pltpu.VMEM((rows, width), F32), pltpu.VMEM((width, rows), BF16),
            pltpu.VMEM((rows, width), BF16), pltpu.VMEM((rows, width), BF16),
            pltpu.VMEM((rows, width), F32), pltpu.VMEM((GROUPS, width // GROUPS, width), BF16),
            pltpu.SemaphoreType.DMA((32,)), pltpu.SemaphoreType.DMA((32,)), pltpu.SemaphoreType.DMA((2,)),
        ],
        "ffn", 12 * rows * width * ff, 8 * width * ff,
    )
    return results[:6], results[6:]


def close_kernel(
    place, n1_ref, x_ref, q1, k1, v1, far_k1, far_v1, q2, k2, v2, far_k2, far_v2, o1, o2,
    dz_ref, dm_ref, packed, v48, g48_in, g192, *refs,
):
    join = lambda first, second: jnp.concatenate([first[...], second[...]], axis=1)
    grad_ref, outs, (grads, g48, g96, dt, sems) = refs[0], refs[1:9], refs[9:]
    z, x, core, half = spot(place)
    width = x_ref.shape[1]
    part = width // GROUPS
    normed_t = jnp.transpose(n1_ref[...])
    normed_grad = None
    for at in range(3):
        if at == 0:
            dt[...] = join(q1, q2)
        elif at == 1:
            dt[...] = (join(k1, k2).astype(F32) + join(far_k1, far_k2).astype(F32)).astype(BF16)
        else:
            dt[...] = (join(v1, v2).astype(F32) + join(far_v1, far_v2).astype(F32)).astype(BF16)
        if at != 1:
            g96[2:3, (at // 2) * width : (at // 2 + 1) * width] = row_sum(dt[...].astype(F32))
        weight = packed[:, at * part : (at + 1) * part, :].reshape(width, width)
        term = dot(dt[...], weight, 1, 1)
        normed_grad = term if normed_grad is None else normed_grad + term
        grads[:, at * part : (at + 1) * part, :] = dot(normed_t, dt[...], 1, 0).astype(BF16).reshape(GROUPS, part, width)
    grads[:, 3 * part : 4 * part, :] = dot(join(o1, o2), dz_ref[...], 0, 0).astype(BF16).reshape(GROUPS, part, width)
    shape, scale = normalise(x_ref[...].astype(F32))
    g48[...] = g48_in[...]
    g48[0:1, :] = row_sum(shape * normed_grad)
    g48[1:2, :] = row_sum(normed_grad)
    row = lax.broadcasted_iota(jnp.int32, (16, 1), 0)
    for group in range(GROUPS):
        lines = jnp.concatenate([g48[:, group * part : (group + 1) * part], jnp.zeros((8, part), F32)], axis=0)
        grads[group, 4 * part :, :] = jnp.zeros((16, width), BF16)
        pair = g96[2:3, group * 2 * part : (group + 1) * 2 * part]
        wide = g192[0:1, group * 4 * part : (group + 1) * 4 * part]
        spread = jnp.where(row == 6, wide, 0.0)
        left = jnp.where(row == 2, pair, 0.0)
        grads[group, 4 * part :, 0 : 4 * part] = spread.astype(BF16)
        grads[group, 4 * part :, 0 : 2 * part] = (spread[:, : 2 * part] + left).astype(BF16)
        keep = jnp.where((row == 2) | (row == 6), 0.0, lines) + spread[:, :part] + left[:, :part]
        grads[group, 4 * part :, 0:part] = keep.astype(BF16)
    copies = []
    for order in range(4):
        base = ((z - order) & 3) * 4
        for number, out in ((0, outs[2 * order]), (1, outs[2 * order + 1])):
            side = core if number == 0 else 1 - core
            for column in range(2):
                source = base + (x if column == 0 else 1 - x) * 2 + side
                copies.append(pltpu.make_async_copy(grads.at[source], out.at[column], sems.at[len(copies)]))
    for copy in copies:
        copy.start()
    grad_ref[...] = (dm_ref[...] + norm_back(normed_grad, v48[0:1, :], shape, scale)).astype(BF16)
    for copy in copies:
        copy.wait()


def close(place, args):
    rows, width = args[0].shape
    packed = args[16]
    head_rows = packed.shape[1]
    part = jax.ShapeDtypeStruct((2, head_rows, width), BF16)
    results = kernel_call(
        close_kernel, (place,), [whole(arg.shape) for arg in args], args,
        [whole((rows, width))] + [ANYWHERE] * 8,
        [jax.ShapeDtypeStruct((rows, width), BF16)] + [part] * 8,
        [
            pltpu.VMEM(packed.shape, BF16), pltpu.VMEM((8, width), F32), pltpu.VMEM((8, 2 * width), F32),
            pltpu.VMEM((rows, width), BF16), pltpu.SemaphoreType.DMA((16,)),
        ],
        "close", 14 * rows * width * width, 20 * width * width,
    )
    return results[0], results[1:]


def unpack_kernel(slots, place, head, head_far, tail, tail_far, *outs):
    part, width = outs[4].shape[1:]
    total = head[...].astype(F32) + head_far[...].astype(F32)
    own = tail[0].astype(F32) + tail_far[1].astype(F32)
    other = tail[1].astype(F32) + tail_far[0].astype(F32)
    lead = place[1] == 0
    shrink, expand = jnp.where(lead, own, other), jnp.where(lead, other, own)
    for row, number in enumerate(SMALL):
        out = outs[number]
        size = out.shape[1]
        line = total[4 * part + row : 4 * part + row + 1, :size]
        row_at = lax.broadcasted_iota(jnp.int32, out.shape, 0)
        out[...] = jnp.where(row_at == slots[number], line, 0.0)
    for slot in range(outs[2].shape[0]):
        chosen = lambda number, value: jnp.where(slots[number] == slot, value, 0.0)
        for at in range(3):
            outs[2][slot, :, at * width : (at + 1) * width] = chosen(2, total[at * part : (at + 1) * part])
        outs[4][slot] = chosen(4, total[3 * part : 4 * part])
        for at in range(outs[8].shape[2] // width):
            outs[8][slot, :, at * width : (at + 1) * width] = chosen(8, expand[at * part : (at + 1) * part])
        outs[10][slot] = chosen(10, shrink)


def unpack(slots, place, parts, masters):
    return kernel_call(
        unpack_kernel, (slots, place), [whole(part.shape) for part in parts], parts,
        [whole(master.shape) for master in masters],
        [jax.ShapeDtypeStruct(master.shape, F32) for master in masters],
        [], "unpack", 0, 8 * 1024 * 1024,
    )


def per_device_fast(inputs, cotangent, tie_slots, *masters):
    length, count, width = inputs.shape
    index, half = lax.axis_index("dp"), lax.axis_index("seq")
    place = jnp.stack([index, half]).astype(jnp.int32)
    core = index % 2
    moves = core != half
    head, tail = pack(tie_slots, place, masters)
    head_pieces, tail_pieces, values, rest = gather(
        head, tail, inputs.reshape(length, width), cotangent.reshape(length, width), core, moves
    )
    head_pieces = head_pieces + [swap_cores(piece, 16) for piece in head_pieces]
    packed, normed, queries, near, v48, v96, v192 = qkv(place, values, head_pieces)
    remote = swap_cores(near, 16)
    extra = (1 - core).astype(jnp.int32).reshape(1)
    half_pairs = width // 256
    queries = after(queries, tail_pieces[6], tail_pieces[3])
    attended, lse = [None, None], [None, None]
    attended[0], lse[0] = balanced(extra, (queries, near, remote), 0, half_pairs, 1000000)
    queries = after(queries, attended[0])
    attended[1], lse[1] = balanced(extra, (queries, near, remote), half_pairs, half_pairs, 1000000)
    tail_other, out_grad = rest(attended[0], attended[1])
    middle, second = merge(values, attended, packed, v48)
    late = lambda pieces, first: [
        swap_cores(after(piece, attended[1]) if number >= first else piece, 16) for number, piece in enumerate(pieces)
    ]
    tail_pieces = tail_pieces + late(tail_pieces, 4)
    tail_other = tail_other + late(tail_other, 5)
    (output, middle_grad, branch_grad, attended_grad, g48, g192), tail_parts = ffn(
        place, tail_pieces[:8] + tail_other[:8] + tail_pieces[8:] + tail_other[8:],
        middle, second, out_grad, packed, v48, v192,
    )
    z, x, y = Lane(shift_z, 2), Lane(swap_x, 3), Lane(swap_seq, 2)
    turn = lambda value: y(value, functools.partial(turn_rows, back=True))
    cross = lambda value: y(value, exchange_rows)
    came = [swap_cores(send, 16) for send in tail_parts[1::2]]
    kept = [keep + other for keep, other in zip(tail_parts[0::2], came)]
    tail_half, tail_part, head_part = {}, {}, {}
    attended_grad = after(attended_grad, *kept)
    tail_half[1] = kept[1][1, 0] + y(kept[1][1, 1])
    tail_half[2] = kept[2][1, 0] + y(kept[2][1, 1])
    tail_half[3] = kept[3][1, 0] + y(kept[3][1, 1])
    tail_half[0] = kept[0][1, 0] + y(kept[0][1, 1])
    grads = []
    for part in range(2):
        if part:
            attended_grad = after(attended_grad, grads[0], tail_half[1])
        query_grad, key_grad, value_grad, far_key, far_value = balanced(
            extra, (queries, near, remote, attended_grad, attended[part], lse[part]), part * half_pairs, half_pairs, 1000000
        )
        grads += [query_grad, key_grad, value_grad, swap_cores(far_key, 16), swap_cores(far_value, 16)]
    tail_part[1] = jnp.stack([kept[1][0, 0] + x(tail_half[1]), kept[1][0, 1]])
    tail_run = tail_run1 = z(tail_part[1])
    tail_part[2] = jnp.stack([kept[2][0, 0] + x(tail_half[2]), kept[2][0, 1]])
    tail_run = tail_run2 = z(tail_part[2] + tail_run)
    middle_grad = after(middle_grad, tail_run1)
    input_grad, head_parts = close(
        place,
        [
            normed, values, *grads, *attended, branch_grad, middle_grad, packed, v48, g48, g192,
        ],
    )
    came = [swap_cores(send, 16) for send in head_parts[1::2]]
    head_kept = [keep + other for keep, other in zip(head_parts[0::2], came)]
    output = undeal(output, turn, cross, core, moves)
    input_grad = undeal(input_grad, turn, cross, core, moves)
    head_part[1] = head_kept[1][0] + x(head_kept[1][1])
    head_run = head_run1 = z(head_part[1])
    tail_part[3] = jnp.stack([kept[3][0, 0] + x(tail_half[3]), kept[3][0, 1]])
    tail_run = tail_run3 = z(tail_part[3] + tail_run)
    head_part[2] = head_kept[2][0] + x(head_kept[2][1])
    head_run = head_run2 = z(head_part[2] + head_run)
    tail_part[0] = jnp.stack([kept[0][0, 0] + x(tail_half[0]), kept[0][0, 1]])
    tail_sum = tail_part[0] + tail_run
    head_part[3] = head_kept[3][0] + x(head_kept[3][1])
    head_run = head_run3 = z(head_part[3] + head_run)
    head_part[0] = head_kept[0][0] + x(head_kept[0][1])
    head_sum = head_part[0] + head_run
    input_grad = input_grad.astype(F32)
    grads = unpack(
        tie_slots, place, [head_sum, y(head_sum), tail_sum, y(tail_sum)], masters
    )
    shape = (length, count, width)
    return (output.reshape(shape), input_grad.reshape(shape)) + tuple(grads)


def per_device(
    inputs,
    cotangent,
    tie_slots,
    *masters,
):
    dp, sequence_parts = lax.axis_size("dp"), lax.axis_size("seq")
    length, count, width = inputs.shape
    rows = length * count
    block = math.gcd(length, 256)
    moved = sequence_parts == 2 and dp % 2 == 0
    core = lax.axis_index("dp") % 2
    moves = core != lax.axis_index("seq")
    place_index = core if moved else lax.axis_index("seq")
    chosen = [
        lax.dynamic_index_in_dim(masters[number], tie_slots[number], 0, keepdims=False).astype(BF16)
        for number in range(12)
    ]
    part = width // dp
    ff = masters[10].shape[1] * dp
    small = jnp.concatenate([chosen[number] for number in SMALL])
    widths = [chosen[number].shape[0] for number in SMALL]
    pad = 16 * GROUPS // dp
    small = jnp.pad(small.reshape(1, -1), ((0, pad - 1), (0, width - small.shape[0])))
    head_blocks = split_columns(chosen[2], width) + [chosen[4], small]
    tail_blocks = [chosen[10]] + split_columns(chosen[8], width)
    head_sizes = [piece.shape[0] for piece in head_blocks]
    tail_sizes = [piece.shape[0] for piece in tail_blocks]
    head_pack = gather_pack(head_blocks, dp)
    flat_in = inputs.reshape(rows, width)
    flat_cot = cotangent.reshape(rows, width)
    if moved:
        flat_in = regroup(flat_in, dp, moves)
        flat_cot = regroup(flat_cot, dp, moves)
    tail_pack = gather_pack(tail_blocks, dp)

    group_rows = width // GROUPS
    matrix = lambda pack, at: pack[:, at * group_rows : (at + 1) * group_rows].reshape(width, width)
    triple_weight = jnp.concatenate([matrix(head_pack, at) for at in range(3)], axis=1)
    merge_weight = matrix(head_pack, 3)
    per_group = GROUPS // dp if dp < GROUPS else dp // GROUPS
    lines = head_pack[:, 4 * group_rows :].reshape(dp, pad, width)[:, 0]
    vectors, at = [], 0
    for size in widths:
        vectors.append(lines[:, at : at + size].reshape(-1).astype(F32))
        at += size
    gain_one, shift_one, pair_bias, merge_bias, gain_two, shift_two, expand_bias, shrink_bias = vectors

    flat_in = flat_in.astype(F32)
    normed, norm_one_pull = jax.vjp(layer_norm, flat_in, gain_one, shift_one)
    normed_low = normed.astype(BF16)
    bias_full = jnp.concatenate([pair_bias[:width], jnp.zeros((width,), F32), pair_bias[width:]])
    triple = (jnp.dot(normed_low, triple_weight, preferred_element_type=F32) + bias_full).astype(BF16)
    queries, near = triple[:, :width], triple[:, width:]
    if moved:
        remote = swap_cores(near, dp)
    else:
        remote = lax.all_gather(near, "seq", axis=0, tiled=True)
    far_count = place_index.astype(jnp.int32).reshape(1)
    attended_low, lse = attend(far_count, queries, near, remote, block)
    middle = flat_in + jnp.dot(attended_low, merge_weight, preferred_element_type=F32) + merge_bias

    ff_rows = ff // GROUPS
    shrink_weight = tail_pack[:, :ff_rows].reshape(ff, width)
    expand_weight = jnp.concatenate(
        [
            tail_pack[:, ff_rows + at * group_rows : ff_rows + (at + 1) * group_rows].reshape(width, width)
            for at in range(ff // width)
        ],
        axis=1,
    )
    second, norm_two_pull = jax.vjp(layer_norm, middle, gain_two, shift_two)
    second_low = second.astype(BF16)
    hidden = jnp.dot(second_low, expand_weight, preferred_element_type=F32) + expand_bias
    active, gelu_pull = jax.vjp(lambda values: jax.nn.gelu(values, approximate=True), hidden)
    active_low = active.astype(BF16)
    result = middle + jnp.dot(active_low, shrink_weight, preferred_element_type=F32) + shrink_bias
    output = result.astype(BF16)
    if moved:
        output = regroup(output, dp, moves)
    grad_shrink_weight = dot(active_low, flat_cot, 0, 0)
    grad_shrink_bias = jnp.sum(flat_cot.astype(F32), axis=0)
    active_grad = dot(flat_cot, shrink_weight, 1, 1)
    hidden_grad = gelu_pull(active_grad)[0].astype(BF16)
    grad_expand_weight = dot(second_low, hidden_grad, 0, 0)
    grad_expand_bias = jnp.sum(hidden_grad.astype(F32), axis=0)
    second_grad = dot(hidden_grad, expand_weight, 1, 1)
    middle_part, grad_gain_two, grad_shift_two = norm_two_pull(second_grad)
    middle_grad = flat_cot.astype(F32) + middle_part
    grouped = lambda value: value.astype(BF16).reshape(GROUPS, -1, width)
    tail_grads = jnp.concatenate(
        [grouped(grad_shrink_weight)] + [grouped(piece) for piece in split_columns(grad_expand_weight, width)],
        axis=1,
    )
    tail_own = sum_seq(scatter_pack(tail_grads, tail_sizes, dp), sequence_parts)

    branch_grad = middle_grad.astype(BF16)
    grad_merge_weight = dot(attended_low, branch_grad, 0, 0)
    grad_merge_bias = jnp.sum(branch_grad.astype(F32), axis=0)
    attended_grad = dot(branch_grad, merge_weight, 1, 1).astype(BF16)
    query_grad, key_grad, value_grad, far_key, far_value = attend_back(
        far_count, queries, near, remote, attended_grad, attended_low, lse, block
    )
    far_grad = jnp.concatenate([far_key, far_value], axis=1)
    pair_grad = jnp.concatenate([key_grad, value_grad], axis=1)
    if moved:
        pair_grad = pair_grad + swap_cores(far_grad, dp).astype(F32)
    else:
        pair_grad = pair_grad + lax.psum_scatter(far_grad, "seq", scatter_dimension=0, tiled=True).astype(F32)
    triple_grad = jnp.concatenate([query_grad, pair_grad.astype(BF16)], axis=1)
    grad_triple_weight = dot(normed_low, triple_grad, 0, 0)
    column_sums = jnp.sum(triple_grad.astype(F32), axis=0)
    grad_pair_bias = jnp.concatenate([column_sums[:width], column_sums[2 * width :]])
    normed_grad = dot(triple_grad, triple_weight, 1, 1)
    input_part, grad_gain_one, grad_shift_one = norm_one_pull(normed_grad)
    input_grad = middle_grad + input_part
    if moved:
        input_grad = regroup(input_grad, dp, moves)
    small_grads = [
        grad_gain_one, grad_shift_one, grad_pair_bias, grad_merge_bias,
        grad_gain_two, grad_shift_two, grad_expand_bias, grad_shrink_bias,
    ]
    lines = jnp.concatenate([piece.reshape(dp, -1) for piece in small_grads], axis=1).astype(BF16)
    lines = jnp.pad(lines[:, None], ((0, 0), (0, pad - 1), (0, width - lines.shape[1])))
    head_grads = jnp.concatenate(
        [grouped(piece) for piece in split_columns(grad_triple_weight, width)]
        + [grouped(grad_merge_weight), lines.reshape(GROUPS, -1, width)],
        axis=1,
    )
    head_own = sum_seq(scatter_pack(head_grads, head_sizes, dp), sequence_parts)

    piece_rows = chosen[4].shape[0]
    cut = lambda pack, at, size: pack[at : at + size]
    own_triple = jnp.concatenate([cut(head_own, at * piece_rows, piece_rows) for at in range(3)], axis=1)
    own_merge = cut(head_own, 3 * piece_rows, piece_rows)
    own_small, at = [], 0
    for size in widths:
        own_small.append(head_own[4 * piece_rows, at : at + size])
        at += size
    shrink_rows = chosen[10].shape[0]
    own_shrink = tail_own[:shrink_rows]
    own_expand = jnp.concatenate(
        [cut(tail_own, shrink_rows + at * piece_rows, piece_rows) for at in range(ff // width)], axis=1
    )
    own = [
        own_small[0], own_small[1], own_triple, own_small[2], own_merge, own_small[3],
        own_small[4], own_small[5], own_expand, own_small[6], own_shrink, own_small[7],
    ]
    shape = (length, count, width)
    return (output.reshape(shape), input_grad.reshape(shape)) + tuple(
        place(grad, master, tie_slots[number]) for number, (grad, master) in enumerate(zip(own, masters))
    )


def solution(mesh):
    in_specs = (
        P("seq", "dp", None),
        P("seq", "dp", None),
        P(),
        P(None, "dp"),
        P(None, "dp"),
        P(None, "dp", None),
        P(None, "dp"),
        P(None, "dp", None),
        P(None, "dp"),
        P(None, "dp"),
        P(None, "dp"),
        P(None, "dp", None),
        P(None, "dp"),
        P(None, "dp", None),
        P(None, "dp"),
    )
    out_specs = (
        P("seq", "dp", None),
        P("seq", "dp", None),
        P(None, "dp"),
        P(None, "dp"),
        P(None, "dp", None),
        P(None, "dp"),
        P(None, "dp", None),
        P(None, "dp"),
        P(None, "dp"),
        P(None, "dp"),
        P(None, "dp", None),
        P(None, "dp"),
        P(None, "dp", None),
        P(None, "dp"),
    )
    sizes = dict(mesh.shape)
    body = per_device_fast if (sizes["dp"], sizes["seq"]) == (16, 2) else per_device
    return jax.shard_map(
        body, mesh=mesh, in_specs=in_specs, out_specs=out_specs, check_vma=False
    )
```

```python
import functools
import math

import jax
import jax.numpy as jnp
from jax import lax
from jax.experimental import pallas as pl
from jax.experimental.pallas import tpu as pltpu
from jax.sharding import PartitionSpec as P

H = 12
GROUPS = 16
SMALL = (0, 1, 3, 5, 6, 7, 9, 11)
EPSILON = 1e-05
NEGATIVE = -1e30
F32 = jnp.float32
BF16 = jnp.bfloat16
MEGA = 1024 * 1024
VMEM = {"pack": 60, "qkv": 28, "merge": 14, "ffn": 36, "close": 26, "unpack": 36}


def layer_norm(values, gain, shift):
    average = jnp.mean(values, axis=-1, keepdims=True)
    centered = values - average
    variance = jnp.mean(centered * centered, axis=-1, keepdims=True)
    return centered * lax.rsqrt(variance + EPSILON) * gain + shift


def dot(left, right, left_dim, right_dim):
    return lax.dot_general(
        left, right, (((left_dim,), (right_dim,)), ((), ())), preferred_element_type=F32
    )


def pair_masks():
    lane = lax.broadcasted_iota(jnp.int32, (1, 128), 1)
    low = (lane < 64).astype(F32)
    return low, 1.0 - low


def causal(scores, block):
    key = lax.broadcasted_iota(jnp.int32, (block, block), 0)
    query = lax.broadcasted_iota(jnp.int32, (block, block), 1)
    return jnp.where(key <= query, scores, NEGATIVE)


def attend_kernel(count, q_ref, k_ref, v_ref, rk_ref, rv_ref, o_ref, lse_ref, *, block):
    rows = q_ref.shape[0]
    masks = pair_masks()
    for index in range(rows // block):
        here = slice(index * block, (index + 1) * block)
        size = (index + 1) * block
        state = []
        parts = []
        for head in range(2):
            query = q_ref[here, :] * (masks[head] * 0.125).astype(BF16)
            parts.append(query)
            scores = dot(k_ref[0:size, :], query, 1, 1)
            last = causal(scores[size - block :], block)
            top = jnp.max(last, axis=0, keepdims=True)
            if index:
                scores = jnp.concatenate([scores[: size - block], last], axis=0)
                top = jnp.max(scores, axis=0, keepdims=True)
            else:
                scores = last
            lifted = jnp.exp(scores - top)
            total = jnp.sum(lifted, axis=0, keepdims=True)
            state += [top, total, dot(v_ref[0:size, :], lifted.astype(BF16), 0, 0)]

        def far(step, state):
            start = pl.multiple_of(step * rows, rows)
            keys = rk_ref[pl.ds(start, rows), :]
            values = rv_ref[pl.ds(start, rows), :]
            result = []
            for head in range(2):
                top, total, gathered = state[3 * head : 3 * head + 3]
                scores = dot(keys, parts[head], 1, 1)
                new_top = jnp.maximum(top, jnp.max(scores, axis=0, keepdims=True))
                factor = jnp.exp(top - new_top)
                lifted = jnp.exp(scores - new_top)
                total = total * factor + jnp.sum(lifted, axis=0, keepdims=True)
                gathered = gathered * factor + dot(values, lifted.astype(BF16), 0, 0)
                result += [new_top, total, gathered]
            return tuple(result)

        top0, total0, sum0, top1, total1, sum1 = lax.fori_loop(0, count[0], far, tuple(state))
        joined = jnp.concatenate([sum0[:64] / total0, sum1[64:] / total1], axis=0)
        o_ref[here, :] = jnp.transpose(joined).astype(BF16)
        lse_ref[0, 0:1, here] = top0 + jnp.log(total0)
        lse_ref[0, 1:2, here] = top1 + jnp.log(total1)


def attend(count, queries, near, remote, block, first=0, pairs=None):
    rows, width = queries.shape
    total = width // 128
    pairs = pairs or total
    far_rows = remote.shape[0]
    column = lambda size, offset: pl.BlockSpec((size, 128), lambda h, c: (0, h + offset))
    return pl.pallas_call(
        functools.partial(attend_kernel, block=block),
        grid_spec=pltpu.PrefetchScalarGridSpec(
            num_scalar_prefetch=1,
            grid=(pairs,),
            in_specs=[
                column(rows, first),
                column(rows, first),
                column(rows, first + total),
                column(far_rows, first),
                column(far_rows, first + total),
            ],
            out_specs=[column(rows, 0), pl.BlockSpec((1, 2, rows), lambda h, c: (h, 0, 0))],
        ),
        out_shape=[
            jax.ShapeDtypeStruct((rows, pairs * 128), BF16),
            jax.ShapeDtypeStruct((pairs, 2, rows), F32),
        ],
        compiler_params=pltpu.CompilerParams(vmem_limit_bytes=16 * MEGA),
        cost_estimate=pl.CostEstimate(
            flops=rows * rows * pairs * 100 // 1, bytes_accessed=rows * pairs * 150 // 1, transcendentals=0
        ),
        name="attend",
    )(count, queries, near, near, remote, remote)


def attend_back_kernel(
    count, q_ref, k_ref, v_ref, rk_ref, rv_ref, do_ref, o_ref, lse_ref,
    dq_ref, dk_ref, dv_ref, rdk_ref, rdv_ref, dq_sum, dk_sum, dv_sum, *, block,
):
    rows = q_ref.shape[0]
    far_rows = rk_ref.shape[0]
    masks = pair_masks()
    blocks = rows // block

    def prepare(index):
        here = slice(index * block, (index + 1) * block)
        out_grad = do_ref[here, :]
        product = jnp.transpose(out_grad.astype(F32) * o_ref[here, :].astype(F32))
        result = []
        for head in range(2):
            query = q_ref[here, :] * (masks[head] * 0.125).astype(BF16)
            masked = out_grad * masks[head].astype(BF16)
            delta = jnp.sum(product[64 * head : 64 * head + 64], axis=0, keepdims=True)
            lse = lse_ref[0, head : head + 1, here]
            result.append((query, masked, delta, lse))
        return result

    def terms(ready, keys, values, diagonal):
        key_grad = value_grad = query_grad = 0.0
        for head in range(2):
            query, masked, delta, lse = ready[head]
            scores = dot(keys, query, 1, 1)
            if diagonal:
                size = scores.shape[0]
                last = causal(scores[size - block :], block)
                if size > block:
                    scores = jnp.concatenate([scores[: size - block], last], axis=0)
                else:
                    scores = last
            probs = jnp.exp(scores - lse)
            prob_grad = dot(values, masked, 1, 1)
            score_grad = (probs * (prob_grad - delta)).astype(BF16)
            value_grad += dot(probs.astype(BF16), masked, 1, 0)
            key_grad += dot(score_grad, query, 1, 0)
            part = keys * (masks[head] * 0.125).astype(BF16)
            query_grad += dot(part, score_grad, 0, 0)
        return key_grad, value_grad, query_grad

    for index in reversed(range(blocks)):
        here = slice(index * block, (index + 1) * block)
        size = (index + 1) * block
        key_grad, value_grad, query_grad = terms(
            prepare(index), k_ref[0:size, :], v_ref[0:size, :], True
        )
        if index == blocks - 1:
            dk_sum[...] = key_grad
            dv_sum[...] = value_grad
        else:
            dk_sum[0:size, :] += key_grad
            dv_sum[0:size, :] += value_grad
        dq_sum[:, here] = query_grad

    def far(step, unused):
        start = pl.multiple_of(step * rows, rows)
        spot = pl.ds(start, rows)
        keys = rk_ref[spot, :]
        values = rv_ref[spot, :]
        key_total = value_total = 0.0
        for index in range(blocks):
            here = slice(index * block, (index + 1) * block)
            key_grad, value_grad, query_grad = terms(prepare(index), keys, values, False)
            key_total += key_grad
            value_total += value_grad
            dq_sum[:, here] += query_grad
        rdk_ref[spot, :] = key_total.astype(BF16)
        rdv_ref[spot, :] = value_total.astype(BF16)
        return unused

    lax.fori_loop(0, count[0], far, 0)

    def clear(step, unused):
        spot = pl.ds(pl.multiple_of(step * rows, rows), rows)
        rdk_ref[spot, :] = jnp.zeros((rows, 128), BF16)
        rdv_ref[spot, :] = jnp.zeros((rows, 128), BF16)
        return unused

    lax.fori_loop(count[0], far_rows // rows, clear, 0)
    dq_ref[...] = jnp.transpose(dq_sum[...]).astype(BF16)
    dk_ref[...] = dk_sum[...]
    dv_ref[...] = dv_sum[...]


def attend_back(count, queries, near, remote, out_grad, attended, lse, block, first=0):
    rows, width = attended.shape
    pairs, total = width // 128, queries.shape[1] // 128
    far_rows = remote.shape[0]
    column = lambda size, offset: pl.BlockSpec((size, 128), lambda h, c: (0, h + offset))
    return pl.pallas_call(
        functools.partial(attend_back_kernel, block=block),
        grid_spec=pltpu.PrefetchScalarGridSpec(
            num_scalar_prefetch=1,
            grid=(pairs,),
            in_specs=[
                column(rows, first),
                column(rows, first),
                column(rows, first + total),
                column(far_rows, first),
                column(far_rows, first + total),
                column(rows, first),
                column(rows, 0),
                pl.BlockSpec((1, 2, rows), lambda h, c: (h, 0, 0)),
            ],
            out_specs=[
                column(rows, 0),
                column(rows, 0),
                column(rows, 0),
                column(far_rows, 0),
                column(far_rows, 0),
            ],
            scratch_shapes=[
                pltpu.VMEM((128, rows), F32),
                pltpu.VMEM((rows, 128), F32),
                pltpu.VMEM((rows, 128), F32),
            ],
        ),
        out_shape=[
            jax.ShapeDtypeStruct((rows, width), BF16),
            jax.ShapeDtypeStruct((rows, width), F32),
            jax.ShapeDtypeStruct((rows, width), F32),
            jax.ShapeDtypeStruct((far_rows, width), BF16),
            jax.ShapeDtypeStruct((far_rows, width), BF16),
        ],
        compiler_params=pltpu.CompilerParams(vmem_limit_bytes=16 * MEGA),
        cost_estimate=pl.CostEstimate(
            flops=2 * rows * rows * width // 1, bytes_accessed=rows * width * 3 // 1, transcendentals=0
        ),
        name="attend_back",
    )(count, queries, near, near, remote, remote, out_grad, attended, lse)


def pairs_of(count, target):
    return [(index, target(index)) for index in range(count)]


def swap_cores(value, count):
    return lax.ppermute(value, "dp", pairs_of(count, lambda index: index ^ 1))


def swap_seq(value):
    return lax.ppermute(value, "seq", [(0, 1), (1, 0)])


def exchange_rows(value, dp=16):
    pairs = []
    for index in range(0, dp, 2):
        left, right = (index + 1) * 2, index * 2 + 1
        pairs += [(left, right), (right, left)]
    return lax.ppermute(value, ("dp", "seq"), pairs)


def regroup(value, dp, moves):
    return jnp.where(moves, exchange_rows(value, dp), value)


def turn_rows(value, back):
    pairs = []
    for first in range(0, 32, 4):
        steps = [(0, 2), (2, 3), (3, 1), (1, 0)]
        pairs += [(first + b, first + a) if back else (first + a, first + b) for a, b in steps]
    return lax.ppermute(value, ("dp", "seq"), pairs)


def deal(value, turn, cross, core, moves):
    size = value.shape[0] // 2
    first, second = value[:size], value[size:]
    base = jnp.where(moves, cross(first), first)
    came = turn(second)
    lead = core == 0
    return jnp.concatenate([jnp.where(lead, base, came), jnp.where(lead, came, base)], axis=0)


def undeal(value, turn, cross, core, moves):
    size = value.shape[0] // 2
    low, high = value[:size], value[size:]
    lead = core == 0
    base = jnp.where(lead, low, high)
    came = turn(jnp.where(lead, high, low))
    return jnp.concatenate([jnp.where(moves, cross(base), base), came], axis=0)


def split_columns(value, width):
    return [value[:, at : at + width] for at in range(0, value.shape[1], width)]


def gather_pack(blocks, dp):
    sizes = [block.shape[0] for block in blocks]
    packed = lax.all_gather(jnp.concatenate(blocks, axis=0), "dp", axis=0)
    if dp == GROUPS:
        return packed
    parts, at = [], 0
    for size in sizes:
        part = packed[:, at : at + size]
        parts.append(part.reshape(GROUPS, -1, part.shape[2]))
        at += size
    return jnp.concatenate(parts, axis=1)


def scatter_pack(packed, sizes, dp):
    if dp != GROUPS:
        parts, at = [], 0
        for size in sizes:
            whole = size * dp // GROUPS
            part = packed[:, at : at + whole]
            parts.append(part.reshape(dp, size, part.shape[2]))
            at += whole
        packed = jnp.concatenate(parts, axis=1)
    return lax.psum_scatter(packed, "dp", scatter_dimension=0)


def sum_seq(value, sequence_parts):
    if sequence_parts == 2:
        return value.astype(F32) + swap_seq(value).astype(F32)
    return lax.psum(value, "seq").astype(F32)


def place(grad, master, slot):
    marker = (jnp.arange(master.shape[0]) == slot).astype(F32)
    return marker.reshape((-1,) + (1,) * grad.ndim) * grad[None]


def spot(place):
    index = place[0]
    return index >> 2, (index >> 1) & 1, index & 1, place[1]


def whole(shape):
    return pl.BlockSpec(shape, lambda *unused: (0,) * len(shape))


ANYWHERE = pl.BlockSpec(memory_space=pl.ANY)


def kernel_call(body, scalars, in_specs, args, out_specs, out_shape, scratch, name, flops, moved):
    return pl.pallas_call(
        body,
        grid_spec=pltpu.PrefetchScalarGridSpec(
            num_scalar_prefetch=len(scalars),
            grid=(1,),
            in_specs=in_specs,
            out_specs=out_specs,
            scratch_shapes=scratch,
        ),
        out_shape=out_shape,
        compiler_params=pltpu.CompilerParams(vmem_limit_bytes=VMEM[name] * MEGA),
        cost_estimate=pl.CostEstimate(flops=flops // 2, bytes_accessed=moved // 2, transcendentals=0),
        name=name,
    )(*scalars, *args)


def pack_kernel(slots, place, *refs):
    masters, (head, tail, lines) = refs[:12], refs[12:]
    part, width = masters[4].shape
    lines[...] = jnp.zeros_like(lines)
    for row, number in enumerate(SMALL):
        master = masters[number]
        lines[row : row + 1, 0 : master.shape[1]] = master[pl.ds(slots[number], 1), :]
    for at in range(3):
        head[at * part : (at + 1) * part, :] = masters[2][:, at * width : (at + 1) * width].astype(BF16)
    head[3 * part : 4 * part, :] = masters[4][...].astype(BF16)
    head[4 * part :, :] = lines[...].astype(BF16)

    @pl.when(place[1] == 0)
    def shrink():
        tail[...] = masters[10][...].astype(BF16)

    @pl.when(place[1] != 0)
    def expand():
        for at in range(masters[8].shape[1] // width):
            tail[at * part : (at + 1) * part, :] = masters[8][:, at * width : (at + 1) * width].astype(BF16)


def pack(slots, place, masters):
    specs = []
    for number, master in enumerate(masters):
        if master.ndim == 2:
            specs.append(whole(master.shape))
        else:
            specs.append(
                pl.BlockSpec(
                    (None,) + master.shape[1:],
                    functools.partial(lambda step, slots, place, number: (slots[number], 0, 0), number=number),
                )
            )
    part, width = masters[4].shape[1:]
    rows = 4 * part + 16
    tail_rows = masters[10].shape[1]
    return kernel_call(
        pack_kernel, (slots, place), specs, masters,
        [whole((rows, width)), whole((tail_rows, width))],
        [jax.ShapeDtypeStruct((rows, width), BF16), jax.ShapeDtypeStruct((tail_rows, width), BF16)],
        [pltpu.VMEM((16, width), F32)], "pack", 0, 4 * rows * width * 6,
    )


def shift_z(value):
    return lax.ppermute(value, "dp", pairs_of(16, lambda index: (index + 4) % 16))


def swap_x(value):
    return lax.ppermute(value, "dp", pairs_of(16, lambda index: index ^ 2))


def after(value, *earlier):
    return lax.optimization_barrier((value,) + earlier)[0]


class Lane:
    def __init__(self, move, depth=2):
        self.move, self.depth, self.sent = move, depth, []

    def __call__(self, value, move=None):
        if len(self.sent) >= self.depth:
            value = after(value, self.sent[-self.depth])
        self.sent.append((move or self.move)(value))
        return self.sent[-1]


def ring_slots(z, x):
    slots = []
    for step in range(4):
        base = ((z - step) & 3) * 4
        slots += [base + x * 2, base + (1 - x) * 2]
    return slots


def gather(head, tail, values, out_grad, core, moves):
    z, x, y = Lane(shift_z, 2), Lane(swap_x, 1), Lane(swap_seq, 2)
    head, tail = [head], [tail]
    head_x, tail_x, tail_y, tail_xy = [], [], [], []
    head.append(z(head[0]))
    head_x.append(x(head[0]))
    tail_y.append(y(tail[0]))
    head.append(z(head[1]))
    tail_x.append(x(tail[0]))
    turn = lambda value: y(value, functools.partial(turn_rows, back=False))
    cross = lambda value: y(value, exchange_rows)
    values = deal(values, turn, cross, core, moves)
    tail.append(z(tail[0]))
    head_x.append(x(head[1]))
    out_grad = deal(out_grad, turn, cross, core, moves)
    head.append(z(head[2]))
    head_x.append(x(head[2]))
    tail_xy.append(y(tail_x[0]))
    tail.append(z(tail[1]))
    head_x.append(x(head[3]))
    tail_y.append(y(tail[1]))
    tail_x.append(x(tail[1]))
    values = after(values, tail_xy[0], tail[2], tail_x[1])
    tail.append(z(tail[2]))
    tail_xy.append(y(tail_x[1]))
    tail_x.append(x(tail[2]))
    tail_y.append(y(tail[2]))
    tail_x.append(x(tail[3]))
    mix = lambda first, second: [piece for pair in zip(first, second) for piece in pair]

    def rest(first, second):
        tail_xy.append(y(after(tail_x[2], first)))
        tail_y.append(y(after(tail[3], first)))
        tail_xy.append(y(after(tail_x[3], second)))
        return mix(tail_y, tail_xy), out_grad

    return mix(head, head_x), mix(tail, tail_x), values, rest


def row_sum(value):
    return jnp.sum(value, axis=0, keepdims=True)


def normalise(values):
    average = jnp.mean(values, axis=-1, keepdims=True)
    centered = values - average
    scale = lax.rsqrt(jnp.mean(centered * centered, axis=-1, keepdims=True) + EPSILON)
    return centered * scale, scale


def norm_back(grad, gain, shape, scale):
    inner = grad * gain
    first = jnp.mean(inner, axis=-1, keepdims=True)
    second = jnp.mean(inner * shape, axis=-1, keepdims=True)
    return scale * (inner - first - shape * second)


def balanced_kernel(extra, q_ref, k_ref, v_ref, rk_ref, rv_ref, o_ref, lse_ref, *, block):
    masks = pair_masks()
    index = extra[0]
    first = (index == 0).astype(F32)
    spot = pl.ds(pl.multiple_of(index * block, block), block)
    keys = jnp.concatenate([k_ref[0:block, :], rk_ref[0:block, :], k_ref[block:, :]], axis=0)
    values = jnp.concatenate([v_ref[0:block, :], rv_ref[0:block, :], v_ref[block:, :]], axis=0)
    sums, totals = [[], []], [[], []]
    for head in range(2):
        mask = (masks[head] * 0.125).astype(BF16)
        long = dot(keys, q_ref[block:, :] * mask, 1, 1)
        last = causal(long[2 * block :], block)
        long = long[: 2 * block]
        short = causal(dot(keys[0:block], q_ref[0:block, :] * mask, 1, 1), block)
        more = dot(rk_ref[spot, :], q_ref[spot, :] * mask, 1, 1)
        peak = lambda value: jnp.max(value, axis=0, keepdims=True)
        top_more = peak(more)
        top_short = peak(short)
        top_long = jnp.maximum(peak(long), peak(last))
        joined_short = jnp.maximum(top_short, top_more)
        joined_long = jnp.maximum(top_long, top_more)
        at_first = index == 0
        top_short = jnp.where(at_first, joined_short, top_short)
        top_long = jnp.where(at_first, top_long, joined_long)
        more = jnp.exp(more - jnp.where(at_first, top_short, top_long))
        short = jnp.exp(short - top_short)
        long = jnp.exp(long - top_long)
        last = jnp.exp(last - top_long)
        more_total = row_sum(more)
        more_sum = dot(rv_ref[spot, :], more.astype(BF16), 0, 0)
        short_total = row_sum(short) + first * more_total
        long_total = row_sum(long) + row_sum(last) + (1.0 - first) * more_total
        long_low = jnp.concatenate([long.astype(BF16), last.astype(BF16)], axis=0)
        half = slice(64 * head, 64 * head + 64)
        sums[0].append((dot(values[0:block], short.astype(BF16), 0, 0) + first * more_sum)[half] / short_total)
        sums[1].append((dot(values, long_low, 0, 0) + (1.0 - first) * more_sum)[half] / long_total)
        lse_ref[0, head : head + 1, 0:block] = top_short + jnp.log(short_total)
        lse_ref[0, head : head + 1, block:] = top_long + jnp.log(long_total)
    for part in range(2):
        joined = jnp.concatenate(sums[part], axis=0)
        o_ref[part * block : (part + 1) * block, :] = jnp.transpose(joined).astype(BF16)


def balanced_back_kernel(
    extra, q_ref, k_ref, v_ref, rk_ref, rv_ref, do_ref, o_ref, lse_ref,
    dq_ref, dk_ref, dv_ref, rdk_ref, rdv_ref, *, block,
):
    masks = pair_masks()
    index = extra[0]
    first = (index == 0).astype(F32)
    spot = pl.ds(pl.multiple_of(index * block, block), block)
    keys = jnp.concatenate([k_ref[0:block, :], rk_ref[0:block, :], k_ref[block:, :]], axis=0)
    values = jnp.concatenate([v_ref[0:block, :], rv_ref[0:block, :], v_ref[block:, :]], axis=0)
    product = jnp.transpose(do_ref[...].astype(F32) * o_ref[...].astype(F32))
    key_grads, value_grads, query_grads = [0.0] * 3, [0.0] * 3, [0.0] * 3
    for head in range(2):
        mask = masks[head].astype(BF16)
        scaled = (masks[head] * 0.125).astype(BF16)
        delta = row_sum(product[64 * head : 64 * head + 64])
        lse = lse_ref[0, head : head + 1, :]
        pick = lambda row: jnp.where(index == 0, row[:, :block], row[:, block:])
        sets = (
            (slice(block, None), keys, values, lse[:, block:], delta[:, block:], 3),
            (slice(0, block), keys[0:block], values[0:block], lse[:, :block], delta[:, :block], 1),
            (spot, rk_ref[spot, :], rv_ref[spot, :], pick(lse), pick(delta), 0),
        )
        for at, (rows, near_keys, near_values, norm, shift, blocks) in enumerate(sets):
            query = q_ref[rows, :] * scaled
            grad = do_ref[rows, :] * mask
            scores = dot(near_keys, query, 1, 1)
            if blocks:
                last = causal(scores[(blocks - 1) * block :], block)
                scores = jnp.concatenate([scores[: (blocks - 1) * block], last], axis=0) if blocks > 1 else last
            probs = jnp.exp(scores - norm)
            score_grad = (probs * (dot(near_values, grad, 1, 1) - shift)).astype(BF16)
            value_grads[at] += dot(probs.astype(BF16), grad, 1, 0)
            key_grads[at] += dot(score_grad, query, 1, 0)
            query_grads[at] += dot(near_keys * scaled, score_grad, 0, 0)
    turned = jnp.concatenate([query_grads[1] + first * query_grads[2], query_grads[0] + (1.0 - first) * query_grads[2]], axis=1)
    dq_ref[...] = jnp.transpose(turned).astype(BF16)
    for out, far, grads in ((dk_ref, rdk_ref, key_grads), (dv_ref, rdv_ref, value_grads)):
        out[0:block, :] = (grads[0][0:block] + grads[1]).astype(BF16)
        out[block:, :] = grads[0][2 * block :].astype(BF16)
        far[0:block, :] = (grads[0][block : 2 * block] + first * grads[2]).astype(BF16)
        far[block:, :] = ((1.0 - first) * grads[2]).astype(BF16)


def balanced(extra, args, first, pairs, cost):
    queries = args[0]
    rows, width = queries.shape
    total = width // 128
    column = lambda offset: pl.BlockSpec((rows, 128), lambda h, c: (0, h + offset))
    line = pl.BlockSpec((1, 2, rows), lambda h, c: (h, 0, 0))
    half = jax.ShapeDtypeStruct((rows, pairs * 128), BF16)
    in_specs = [column(first), column(first), column(first + total), column(first), column(first + total)]
    operands = [queries, args[1], args[1], args[2], args[2]]
    if len(args) == 3:
        body, out_specs = balanced_kernel, [column(0), line]
        out_shape = [half, jax.ShapeDtypeStruct((pairs, 2, rows), F32)]
    else:
        body, out_specs, out_shape = balanced_back_kernel, [column(0)] * 5, [half] * 5
        in_specs += [column(first), column(0), line]
        operands += list(args[3:])
    return pl.pallas_call(
        functools.partial(body, block=rows // 2),
        grid_spec=pltpu.PrefetchScalarGridSpec(
            num_scalar_prefetch=1, grid=(pairs,), in_specs=in_specs, out_specs=out_specs
        ),
        out_shape=out_shape,
        compiler_params=pltpu.CompilerParams(vmem_limit_bytes=16 * MEGA),
        cost_estimate=pl.CostEstimate(flops=cost, bytes_accessed=cost // 1000, transcendentals=0),
        name="attend" if len(args) == 3 else "attend_back",
    )(extra, *operands)


def qkv_kernel(place, x_ref, *refs):
    pieces, (packed, n1_ref, q_ref, kv_ref, v48, v96, v192, sems) = refs[:16], refs[16:]
    z, x, core, half = spot(place)
    slots = ring_slots(z, x)
    slots = [slot + core for slot in slots] + [slot + 1 - core for slot in slots]
    copies = [
        pltpu.make_async_copy(piece, packed.at[slots[number]], sems.at[number])
        for number, piece in enumerate(pieces)
    ]
    for copy in copies:
        copy.start()
    width = x_ref.shape[1]
    part = width // GROUPS
    shape, unused = normalise(x_ref[...].astype(F32))
    for copy in copies:
        copy.wait()
    for group in range(GROUPS):
        lines = packed[group, 4 * part : 4 * part + 16, :].astype(F32)[0:8]
        for out in (v48, v96, v192):
            size = out.shape[1] // GROUPS
            out[:, group * size : (group + 1) * size] = lines[:, :size]
    normed = (shape * v48[0:1, :] + v48[1:2, :]).astype(BF16)
    n1_ref[...] = normed
    for at in range(3):
        weight = packed[:, at * part : (at + 1) * part, :].reshape(width, width)
        result = dot(normed, weight, 1, 0)
        if at == 0:
            q_ref[...] = (result + v96[2:3, :width]).astype(BF16)
        elif at == 1:
            kv_ref[:, :width] = result.astype(BF16)
        else:
            kv_ref[:, width:] = (result + v96[2:3, width:]).astype(BF16)


def qkv(place, values, pieces):
    rows, width = values.shape
    shapes = [
        ((GROUPS,) + pieces[0].shape, BF16), ((rows, width), BF16), ((rows, width), BF16), ((rows, 2 * width), BF16),
        ((8, width), F32), ((8, 2 * width), F32), ((8, 4 * width), F32),
    ]
    return kernel_call(
        qkv_kernel, (place,), [whole(values.shape)] + [ANYWHERE] * 16, [values] + pieces,
        [whole(shape) for shape, unused in shapes],
        [jax.ShapeDtypeStruct(shape, dtype) for shape, dtype in shapes],
        [pltpu.SemaphoreType.DMA((16,))], "qkv", 6 * rows * width * width, 20 * width * width,
    )


def merge_kernel(x_ref, o1_ref, o2_ref, weight, v48, m_ref, n2_ref):
    width = x_ref.shape[1]
    attended = jnp.concatenate([o1_ref[...], o2_ref[...]], axis=1)
    middle = x_ref[...].astype(F32) + dot(attended, weight[...].reshape(width, width), 1, 0) + v48[3:4, :]
    m_ref[...] = middle
    shape, unused = normalise(middle)
    n2_ref[...] = (shape * v48[4:5, :] + v48[5:6, :]).astype(BF16)


def merge_spec(packed):
    part = packed.shape[2] // GROUPS
    return pl.BlockSpec((GROUPS, part, packed.shape[2]), lambda *unused: (0, 3, 0))


def merge(values, attended, packed, v48):
    rows, width = values.shape
    return kernel_call(
        merge_kernel, (),
        [whole(values.shape)] + [whole(piece.shape) for piece in attended] + [merge_spec(packed), whole(v48.shape)],
        [values] + attended + [packed, v48], [whole(values.shape)] * 2,
        [jax.ShapeDtypeStruct((rows, width), F32), jax.ShapeDtypeStruct((rows, width), BF16)],
        [], "merge", 2 * rows * width * width, 12 * rows * width,
    )


def gelu_pair(value):
    scale, cubic = math.sqrt(2 / math.pi), 0.044715
    square = value * value
    bent = jnp.tanh(scale * value * (1.0 + cubic * square))
    half = 0.5 * (1.0 + bent)
    slope = half + 0.5 * value * (1.0 - bent * bent) * (scale * (1.0 + 3.0 * cubic * square))
    return value * half, slope


def ffn_kernel(place, *refs):
    pieces, refs = refs[:32], refs[32:]
    m_far, n2_ref, gy_ref, packed, v48, v192, out_ref, dm_ref, do_ref, g48, g192 = refs[:11]
    outs, (weights, grads, y, dn2, n2_t, u, df, m_ref, merge_weight, in_sems, out_sems, late_sems) = refs[11:19], refs[19:]
    z, x, core, half = spot(place)
    slots = ring_slots(z, x)
    spots = [(slot + core, half) for slot in slots] + [(slot + core, 1 - half) for slot in slots]
    spots += [(slot + 1 - core, half) for slot in slots] + [(slot + 1 - core, 1 - half) for slot in slots]
    copies = [
        pltpu.make_async_copy(piece, weights.at[spots[number][0], spots[number][1]], in_sems.at[number])
        for number, piece in enumerate(pieces)
    ]
    for copy in copies:
        copy.start()
    width = m_ref.shape[1]
    part = width // GROUPS
    late = [
        pltpu.make_async_copy(m_far, m_ref, late_sems.at[0]),
        pltpu.make_async_copy(packed.at[:, 3 * part : 4 * part, :], merge_weight, late_sems.at[1]),
    ]
    for copy in late:
        copy.start()
    n2_t[...] = jnp.transpose(n2_ref[...])
    y[...] = jnp.zeros_like(y)
    dn2[...] = jnp.zeros_like(dn2)
    for copy in copies:
        copy.wait()

    def step(at, unused):
        first = pl.multiple_of(at * 4, 4)
        lines = pl.ds(pl.multiple_of(at * part, 16), part)
        chunk = 256
        for column in range(0, width, chunk):
            place_in = pl.ds(pl.multiple_of(at * width + column, 128), chunk)
            expand = weights[:, 1, lines, column : column + chunk].reshape(width, chunk)
            hidden = dot(n2_ref[...], expand, 1, 0) + v192[6:7, place_in]
            shrink = weights[pl.ds(first, 4), 0].reshape(width, width)[column : column + chunk]
            active, slope = gelu_pair(hidden)
            u[:, column : column + chunk] = active.astype(BF16)
            hidden_grad = (dot(gy_ref[...], shrink, 1, 1) * slope).astype(BF16)
            df[:, column : column + chunk] = hidden_grad
            g192[0:1, place_in] = row_sum(hidden_grad.astype(F32))
        shrink = weights[pl.ds(first, 4), 0].reshape(width, width)
        expand = weights[:, 1, lines, :].reshape(width, width)
        y[...] += dot(u[...], shrink, 1, 0)
        dn2[...] += dot(df[...], expand, 1, 1)
        grads[pl.ds(first, 4), 0] = dot(u[...], gy_ref[...], 0, 0).astype(BF16).reshape(4, 4 * part, width)
        grads[:, 1, lines, :] = dot(n2_t[...], df[...], 1, 0).astype(BF16).reshape(GROUPS, part, width)
        return unused

    lax.fori_loop(0, 4, step, 0)
    copies = []
    for order in range(4):
        base = ((z - order) & 3) * 4
        for number, out in ((0, outs[2 * order]), (1, outs[2 * order + 1])):
            side = core if number == 0 else 1 - core
            for kind in range(2):
                for column in range(2):
                    source = base + (x if column == 0 else 1 - x) * 2 + side
                    copies.append(
                        pltpu.make_async_copy(
                            grads.at[source, half if kind == 0 else 1 - half],
                            out.at[column, kind],
                            out_sems.at[len(copies)],
                        )
                    )
    for copy in copies:
        copy.start()
    for copy in late:
        copy.wait()
    middle = m_ref[...]
    out_ref[...] = (middle + y[...] + v48[7:8, :]).astype(BF16)
    shape, scale = normalise(middle)
    second_grad = dn2[...]
    out_grad = gy_ref[...].astype(F32)
    middle_grad = out_grad + norm_back(second_grad, v48[4:5, :], shape, scale)
    dm_ref[...] = middle_grad
    low = middle_grad.astype(BF16)
    g48[...] = jnp.zeros_like(g48)
    g48[3:4, :] = row_sum(low.astype(F32))
    g48[4:5, :] = row_sum(shape * second_grad)
    g48[5:6, :] = row_sum(second_grad)
    g48[7:8, :] = row_sum(out_grad)
    do_ref[...] = dot(low, merge_weight[...].reshape(width, width), 1, 1).astype(BF16)
    for copy in copies:
        copy.wait()


def ffn(place, pieces, middle, second, out_grad, packed, v48, v192):
    rows, width = middle.shape
    ff = 4 * width
    tail_rows = pieces[0].shape[0]
    shapes = [
        ((rows, width), BF16), ((rows, width), F32), ((rows, width), BF16),
        ((8, width), F32), ((8, ff), F32),
    ]
    part = jax.ShapeDtypeStruct((2, 2, tail_rows, width), BF16)
    pack_shape = (GROUPS, 2, tail_rows, width)
    results = kernel_call(
        ffn_kernel, (place,),
        [ANYWHERE] * 32
        + [ANYWHERE, whole(second.shape), whole(out_grad.shape), ANYWHERE, whole(v48.shape), whole(v192.shape)],
        pieces + [middle, second, out_grad, packed, v48, v192],
        [whole(shape) for shape, unused in shapes] + [ANYWHERE] * 8,
        [jax.ShapeDtypeStruct(shape, dtype) for shape, dtype in shapes] + [part] * 8,
        [
            pltpu.VMEM(pack_shape, BF16), pltpu.VMEM(pack_shape, BF16),
            pltpu.VMEM((rows, width), F32), pltpu.VMEM((rows, width), F32), pltpu.VMEM((width, rows), BF16),
            pltpu.VMEM((rows, width), BF16), pltpu.VMEM((rows, width), BF16),
            pltpu.VMEM((rows, width), F32), pltpu.VMEM((GROUPS, width // GROUPS, width), BF16),
            pltpu.SemaphoreType.DMA((32,)), pltpu.SemaphoreType.DMA((32,)), pltpu.SemaphoreType.DMA((2,)),
        ],
        "ffn", 12 * rows * width * ff, 8 * width * ff,
    )
    return results[:5], results[5:]


def close_kernel(
    place, n1_ref, x_ref, q1, k1, v1, far_k1, far_v1, q2, k2, v2, far_k2, far_v2, o1, o2,
    dm_ref, packed, v48, g48_in, g192, *refs,
):
    join = lambda first, second: jnp.concatenate([first[...], second[...]], axis=1)
    grad_ref, outs, (grads, g48, g96, dt, sems) = refs[0], refs[1:9], refs[9:]
    z, x, core, half = spot(place)
    width = x_ref.shape[1]
    part = width // GROUPS
    normed_t = jnp.transpose(n1_ref[...])
    normed_grad = None
    for at in range(3):
        if at == 0:
            dt[...] = join(q1, q2)
        elif at == 1:
            dt[...] = (join(k1, k2).astype(F32) + join(far_k1, far_k2).astype(F32)).astype(BF16)
        else:
            dt[...] = (join(v1, v2).astype(F32) + join(far_v1, far_v2).astype(F32)).astype(BF16)
        if at != 1:
            g96[2:3, (at // 2) * width : (at // 2 + 1) * width] = row_sum(dt[...].astype(F32))
        weight = packed[:, at * part : (at + 1) * part, :].reshape(width, width)
        term = dot(dt[...], weight, 1, 1)
        normed_grad = term if normed_grad is None else normed_grad + term
        grads[:, at * part : (at + 1) * part, :] = dot(normed_t, dt[...], 1, 0).astype(BF16).reshape(GROUPS, part, width)
    grads[:, 3 * part : 4 * part, :] = dot(join(o1, o2), dm_ref[...].astype(BF16), 0, 0).astype(BF16).reshape(GROUPS, part, width)
    shape, scale = normalise(x_ref[...].astype(F32))
    g48[...] = g48_in[...]
    g48[0:1, :] = row_sum(shape * normed_grad)
    g48[1:2, :] = row_sum(normed_grad)
    row = lax.broadcasted_iota(jnp.int32, (16, 1), 0)
    for group in range(GROUPS):
        lines = jnp.concatenate([g48[:, group * part : (group + 1) * part], jnp.zeros((8, part), F32)], axis=0)
        grads[group, 4 * part :, :] = jnp.zeros((16, width), BF16)
        pair = g96[2:3, group * 2 * part : (group + 1) * 2 * part]
        wide = g192[0:1, group * 4 * part : (group + 1) * 4 * part]
        spread = jnp.where(row == 6, wide, 0.0)
        left = jnp.where(row == 2, pair, 0.0)
        grads[group, 4 * part :, 0 : 4 * part] = spread.astype(BF16)
        grads[group, 4 * part :, 0 : 2 * part] = (spread[:, : 2 * part] + left).astype(BF16)
        keep = jnp.where((row == 2) | (row == 6), 0.0, lines) + spread[:, :part] + left[:, :part]
        grads[group, 4 * part :, 0:part] = keep.astype(BF16)
    copies = []
    for order in range(4):
        base = ((z - order) & 3) * 4
        for number, out in ((0, outs[2 * order]), (1, outs[2 * order + 1])):
            side = core if number == 0 else 1 - core
            for column in range(2):
                source = base + (x if column == 0 else 1 - x) * 2 + side
                copies.append(pltpu.make_async_copy(grads.at[source], out.at[column], sems.at[len(copies)]))
    for copy in copies:
        copy.start()
    grad_ref[...] = (dm_ref[...] + norm_back(normed_grad, v48[0:1, :], shape, scale)).astype(BF16)
    for copy in copies:
        copy.wait()


def close(place, args):
    rows, width = args[0].shape
    packed = args[15]
    head_rows = packed.shape[1]
    part = jax.ShapeDtypeStruct((2, head_rows, width), BF16)
    results = kernel_call(
        close_kernel, (place,), [whole(arg.shape) for arg in args], args,
        [whole((rows, width))] + [ANYWHERE] * 8,
        [jax.ShapeDtypeStruct((rows, width), BF16)] + [part] * 8,
        [
            pltpu.VMEM(packed.shape, BF16), pltpu.VMEM((8, width), F32), pltpu.VMEM((8, 2 * width), F32),
            pltpu.VMEM((rows, width), BF16), pltpu.SemaphoreType.DMA((16,)),
        ],
        "close", 14 * rows * width * width, 20 * width * width,
    )
    return results[0], results[1:]


def unpack_kernel(slots, place, head, head_far, tail, tail_far, *outs):
    part, width = outs[4].shape[1:]
    total = head[...].astype(F32) + head_far[...].astype(F32)
    own = tail[0].astype(F32) + tail_far[1].astype(F32)
    other = tail[1].astype(F32) + tail_far[0].astype(F32)
    lead = place[1] == 0
    shrink, expand = jnp.where(lead, own, other), jnp.where(lead, other, own)
    for row, number in enumerate(SMALL):
        out = outs[number]
        size = out.shape[1]
        line = total[4 * part + row : 4 * part + row + 1, :size]
        row_at = lax.broadcasted_iota(jnp.int32, out.shape, 0)
        out[...] = jnp.where(row_at == slots[number], line, 0.0)
    for slot in range(outs[2].shape[0]):
        chosen = lambda number, value: jnp.where(slots[number] == slot, value, 0.0)
        for at in range(3):
            outs[2][slot, :, at * width : (at + 1) * width] = chosen(2, total[at * part : (at + 1) * part])
        outs[4][slot] = chosen(4, total[3 * part : 4 * part])
        for at in range(outs[8].shape[2] // width):
            outs[8][slot, :, at * width : (at + 1) * width] = chosen(8, expand[at * part : (at + 1) * part])
        outs[10][slot] = chosen(10, shrink)


def unpack(slots, place, parts, masters):
    return kernel_call(
        unpack_kernel, (slots, place), [whole(part.shape) for part in parts], parts,
        [whole(master.shape) for master in masters],
        [jax.ShapeDtypeStruct(master.shape, F32) for master in masters],
        [], "unpack", 0, 8 * 1024 * 1024,
    )


def per_device_fast(inputs, cotangent, tie_slots, *masters):
    length, count, width = inputs.shape
    index, half = lax.axis_index("dp"), lax.axis_index("seq")
    place = jnp.stack([index, half]).astype(jnp.int32)
    core = index % 2
    moves = core != half
    head, tail = pack(tie_slots, place, masters)
    head_pieces, tail_pieces, values, rest = gather(
        head, tail, inputs.reshape(length, width), cotangent.reshape(length, width), core, moves
    )
    head_pieces = head_pieces + [swap_cores(piece, 16) for piece in head_pieces]
    packed, normed, queries, near, v48, v96, v192 = qkv(place, values, head_pieces)
    remote = swap_cores(near, 16)
    extra = (1 - core).astype(jnp.int32).reshape(1)
    half_pairs = width // 256
    queries = after(queries, tail_pieces[6], tail_pieces[3])
    attended, lse = [None, None], [None, None]
    attended[0], lse[0] = balanced(extra, (queries, near, remote), 0, half_pairs, 1000000)
    queries = after(queries, attended[0])
    attended[1], lse[1] = balanced(extra, (queries, near, remote), half_pairs, half_pairs, 1000000)
    tail_other, out_grad = rest(attended[0], attended[1])
    middle, second = merge(values, attended, packed, v48)
    late = lambda pieces, first: [
        swap_cores(after(piece, attended[1]) if number >= first else piece, 16) for number, piece in enumerate(pieces)
    ]
    tail_pieces = tail_pieces + late(tail_pieces, 4)
    tail_other = tail_other + late(tail_other, 5)
    (output, middle_grad, attended_grad, g48, g192), tail_parts = ffn(
        place, tail_pieces[:8] + tail_other[:8] + tail_pieces[8:] + tail_other[8:],
        middle, second, out_grad, packed, v48, v192,
    )
    z, x, y = Lane(shift_z, 2), Lane(swap_x, 3), Lane(swap_seq, 2)
    turn = lambda value: y(value, functools.partial(turn_rows, back=True))
    cross = lambda value: y(value, exchange_rows)
    came = [swap_cores(send, 16) for send in tail_parts[1::2]]
    kept = [keep + other for keep, other in zip(tail_parts[0::2], came)]
    tail_half, tail_part, head_part = {}, {}, {}
    attended_grad = after(attended_grad, *kept)
    tail_half[1] = kept[1][1, 0] + y(kept[1][1, 1])
    tail_half[2] = kept[2][1, 0] + y(kept[2][1, 1])
    tail_half[3] = kept[3][1, 0] + y(kept[3][1, 1])
    tail_half[0] = kept[0][1, 0] + y(kept[0][1, 1])
    grads = []
    for part in range(2):
        if part:
            attended_grad = after(attended_grad, grads[0], tail_half[1])
        query_grad, key_grad, value_grad, far_key, far_value = balanced(
            extra, (queries, near, remote, attended_grad, attended[part], lse[part]), part * half_pairs, half_pairs, 1000000
        )
        grads += [query_grad, key_grad, value_grad, swap_cores(far_key, 16), swap_cores(far_value, 16)]
    tail_part[1] = jnp.stack([kept[1][0, 0] + x(tail_half[1]), kept[1][0, 1]])
    tail_run = tail_run1 = z(tail_part[1])
    tail_part[2] = jnp.stack([kept[2][0, 0] + x(tail_half[2]), kept[2][0, 1]])
    tail_run = tail_run2 = z(tail_part[2] + tail_run)
    middle_grad = after(middle_grad, tail_run1)
    input_grad, head_parts = close(
        place,
        [
            normed, values, *grads, *attended, middle_grad, packed, v48, g48, g192,
        ],
    )
    came = [swap_cores(send, 16) for send in head_parts[1::2]]
    head_kept = [keep + other for keep, other in zip(head_parts[0::2], came)]
    output = undeal(output, turn, cross, core, moves)
    input_grad = undeal(input_grad, turn, cross, core, moves)
    head_part[1] = head_kept[1][0] + x(head_kept[1][1])
    head_run = head_run1 = z(head_part[1])
    tail_part[3] = jnp.stack([kept[3][0, 0] + x(tail_half[3]), kept[3][0, 1]])
    tail_run = tail_run3 = z(tail_part[3] + tail_run)
    head_part[2] = head_kept[2][0] + x(head_kept[2][1])
    head_run = head_run2 = z(head_part[2] + head_run)
    tail_part[0] = jnp.stack([kept[0][0, 0] + x(tail_half[0]), kept[0][0, 1]])
    tail_sum = tail_part[0] + tail_run
    head_part[3] = head_kept[3][0] + x(head_kept[3][1])
    head_run = head_run3 = z(head_part[3] + head_run)
    head_part[0] = head_kept[0][0] + x(head_kept[0][1])
    head_sum = head_part[0] + head_run
    input_grad = input_grad.astype(F32)
    grads = unpack(
        tie_slots, place, [head_sum, y(head_sum), tail_sum, y(tail_sum)], masters
    )
    shape = (length, count, width)
    return (output.reshape(shape), input_grad.reshape(shape)) + tuple(grads)


def per_device(
    inputs,
    cotangent,
    tie_slots,
    *masters,
):
    dp, sequence_parts = lax.axis_size("dp"), lax.axis_size("seq")
    length, count, width = inputs.shape
    rows = length * count
    block = math.gcd(length, 256)
    moved = sequence_parts == 2 and dp % 2 == 0
    core = lax.axis_index("dp") % 2
    moves = core != lax.axis_index("seq")
    place_index = core if moved else lax.axis_index("seq")
    chosen = [
        lax.dynamic_index_in_dim(masters[number], tie_slots[number], 0, keepdims=False).astype(BF16)
        for number in range(12)
    ]
    part = width // dp
    ff = masters[10].shape[1] * dp
    small = jnp.concatenate([chosen[number] for number in SMALL])
    widths = [chosen[number].shape[0] for number in SMALL]
    pad = 16 * GROUPS // dp
    small = jnp.pad(small.reshape(1, -1), ((0, pad - 1), (0, width - small.shape[0])))
    head_blocks = split_columns(chosen[2], width) + [chosen[4], small]
    tail_blocks = [chosen[10]] + split_columns(chosen[8], width)
    head_sizes = [piece.shape[0] for piece in head_blocks]
    tail_sizes = [piece.shape[0] for piece in tail_blocks]
    head_pack = gather_pack(head_blocks, dp)
    flat_in = inputs.reshape(rows, width)
    flat_cot = cotangent.reshape(rows, width)
    if moved:
        flat_in = regroup(flat_in, dp, moves)
        flat_cot = regroup(flat_cot, dp, moves)
    tail_pack = gather_pack(tail_blocks, dp)

    group_rows = width // GROUPS
    matrix = lambda pack, at: pack[:, at * group_rows : (at + 1) * group_rows].reshape(width, width)
    triple_weight = jnp.concatenate([matrix(head_pack, at) for at in range(3)], axis=1)
    merge_weight = matrix(head_pack, 3)
    per_group = GROUPS // dp if dp < GROUPS else dp // GROUPS
    lines = head_pack[:, 4 * group_rows :].reshape(dp, pad, width)[:, 0]
    vectors, at = [], 0
    for size in widths:
        vectors.append(lines[:, at : at + size].reshape(-1).astype(F32))
        at += size
    gain_one, shift_one, pair_bias, merge_bias, gain_two, shift_two, expand_bias, shrink_bias = vectors

    flat_in = flat_in.astype(F32)
    normed, norm_one_pull = jax.vjp(layer_norm, flat_in, gain_one, shift_one)
    normed_low = normed.astype(BF16)
    bias_full = jnp.concatenate([pair_bias[:width], jnp.zeros((width,), F32), pair_bias[width:]])
    triple = (jnp.dot(normed_low, triple_weight, preferred_element_type=F32) + bias_full).astype(BF16)
    queries, near = triple[:, :width], triple[:, width:]
    if moved:
        remote = swap_cores(near, dp)
    else:
        remote = lax.all_gather(near, "seq", axis=0, tiled=True)
    far_count = place_index.astype(jnp.int32).reshape(1)
    attended_low, lse = attend(far_count, queries, near, remote, block)
    middle = flat_in + jnp.dot(attended_low, merge_weight, preferred_element_type=F32) + merge_bias

    ff_rows = ff // GROUPS
    shrink_weight = tail_pack[:, :ff_rows].reshape(ff, width)
    expand_weight = jnp.concatenate(
        [
            tail_pack[:, ff_rows + at * group_rows : ff_rows + (at + 1) * group_rows].reshape(width, width)
            for at in range(ff // width)
        ],
        axis=1,
    )
    second, norm_two_pull = jax.vjp(layer_norm, middle, gain_two, shift_two)
    second_low = second.astype(BF16)
    hidden = jnp.dot(second_low, expand_weight, preferred_element_type=F32) + expand_bias
    active, gelu_pull = jax.vjp(lambda values: jax.nn.gelu(values, approximate=True), hidden)
    active_low = active.astype(BF16)
    result = middle + jnp.dot(active_low, shrink_weight, preferred_element_type=F32) + shrink_bias
    output = result.astype(BF16)
    if moved:
        output = regroup(output, dp, moves)
    grad_shrink_weight = dot(active_low, flat_cot, 0, 0)
    grad_shrink_bias = jnp.sum(flat_cot.astype(F32), axis=0)
    active_grad = dot(flat_cot, shrink_weight, 1, 1)
    hidden_grad = gelu_pull(active_grad)[0].astype(BF16)
    grad_expand_weight = dot(second_low, hidden_grad, 0, 0)
    grad_expand_bias = jnp.sum(hidden_grad.astype(F32), axis=0)
    second_grad = dot(hidden_grad, expand_weight, 1, 1)
    middle_part, grad_gain_two, grad_shift_two = norm_two_pull(second_grad)
    middle_grad = flat_cot.astype(F32) + middle_part
    grouped = lambda value: value.astype(BF16).reshape(GROUPS, -1, width)
    tail_grads = jnp.concatenate(
        [grouped(grad_shrink_weight)] + [grouped(piece) for piece in split_columns(grad_expand_weight, width)],
        axis=1,
    )
    tail_own = sum_seq(scatter_pack(tail_grads, tail_sizes, dp), sequence_parts)

    branch_grad = middle_grad.astype(BF16)
    grad_merge_weight = dot(attended_low, branch_grad, 0, 0)
    grad_merge_bias = jnp.sum(branch_grad.astype(F32), axis=0)
    attended_grad = dot(branch_grad, merge_weight, 1, 1).astype(BF16)
    query_grad, key_grad, value_grad, far_key, far_value = attend_back(
        far_count, queries, near, remote, attended_grad, attended_low, lse, block
    )
    far_grad = jnp.concatenate([far_key, far_value], axis=1)
    pair_grad = jnp.concatenate([key_grad, value_grad], axis=1)
    if moved:
        pair_grad = pair_grad + swap_cores(far_grad, dp).astype(F32)
    else:
        pair_grad = pair_grad + lax.psum_scatter(far_grad, "seq", scatter_dimension=0, tiled=True).astype(F32)
    triple_grad = jnp.concatenate([query_grad, pair_grad.astype(BF16)], axis=1)
    grad_triple_weight = dot(normed_low, triple_grad, 0, 0)
    column_sums = jnp.sum(triple_grad.astype(F32), axis=0)
    grad_pair_bias = jnp.concatenate([column_sums[:width], column_sums[2 * width :]])
    normed_grad = dot(triple_grad, triple_weight, 1, 1)
    input_part, grad_gain_one, grad_shift_one = norm_one_pull(normed_grad)
    input_grad = middle_grad + input_part
    if moved:
        input_grad = regroup(input_grad, dp, moves)
    small_grads = [
        grad_gain_one, grad_shift_one, grad_pair_bias, grad_merge_bias,
        grad_gain_two, grad_shift_two, grad_expand_bias, grad_shrink_bias,
    ]
    lines = jnp.concatenate([piece.reshape(dp, -1) for piece in small_grads], axis=1).astype(BF16)
    lines = jnp.pad(lines[:, None], ((0, 0), (0, pad - 1), (0, width - lines.shape[1])))
    head_grads = jnp.concatenate(
        [grouped(piece) for piece in split_columns(grad_triple_weight, width)]
        + [grouped(grad_merge_weight), lines.reshape(GROUPS, -1, width)],
        axis=1,
    )
    head_own = sum_seq(scatter_pack(head_grads, head_sizes, dp), sequence_parts)

    piece_rows = chosen[4].shape[0]
    cut = lambda pack, at, size: pack[at : at + size]
    own_triple = jnp.concatenate([cut(head_own, at * piece_rows, piece_rows) for at in range(3)], axis=1)
    own_merge = cut(head_own, 3 * piece_rows, piece_rows)
    own_small, at = [], 0
    for size in widths:
        own_small.append(head_own[4 * piece_rows, at : at + size])
        at += size
    shrink_rows = chosen[10].shape[0]
    own_shrink = tail_own[:shrink_rows]
    own_expand = jnp.concatenate(
        [cut(tail_own, shrink_rows + at * piece_rows, piece_rows) for at in range(ff // width)], axis=1
    )
    own = [
        own_small[0], own_small[1], own_triple, own_small[2], own_merge, own_small[3],
        own_small[4], own_small[5], own_expand, own_small[6], own_shrink, own_small[7],
    ]
    shape = (length, count, width)
    return (output.reshape(shape), input_grad.reshape(shape)) + tuple(
        place(grad, master, tie_slots[number]) for number, (grad, master) in enumerate(zip(own, masters))
    )


def solution(mesh):
    in_specs = (
        P("seq", "dp", None),
        P("seq", "dp", None),
        P(),
        P(None, "dp"),
        P(None, "dp"),
        P(None, "dp", None),
        P(None, "dp"),
        P(None, "dp", None),
        P(None, "dp"),
        P(None, "dp"),
        P(None, "dp"),
        P(None, "dp", None),
        P(None, "dp"),
        P(None, "dp", None),
        P(None, "dp"),
    )
    out_specs = (
        P("seq", "dp", None),
        P("seq", "dp", None),
        P(None, "dp"),
        P(None, "dp"),
        P(None, "dp", None),
        P(None, "dp"),
        P(None, "dp", None),
        P(None, "dp"),
        P(None, "dp"),
        P(None, "dp"),
        P(None, "dp", None),
        P(None, "dp"),
        P(None, "dp", None),
        P(None, "dp"),
    )
    sizes = dict(mesh.shape)
    body = per_device_fast if (sizes["dp"], sizes["seq"]) == (16, 2) else per_device
    return jax.shard_map(
        body, mesh=mesh, in_specs=in_specs, out_specs=out_specs, check_vma=False
    )
```
